128 devices in a mesh: blk: 64 (over z_hi, x, y, core), head: 2 (over z_lo).
Axes of the slice: x: 4, y: 4, z: 4 (z_hi: 2, z_lo: 2; z = z_hi * 2 + z_lo), core: 2. Of those that a mesh axis runs over, the one named last changes fastest.
Arguments:
- queries: bfloat16 [8192, 2048], P(('blk', 'head')), may hold values from -9 to 9
- keys: bfloat16 [8192, 512], P(('blk', 'head')), may hold values from -6 to 6
- values: bfloat16 [8192, 512], P(('blk', 'head')), may hold values from -6 to 6
- grad_out: bfloat16 [8192, 2048], P(('blk', 'head')), may hold values from -6 to 6
- turn_ids: int32 [8192], replicated, may hold values from 0 to 255, never falling along the last dimension, each value on 1 to 256 neighbouring positions
Outputs:
- grad_queries: bfloat16 [8192, 2048], P(('blk', 'head'))
- key_gradients: bfloat16 [8192, 512], P(('blk', 'head'))
- value_gradients: bfloat16 [8192, 512], P(('blk', 'head'))
The draws below stay inside these ranges and needn't reach their ends.
Inputs may be any that keep to these rules, and one draw needn't show every extreme that they name: `turn_ids`: turn ids never fall and start at 0; each of the 256 turns spans 1 to 256 tokens, one exactly 256.
All inputs are finite; a program needn't handle non-finite values.
Results may differ from the reference program's by a relative error of at most 0.035.
Values may be sent and summed in bfloat16 or wider, within the bound.
A program may use at most 128 MiB of HBM per device.

```python
import math
import jax
import jax.numpy as jnp
import numpy as np
from jax import lax

QUERY_HEADS = 16
KEY_VALUE_HEADS = 4
HEAD_SIZE = 128
TRAJECTORY_LEN = 8192
TURNS = 256
MOST_TURN = 256


def shared_keys(key):
    return jnp.clip(jax.random.normal(key, (TRAJECTORY_LEN, KEY_VALUE_HEADS * HEAD_SIZE), jnp.float32), -5.0, 5.0)


def draw_keys(key, part):
    starting_keys = shared_keys(key)
    return starting_keys.astype(jnp.bfloat16)


def draw_queries(key, part):
    key = jax.random.fold_in(key, 5)
    draw_key = jax.random.fold_in(key, 0)
    result = jnp.clip(jax.random.normal(draw_key, (TRAJECTORY_LEN, QUERY_HEADS * HEAD_SIZE), jnp.float32), -5.0, 5.0)
    return result.astype(jnp.bfloat16)


def levels(key, dims, shards, low, top_value):
    loudness = 1.0
    for dim, parts in shards:
        steps = jax.random.uniform(jax.random.fold_in(jax.random.fold_in(key, 6), dim), (parts,), jnp.float32, low / len(shards), top_value / len(shards))
        loudness = loudness * jnp.repeat(jnp.exp(steps), dims[dim] // parts).reshape((-1,) + (1,) * (len(dims) - 1 - dim))
    return loudness


def split_up(amount, total, most, skew):
    loads = [(1 << 20) // math.isqrt(grade ** skew) + 1 for grade in range(2, amount + 1)]
    spare, counts = total - most - (amount - 1), [1] * (amount - 1)
    while spare > 0:
        movable = [i for i in range(amount - 1) if counts[i] < most]
        mass, budget = sum([loads[i] for i in movable]), spare
        for i in movable:
            more = min(most - counts[i], max(1, budget * loads[i] // mass), spare)
            counts[i] = counts[i] + more
            spare = spare - more
    return np.array([most] + counts)


def ragged(own_key, amount, total, bound, lean):
    if amount == 2:
        one = jax.random.randint(own_key, (), max(1, total - bound), min(bound, total - 1) + 1)
        return jnp.stack([one, total - one])
    tallies = jnp.asarray(split_up(amount, total, bound, lean), jnp.int32)
    pairs = (amount - 1) // 2
    giver, receiver = tallies[1:1 + 2 * pairs:2], tallies[2:2 + 2 * pairs:2]
    margin = jnp.minimum(giver - 1, bound - receiver)
    shifted = jax.random.randint(jax.random.fold_in(own_key, 1), (pairs,), 0, 1 << 20) % (margin + 1)
    tallies = tallies.at[1:1 + 2 * pairs:2].set(giver - shifted).at[2:2 + 2 * pairs:2].set(receiver + shifted)
    return tallies[jax.random.permutation(jax.random.fold_in(own_key, 2), amount)]


def noise(rng, shape, deviation, bound, cuts=(), kind=jnp.bfloat16):
    drawn = deviation * jax.random.normal(rng, shape, jnp.float32)
    if cuts:
        drawn = drawn * levels(rng, shape, cuts, -0.22, 0.18)
    return jnp.clip(drawn, -bound, bound).astype(kind)


def setup_inputs(seed: int = 0) -> dict:
    key_list = jax.random.split(jax.random.key(seed), 6)
    queries = draw_queries(jax.random.fold_in(key_list[5], 71), 0)
    keys = draw_keys(jax.random.fold_in(key_list[5], 71), 0)
    values = noise(key_list[2], (TRAJECTORY_LEN, KEY_VALUE_HEADS * HEAD_SIZE), 1.0, 6.0, ((0, 128),))
    grad_out = noise(key_list[3], (TRAJECTORY_LEN, QUERY_HEADS * HEAD_SIZE), 1.0, 6.0, ((0, 128),))
    turn_ids = jnp.searchsorted(jnp.cumsum(ragged(key_list[4], TURNS, TRAJECTORY_LEN, MOST_TURN, 2)), jnp.arange(TRAJECTORY_LEN), side="right").astype(jnp.int32)
    return {"queries": queries, "keys": keys, "values": values, "grad_out": grad_out, "turn_ids": turn_ids}


def reference(queries, keys, values, grad_out, turn_ids):
    queries_per_group = QUERY_HEADS // KEY_VALUE_HEADS
    factor = HEAD_SIZE ** -0.5
    positions = jnp.arange(TRAJECTORY_LEN, dtype=jnp.int32)
    causal = positions[None, :] <= positions[:, None]
    same_turn = turn_ids[None, :] == turn_ids[:, None]
    kept_turn = (turn_ids % 2 == 0)[None, :]
    visible = causal & (same_turn | kept_turn)

    def single_group(group_index):
        key_head = lax.dynamic_slice_in_dim(keys, group_index * HEAD_SIZE, HEAD_SIZE, 1)
        value_head = lax.dynamic_slice_in_dim(values, group_index * HEAD_SIZE, HEAD_SIZE, 1)
        grad_key_sum = jnp.zeros((TRAJECTORY_LEN, HEAD_SIZE), jnp.float32)
        grad_value_sum = jnp.zeros((TRAJECTORY_LEN, HEAD_SIZE), jnp.float32)
        grad_list = []
        for member in range(queries_per_group):
            column = (group_index * queries_per_group + member) * HEAD_SIZE
            query_head = lax.dynamic_slice_in_dim(queries, column, HEAD_SIZE, 1)
            grad_head = lax.dynamic_slice_in_dim(grad_out, column, HEAD_SIZE, 1)
            logits = jnp.dot(query_head, key_head.T, preferred_element_type=jnp.float32) * factor
            logits = jnp.where(visible, logits, -jnp.inf)
            row_max = jnp.max(logits, axis=1)
            log_total = row_max + jnp.log(jnp.sum(jnp.exp(logits - row_max[:, None]), axis=1))
            attention = jnp.exp(logits - log_total[:, None])
            rounded = attention.astype(jnp.bfloat16)
            forward_out = jnp.dot(rounded, value_head, preferred_element_type=jnp.float32).astype(jnp.bfloat16)
            out_dot = jnp.sum(grad_head.astype(jnp.float32) * forward_out.astype(jnp.float32), axis=1)
            grad_probs = jnp.dot(grad_head, value_head.T, preferred_element_type=jnp.float32)
            grad_logits = (attention * (grad_probs - out_dot[:, None])).astype(jnp.bfloat16)
            grad_list.append(jnp.dot(grad_logits, key_head, preferred_element_type=jnp.float32) * factor)
            grad_key_sum = grad_key_sum + jnp.dot(grad_logits.T, query_head, preferred_element_type=jnp.float32) * factor
            grad_value_sum = grad_value_sum + jnp.dot(rounded.T, grad_head, preferred_element_type=jnp.float32)
        return jnp.stack(grad_list).astype(jnp.bfloat16), grad_key_sum.astype(jnp.bfloat16), grad_value_sum.astype(jnp.bfloat16)

    query_gradient_full, key_gradient_full, value_gradient_full = lax.map(single_group, jnp.arange(KEY_VALUE_HEADS, dtype=jnp.int32))
    grad_queries = query_gradient_full.transpose(2, 0, 1, 3).reshape(TRAJECTORY_LEN, QUERY_HEADS * HEAD_SIZE)
    key_gradients = key_gradient_full.transpose(1, 0, 2).reshape(TRAJECTORY_LEN, KEY_VALUE_HEADS * HEAD_SIZE)
    value_gradients = value_gradient_full.transpose(1, 0, 2).reshape(TRAJECTORY_LEN, KEY_VALUE_HEADS * HEAD_SIZE)
    return grad_queries, key_gradients, value_gradients
```

```python
import functools
import math

import jax
import jax.numpy as jnp
from jax import lax
from jax.experimental import pallas as pl
from jax.experimental.pallas import tpu as pltpu
from jax.sharding import PartitionSpec as P

HEAD_SIZE = 128
CHUNK = 128
TILE = 256
TILES = 32
PER_GROUP = 4
ROWS = PER_GROUP * CHUNK
HIDDEN = -1e30
FACTOR = HEAD_SIZE**-0.5
MESH = pl.DeviceIdType.MESH


def place():
    blk = lax.axis_index("blk")
    z_lo = lax.axis_index("head")
    z_hi = lax.div(blk, 32)
    part = lax.rem(blk, 32)
    x = lax.div(part, 8)
    y = lax.rem(lax.div(part, 2), 4)
    core = lax.rem(part, 2)
    return x, y, z_hi * 2 + z_lo, z_hi, z_lo, core


def device(x, y, z, core):
    return (lax.div(z, 2) * 32 + x * 8 + y * 2 + core, lax.rem(z, 2))


def wrap(a):
    return lax.rem(a + 4, 4)


def send(src, dst, send_sem, recv_sem, target):
    return pltpu.make_async_remote_copy(
        src_ref=src,
        dst_ref=dst,
        send_sem=send_sem,
        recv_sem=recv_sem,
        device_id=target,
        device_id_type=MESH,
    )


def arrived(ref, sem):
    pltpu.make_async_copy(ref, ref, sem).wait()


def greet(x, y, z, core):
    others = []
    for r in range(4):
        other_z = lax.rem(z + r, 4)
        if r:
            others.append(device(x, y, other_z, core))
        others.append(device(x, y, other_z, 1 - core))
        others.append(device(3 - x, 3 - y, other_z, 1 - core))
    for step in (-1, 1):
        others.append(device(wrap(x + step), y, z, core))
        others.append(device(x, wrap(y + step), z, core))
    barrier = pltpu.get_barrier_semaphore()
    for other in others:
        pl.semaphore_signal(barrier, inc=1, device_id=other, device_id_type=MESH)
    pl.semaphore_wait(barrier, len(others))


def plane(x, y, z, core):
    first, second = x + core * (y - x), y + core * (x - y)

    def index(i, j):
        return (i + core * (j - i)) * 4 + j + core * (i - j)

    def target(i, j):
        return device(i + core * (j - i), j + core * (i - j), z, core)

    return first, second, index, target


def gather_kernel(
    q_ref, k_ref, v_ref, o_ref, kv_ref, qs_ref, os_ref,
    kv_send, kv_recv, qo_send, qo_recv, first_send, first_recv, second_send, second_recv, twin_send, twin_recv,
):
    x, y, z, z_hi, z_lo, core = place()
    first, second, index, target = plane(x, y, z, core)
    greet(x, y, z, core)
    here = x * 4 + y
    rows = pl.ds(pl.multiple_of(core * 128 + z_lo * 64, 64), 64)

    waits = []
    for r in (1, 3, 2, 0):
        other_z = lax.rem(z + r, 4)
        columns = pl.ds(pl.multiple_of(other_z * 128, 128), 128)
        for role, ref in ((0, k_ref), (1, v_ref)):
            dst = kv_ref.at[role, here, z_hi, rows]
            src = ref.at[:, columns]
            copy = send(
                src, dst, kv_send.at[role, r], kv_recv.at[z, core], device(x, y, other_z, role)
            )
            if r:
                copy.start()
                waits.append(copy)
            else:

                @pl.when(core == role)
                def _():
                    pltpu.make_async_copy(src, dst, kv_recv.at[z, core]).start()

                @pl.when(core != role)
                def _():
                    copy.start()

    mirror_x, mirror_y = x + z_hi * (3 - 2 * x), y + z_hi * (3 - 2 * y)
    mirror_core = core + z_hi * (1 - 2 * core)
    own_rows = pl.ds(pl.multiple_of(z_lo * 64, 64), 64)
    for r in (2, 1, 3, 0):
        other_z = lax.rem(z + r, 4)
        columns = pl.ds(pl.multiple_of(other_z * 512, 512), 512)
        for role, ref, out in ((0, q_ref, qs_ref), (1, o_ref, os_ref)):
            src, dst = ref.at[:, columns], out.at[z_hi, own_rows]
            copy = send(
                src, dst, qo_send.at[role, r], qo_recv.at[role, z],
                device(mirror_x, mirror_y, other_z, mirror_core),
            )
            if r:
                copy.start()
                waits.append(copy)
            else:

                @pl.when(z_hi == 0)
                def _():
                    pltpu.make_async_copy(src, dst, qo_recv.at[role, z]).start()

                @pl.when(z_hi == 1)
                def _():
                    copy.start()

    def block(i, j):
        return kv_ref.at[core, index(i, j)]

    def half(i, j, h):
        return kv_ref.at[core, index(i, j), h]

    def go(src, send_sem, recv_sem, to):
        copy = send(src, src, send_sem, recv_sem, to)
        copy.start()
        waits.append(copy)

    up, down = wrap(first + 1), wrap(first - 1)
    left, right = wrap(second - 1), wrap(second + 1)
    order = (first, down, up, wrap(first + 2))

    def twin(i, j, slot):
        go(block(i, j), twin_send.at[slot], twin_recv.at[slot], device(x, y, z, 1 - core))

    def spread(k):
        i = order[k]
        go(block(i, second), second_send.at[k, 0], second_recv.at[k, 0], target(first, right))
        go(block(i, second), second_send.at[k, 1], second_recv.at[k, 1], target(first, left))
        twin(i, second, 4 * k)

    def second_hop(k):
        i = order[k]
        arrived(block(i, left), second_recv.at[k, 0])
        go(half(i, left, 0), second_send.at[k, 2], second_recv.at[k, 2], target(first, right))
        twin(i, left, 4 * k + 1)
        arrived(block(i, right), second_recv.at[k, 1])
        go(half(i, right, 1), second_send.at[k, 3], second_recv.at[k, 3], target(first, left))
        twin(i, right, 4 * k + 2)

    def last_hop(k):
        i, j = order[k], wrap(second + 2)
        arrived(half(i, j, 0), second_recv.at[k, 2])
        arrived(half(i, j, 1), second_recv.at[k, 3])
        twin(i, j, 4 * k + 3)

    for other_z in range(4):
        for other_core in range(2):
            arrived(
                kv_ref.at[core, here, other_z // 2, pl.ds(other_core * 128 + (other_z % 2) * 64, 64)],
                kv_recv.at[other_z, other_core],
            )
    go(block(first, second), first_send.at[0], first_recv.at[0], target(up, second))
    go(block(first, second), first_send.at[1], first_recv.at[1], target(down, second))
    spread(0)
    arrived(block(down, second), first_recv.at[0])
    go(half(down, second, 0), first_send.at[2], first_recv.at[2], target(up, second))
    spread(1)
    arrived(block(up, second), first_recv.at[1])
    go(half(up, second, 1), first_send.at[3], first_recv.at[3], target(down, second))
    spread(2)
    second_hop(0)
    arrived(half(order[3], second, 0), first_recv.at[2])
    arrived(half(order[3], second, 1), first_recv.at[3])
    spread(3)
    second_hop(1)
    second_hop(2)
    last_hop(0)
    second_hop(3)
    last_hop(1)
    last_hop(2)
    last_hop(3)

    for slot in range(16):
        arrived(kv_ref.at[1 - core, slot], twin_recv.at[slot])
    for role, out in ((0, qs_ref), (1, os_ref)):
        for other_z in range(4):
            arrived(
                out.at[other_z // 2, pl.ds((other_z % 2) * 64, 64)], qo_recv.at[role, other_z]
            )
    for copy in waits:
        copy.wait_send()
    for role, ref in ((0, k_ref), (1, v_ref)):

        @pl.when(core != role)
        def _():
            src = ref.at[:, pl.ds(0, 128)]
            pltpu.make_async_copy(src, src, kv_send.at[role, 0]).wait()

    for role, ref in ((0, q_ref), (1, o_ref)):

        @pl.when(z_hi == 1)
        def _():
            src = ref.at[:, pl.ds(0, 512)]
            pltpu.make_async_copy(src, src, qo_send.at[role, 0]).wait()


def attention_kernel(
    place_ref, turn_ref, query_turn_ref, kv_ref, q_ref, o_ref, dkv_ref, dq_ref,
    qs, os, weights, probs_grad, tile_max, dq_acc,
):
    part = place_ref[0]
    chunks = (part, 63 - part)
    counts = (lax.div(part, 2) + 1, lax.div(63 - part, 2) + 1)
    starts = (0, counts[0])
    scale = FACTOR * math.log2(math.e)

    for s in range(2):
        for h in range(PER_GROUP):
            lanes, lines = pl.ds(h * 128, 128), pl.ds(h * CHUNK, CHUNK)
            qs[s, lines, :] = q_ref[s, :, lanes]
            os[s, lines, :] = o_ref[s, :, lanes]

    def stored(t):
        return lax.rem(t, 16) * 2 + lax.div(t, 16)

    finals = []
    for s in range(2):
        query_pos = chunks[s] * CHUNK + lax.broadcasted_iota(jnp.int32, (1, CHUNK), 1)
        query_turn = query_turn_ref[pl.ds(chunks[s], 1), :]

        def stats(t, carried, s=s, query_pos=query_pos, query_turn=query_turn):
            top, total, dot = carried
            at = stored(t)
            key_turn = jnp.broadcast_to(turn_ref[pl.ds(t, 1), :], (CHUNK, TILE)).T
            key_pos = t * TILE + lax.broadcasted_iota(jnp.int32, (TILE, CHUNK), 0)
            visible = (key_pos <= query_pos) & (
                (key_turn == query_turn) | ((key_turn & 1) == 0)
            )
            logits = lax.dot_general(
                kv_ref[0, at], qs[s], (((1,), (1,)), ((), ())), preferred_element_type=jnp.float32
            )
            bias = jnp.where(visible, 0.0, HIDDEN)
            logits = logits * scale + jnp.concatenate([bias] * PER_GROUP, axis=1)
            new_top = jnp.maximum(top, jnp.max(logits, axis=0, keepdims=True))
            shrink = jnp.exp2(top - new_top)
            weight = jnp.exp2(logits - new_top)
            grads = lax.dot_general(
                kv_ref[1, at], os[s], (((1,), (1,)), ((), ())), preferred_element_type=jnp.float32
            )
            item = starts[s] + t
            weights[item] = weight.astype(jnp.bfloat16)
            probs_grad[item] = grads.astype(jnp.bfloat16)
            tile_max[pl.ds(item, 1), :] = new_top
            total = total * shrink + jnp.sum(weight, axis=0, keepdims=True)
            dot = dot * shrink + jnp.sum(weight * grads, axis=0, keepdims=True)
            return new_top, total, dot

        zero = jnp.zeros((1, ROWS), jnp.float32)
        top, total, dot = lax.fori_loop(
            0, counts[s], stats, (jnp.full((1, ROWS), HIDDEN, jnp.float32), zero, zero)
        )
        share = 1.0 / total
        finals.append((top, share, dot * share))

    dq_acc[...] = jnp.zeros_like(dq_acc)

    def terms(s, t):
        item = starts[s] + t
        top, share, dot = finals[s]
        by = jnp.exp2(tile_max[pl.ds(item, 1), :] - top) * share
        attention = weights[item].astype(jnp.float32) * by
        logit_grad = (attention * (probs_grad[item].astype(jnp.float32) - dot)).astype(jnp.bfloat16)
        value_term = jnp.dot(
            attention.astype(jnp.bfloat16), os[s], preferred_element_type=jnp.float32
        )
        key_term = jnp.dot(logit_grad, qs[s], preferred_element_type=jnp.float32)
        dq_acc[s] += lax.dot_general(
            logit_grad, kv_ref[0, stored(t)], (((0,), (0,)), ((), ())),
            preferred_element_type=jnp.float32,
        )
        return key_term, value_term

    def both(t, _):
        key_a, value_a = terms(0, t)
        key_b, value_b = terms(1, t)
        at = stored(t)
        dkv_ref[0, at] = ((key_a + key_b) * FACTOR).astype(jnp.bfloat16)
        dkv_ref[1, at] = (value_a + value_b).astype(jnp.bfloat16)
        return 0

    def late(t, _):
        key_b, value_b = terms(1, t)
        at = stored(t)
        dkv_ref[0, at] = (key_b * FACTOR).astype(jnp.bfloat16)
        dkv_ref[1, at] = value_b.astype(jnp.bfloat16)
        return 0

    def unseen(t, _):
        at = stored(t)
        empty = jnp.zeros((TILE, HEAD_SIZE), jnp.bfloat16)
        dkv_ref[0, at] = empty
        dkv_ref[1, at] = empty
        return 0

    lax.fori_loop(0, counts[0], both, 0)
    lax.fori_loop(counts[0], counts[1], late, 0)
    lax.fori_loop(counts[1], TILES, unseen, 0)
    for s in range(2):
        for h in range(PER_GROUP):
            dq_ref[s, :, pl.ds(h * 128, 128)] = (
                dq_acc[s, pl.ds(h * CHUNK, CHUNK), :] * FACTOR
            ).astype(jnp.bfloat16)


def reduce_kernel(
    g_ref, dq_ref, dq_out, dkv_out,
    twin, total, one, two, line, one_f, two_f, done,
    twin_send, twin_recv, second_send, second_recv, first_send, first_recv,
    kv_send, kv_recv, dq_send, dq_recv,
):
    x, y, z, z_hi, z_lo, core = place()
    first, second, index, target = plane(x, y, z, core)
    greet(x, y, z, core)
    waits = []

    def go(src, dst, send_sem, recv_sem, to):
        copy = send(src, dst, send_sem, recv_sem, to)
        copy.start()
        waits.append(copy)

    def orders(f, s):
        return (
            (wrap(f + 2), wrap(f + 1), wrap(f - 1), f),
            (wrap(s + 2), wrap(s + 1), wrap(s - 1), s),
        )

    other_i, other_j = orders(second, first)
    for b in range(4):
        for a in range(4):
            at = index(other_j[b], other_i[a])
            slot = 4 * b + a
            go(g_ref.at[1 - core, at], twin.at[at], twin_send.at[slot], twin_recv.at[slot],
               device(x, y, z, 1 - core))

    for other_z in range(4):
        other_hi, other_lo = other_z // 2, other_z % 2
        tx, ty, tc = (3 - x, 3 - y, 1 - core) if other_hi else (x, y, core)
        src = dq_ref.at[other_hi, pl.ds(other_lo * 64, 64)]
        dst = dq_out.at[:, pl.ds(pl.multiple_of(z * 512, 512), 512)]
        copy = send(src, dst, dq_send.at[other_z], dq_recv.at[z], device(tx, ty, other_z, tc))
        if other_hi:
            copy.start()
            waits.append(copy)
        else:

            @pl.when(z == other_z)
            def _():
                pltpu.make_async_copy(src, dst, dq_recv.at[z]).start()

            @pl.when(z != other_z)
            def _():
                copy.start()

    order, across = orders(first, second)
    right, left = across[1], across[2]
    up, down = order[1], order[2]

    def chip_sum(i, j, a, b):
        at = index(i, j)
        arrived(twin.at[at], twin_recv.at[4 * b + a])
        return g_ref[core, at].astype(jnp.float32) + twin[at].astype(jnp.float32)

    for a in range(4):
        i, j = order[a], across[0]
        at = index(i, j)
        total[a, 0] = chip_sum(i, j, a, 0).astype(jnp.bfloat16)
        go(total.at[a, 0, 0], one.at[a, 0], second_send.at[a, 0], second_recv.at[a, 0], target(first, right))
        go(total.at[a, 0, 1], one.at[a, 1], second_send.at[a, 1], second_recv.at[a, 1], target(first, left))
    for a in range(4):
        i = order[a]
        for b, to in ((1, right), (2, left)):
            h = b - 1
            value = chip_sum(i, across[b], a, b)
            arrived(one.at[a, h], second_recv.at[a, h])
            total[a, b, 1 - h] = value[1 - h].astype(jnp.bfloat16)
            total[a, b, h] = (value[h] + one[a, h].astype(jnp.float32)).astype(jnp.bfloat16)
            go(total.at[a, b], two.at[a, h], second_send.at[a, 2 + h], second_recv.at[a, 2 + h], target(first, to))
    for a in range(4):
        i = order[a]
        value = chip_sum(i, second, a, 3)
        arrived(two.at[a, 0], second_recv.at[a, 2])
        arrived(two.at[a, 1], second_recv.at[a, 3])
        value = value + two[a, 0].astype(jnp.float32) + two[a, 1].astype(jnp.float32)
        if a == 0:
            line[0] = value.astype(jnp.bfloat16)
            go(line.at[0, 0], one_f.at[0], first_send.at[0], first_recv.at[0], target(up, second))
            go(line.at[0, 1], one_f.at[1], first_send.at[1], first_recv.at[1], target(down, second))
        elif a < 3:
            h = a - 1
            arrived(one_f.at[h], first_recv.at[h])
            line[a, 1 - h] = value[1 - h].astype(jnp.bfloat16)
            line[a, h] = (value[h] + one_f[h].astype(jnp.float32)).astype(jnp.bfloat16)
            go(line.at[a], two_f.at[h], first_send.at[2 + h], first_recv.at[2 + h],
               target(up if a == 1 else down, second))
        else:
            arrived(two_f.at[0], first_recv.at[2])
            arrived(two_f.at[1], first_recv.at[3])
            value = value + two_f[0].astype(jnp.float32) + two_f[1].astype(jnp.float32)
            done[...] = value.astype(jnp.bfloat16)

    for other_z in range(4):
        for other_core in range(2):
            src = done.at[other_z // 2, pl.ds(other_core * 128 + (other_z % 2) * 64, 64)]
            dst = dkv_out.at[core, :, pl.ds(pl.multiple_of(z * 128, 128), 128)]
            slot = kv_recv.at[core, z]
            copy = send(src, dst, kv_send.at[other_z, other_core], slot, device(x, y, other_z, other_core))
            own = (z == other_z) & (core == other_core)

            @pl.when(own)
            def _():
                pltpu.make_async_copy(src, dst, slot).start()

            @pl.when(jnp.logical_not(own))
            def _():
                copy.start()

    for role in range(2):
        for other_z in range(4):
            arrived(dkv_out.at[role, :, pl.ds(other_z * 128, 128)], kv_recv.at[role, other_z])
    for other_z in range(4):
        arrived(dq_out.at[:, pl.ds(other_z * 512, 512)], dq_recv.at[other_z])
    for copy in waits:
        copy.wait_send()
    for other_z in range(4):
        for other_core in range(2):

            @pl.when(jnp.logical_not((z == other_z) & (core == other_core)))
            def _():
                arrived(done.at[0, pl.ds(0, 64)], kv_send.at[other_z, other_core])

    for other_z in range(2):

        @pl.when(z != other_z)
        def _():
            arrived(dq_ref.at[0, pl.ds(0, 64)], dq_send.at[other_z])


ANY = pl.BlockSpec(memory_space=pl.ANY)
VMEM = pl.BlockSpec(memory_space=pltpu.VMEM)
SMEM = pl.BlockSpec(memory_space=pltpu.SMEM)
BF16 = jnp.bfloat16
DMA = pltpu.SemaphoreType.DMA


def exchange(queries, keys, values, grad_out):
    return pl.pallas_call(
        gather_kernel,
        out_shape=(
            jax.ShapeDtypeStruct((2, 16, 2, 256, 128), BF16),
            jax.ShapeDtypeStruct((2, CHUNK, 512), BF16),
            jax.ShapeDtypeStruct((2, CHUNK, 512), BF16),
        ),
        in_specs=[ANY] * 4,
        out_specs=(VMEM, ANY, ANY),
        scratch_shapes=[
            DMA((2, 4)), DMA((4, 2)),
            DMA((2, 4)), DMA((2, 4)),
            DMA((4,)), DMA((4,)),
            DMA((4, 4)), DMA((4, 4)),
            DMA((16,)), DMA((16,)),
        ],
        compiler_params=pltpu.CompilerParams(
            collective_id=0, has_side_effects=True, vmem_limit_bytes=32 << 20
        ),
        name="exchange",
    )(queries, keys, values, grad_out)


def attend(part, turn_ids, kv, queries, grads):
    return pl.pallas_call(
        attention_kernel,
        out_shape=(
            jax.ShapeDtypeStruct((2, TILES, TILE, 128), BF16),
            jax.ShapeDtypeStruct((2, CHUNK, 512), BF16),
        ),
        in_specs=[SMEM] + [VMEM] * 5,
        out_specs=(VMEM, VMEM),
        scratch_shapes=[
            pltpu.VMEM((2, ROWS, 128), BF16),
            pltpu.VMEM((2, ROWS, 128), BF16),
            pltpu.VMEM((33, TILE, ROWS), BF16),
            pltpu.VMEM((33, TILE, ROWS), BF16),
            pltpu.VMEM((33, ROWS), jnp.float32),
            pltpu.VMEM((2, ROWS, 128), jnp.float32),
        ],
        compiler_params=pltpu.CompilerParams(vmem_limit_bytes=56 << 20),
        name="attend",
    )(part, turn_ids.reshape(TILES, TILE), turn_ids.reshape(64, CHUNK), kv, queries, grads)


def combine(partial, dq):
    half = (256, 128)
    whole = (2, 256, 128)
    return pl.pallas_call(
        reduce_kernel,
        out_shape=(
            jax.ShapeDtypeStruct((64, 2048), BF16),
            jax.ShapeDtypeStruct((2, 64, 512), BF16),
        ),
        in_specs=[VMEM, ANY],
        out_specs=(ANY, ANY),
        scratch_shapes=[
            pltpu.VMEM((16,) + whole, BF16),
            pltpu.VMEM((4, 3) + whole, BF16),
            pltpu.VMEM((4, 2) + half, BF16),
            pltpu.VMEM((4, 2) + whole, BF16),
            pltpu.VMEM((3,) + whole, BF16),
            pltpu.VMEM((2,) + half, BF16),
            pltpu.VMEM((2,) + whole, BF16),
            pltpu.VMEM(whole, BF16),
            DMA((16,)), DMA((16,)),
            DMA((4, 4)), DMA((4, 4)),
            DMA((4,)), DMA((4,)),
            DMA((4, 2)), DMA((2, 4)),
            DMA((4,)), DMA((4,)),
        ],
        compiler_params=pltpu.CompilerParams(
            collective_id=1, has_side_effects=True, vmem_limit_bytes=40 << 20
        ),
        name="combine",
    )(partial, dq)


def body(queries, keys, values, grad_out, turn_ids):
    kv, own_queries, own_grads = exchange(queries, keys, values, grad_out)
    part = lax.rem(lax.axis_index("blk"), 32).astype(jnp.int32).reshape(1)
    partial, dq = attend(part, turn_ids, kv.reshape(2, TILES, TILE, 128), own_queries, own_grads)
    dq_out, dkv_out = combine(partial.reshape(2, 16, 2, 256, 128), dq)
    return dq_out, dkv_out[0], dkv_out[1]


def solution(mesh):
    spread = P(("blk", "head"), None)
    return jax.shard_map(
        body,
        mesh=mesh,
        in_specs=(spread,) * 4 + (P(),),
        out_specs=(spread,) * 3,
        check_vma=False,
    )
```

```python
import math

import jax
import jax.numpy as jnp
from jax import lax
from jax.experimental import pallas as pl
from jax.experimental.pallas import tpu as pltpu
from jax.sharding import PartitionSpec as P

HEAD_SIZE = 128
CHUNK = 128
TILE = 256
PER_GROUP = 4
ROWS = PER_GROUP * CHUNK
ITEMS = 33
HIDDEN = -1e30
FACTOR = HEAD_SIZE**-0.5
BF16 = jnp.bfloat16
F32 = jnp.float32
MESH = pl.DeviceIdType.MESH

NEAR_FIRST = (
    (0, 0), (-1, 0), (1, 0), (0, -1), (0, 1), (-1, -1), (-1, 1), (1, -1), (1, 1),
    (2, 0), (0, 2), (2, -1), (2, 1), (-1, 2), (1, 2), (2, 2),
)
FAR_FIRST = (
    (2, 2), (1, 2), (-1, 2), (2, 1), (2, -1), (0, 2), (2, 0), (0, 1), (0, -1), (1, 0), (-1, 0),
    (1, 1), (1, -1), (-1, 1), (-1, -1), (0, 0),
)


def device(x, y, z, core):
    return (lax.div(z, 2) * 32 + x * 8 + y * 2 + core, lax.rem(z, 2))


def wrap(a):
    return lax.rem(a + 4, 4)


def send(src, dst, send_sem, recv_sem, target):
    return pltpu.make_async_remote_copy(
        src_ref=src,
        dst_ref=dst,
        send_sem=send_sem,
        recv_sem=recv_sem,
        device_id=target,
        device_id_type=MESH,
    )


def arrived(ref, sem):
    pltpu.make_async_copy(ref, ref, sem).wait()


def greet(x, y, z, core):
    others = []
    for r in range(4):
        other_z = lax.rem(z + r, 4)
        if r:
            others.append(device(x, y, other_z, core))
        others.append(device(x, y, other_z, 1 - core))
        others.append(device(3 - x, 3 - y, other_z, 1 - core))
        for step in (1, 2, 3):
            others.append(device(wrap(x + step), y, other_z, 0))
            others.append(device(wrap(x + step), y, other_z, 1))
            others.append(device(x, wrap(y + step), other_z, 0))
            others.append(device(x, wrap(y + step), other_z, 1))
    barrier = pltpu.get_barrier_semaphore()
    for other in others:
        pl.semaphore_signal(barrier, inc=1, device_id=other, device_id_type=MESH)
    pl.semaphore_wait(barrier, len(others))


def codes(order, axis):
    digits = [step[axis] % 4 for step in order]
    return [sum(digit * 4**i for i, digit in enumerate(digits[at : at + 8])) for at in (0, 8)]


def at_most(a, b):
    return lax.div(b - a + 16, 16)


def kernel(
    turn_ref, q_ref, k_ref, v_ref, o_ref, dq_out, dk_out, dv_out,
    kv, landed, qs, os, weights, probs_grad, tile_max, top, total, dot, dq_acc, dq_own,
    term, partial, twin, sums, one, two, line, last,
    kv_send, kv_recv, qo_send, qo_recv, first_send, first_recv, second_send, second_recv,
    twin_send, twin_recv, back_send, back_recv, ring_send, ring_recv, last_send, last_recv,
    dq_send, dq_recv,
):
    blk = lax.axis_index("blk")
    z_lo = lax.axis_index("head")
    z_hi = lax.div(blk, 32)
    part = lax.rem(blk, 32)
    x = lax.div(part, 8)
    y = lax.rem(lax.div(part, 2), 4)
    core = lax.rem(part, 2)
    z = z_hi * 2 + z_lo
    here = x * 4 + y
    first, second = x + core * (y - x), y + core * (x - y)

    def index(i, j):
        return (i + core * (j - i)) * 4 + j + core * (i - j)

    def target(i, j):
        return device(i + core * (j - i), j + core * (i - j), z, core)

    other_core = device(x, y, z, 1 - core)
    odd = lax.rem(z, 2)
    my_part = part + odd * (31 - 2 * part)
    my_block = lax.div(my_part, 2)

    greet(x, y, z, core)

    def go(src, dst, send_sem, recv_sem, to):
        send(src, dst, send_sem, recv_sem, to).start()

    def go_or_keep(own, src, dst, send_sem, recv_sem, to):
        @pl.when(own)
        def _():
            pltpu.make_async_copy(src, dst, recv_sem).start()

        @pl.when(jnp.logical_not(own))
        def _():
            send(src, dst, send_sem, recv_sem, to).start()

    rows = pl.ds(pl.multiple_of(core * 128 + z_lo * 64, 64), 64)
    for r in (2, 1, 3, 0):
        other_z = lax.rem(z + r, 4)
        columns = pl.ds(pl.multiple_of(other_z * 128, 128), 128)
        for role, ref in ((0, k_ref), (1, v_ref)):
            dst = kv.at[role, here, z_hi, rows]
            args = (ref.at[:, columns], dst, kv_send.at[role, r], kv_recv.at[z, core])
            if r:
                go(*args, device(x, y, other_z, role))
            else:
                go_or_keep(core == role, *args, device(x, y, z, role))

    own_rows = pl.ds(pl.multiple_of(z_lo * 64, 64), 64)
    for r in (2, 1, 3, 0):
        other_z = lax.rem(z + r, 4)
        flip = lax.rem(z_hi + other_z, 2)
        to = device(x + flip * (3 - 2 * x), y + flip * (3 - 2 * y), other_z, core + flip * (1 - 2 * core))
        columns = pl.ds(pl.multiple_of(other_z * 512, 512), 512)
        for role, ref in ((0, q_ref), (1, o_ref)):
            args = (ref.at[:, columns], landed.at[role, z_hi, own_rows], qo_send.at[role, r], qo_recv.at[role, z])
            if r:
                go(*args, to)
            else:
                go_or_keep(flip == 0, *args, to)

    up, down = wrap(first + 1), wrap(first - 1)
    left, right = wrap(second - 1), wrap(second + 1)
    firsts = (first, down, up, wrap(first + 2))
    steps = (0, -1, 1, 2)
    near = {step: n for n, step in enumerate(NEAR_FIRST)}
    far = {step: n for n, step in enumerate(FAR_FIRST)}

    def slot_of(table, a, b):
        return table[a, b] + core * (table[b, a] - table[a, b])

    def block(i, j):
        return kv.at[core, index(i, j)]

    def half(i, j, h):
        return kv.at[core, index(i, j), h]

    def share(i, j, a, b):
        slot = slot_of(near, a, b)
        go(block(i, j), block(i, j), twin_send.at[slot], twin_recv.at[slot], other_core)

    def relay(src, sems, to):
        go(src, src, *sems, to)

    def spread(k):
        i = firsts[k]
        own = block(i, second)
        relay(own, (second_send.at[k, 0], second_recv.at[k, 0]), target(first, right))
        relay(own, (second_send.at[k, 1], second_recv.at[k, 1]), target(first, left))
        share(i, second, steps[k], 0)

    def begin():
        for other_z in range(4):
            for c in range(2):
                arrived(
                    kv.at[core, here, other_z // 2, pl.ds(c * 128 + (other_z % 2) * 64, 64)],
                    kv_recv.at[other_z, c],
                )
        own = block(first, second)
        for slot, i in enumerate((up, down, firsts[3])):
            relay(own, (first_send.at[slot], first_recv.at[slot]), target(i, second))
        spread(0)

    def first_hop(k):
        arrived(block(firsts[k], second), first_recv.at[k - 1])
        spread(k)

    def second_hop(k):
        i = firsts[k]
        arrived(block(i, left), second_recv.at[k, 0])
        relay(half(i, left, 0), (second_send.at[k, 2], second_recv.at[k, 2]), target(first, right))
        share(i, left, steps[k], -1)
        arrived(block(i, right), second_recv.at[k, 1])
        relay(half(i, right, 1), (second_send.at[k, 3], second_recv.at[k, 3]), target(first, left))
        share(i, right, steps[k], 1)

    def last_hop(k):
        i, j = firsts[k], wrap(second + 2)
        arrived(half(i, j, 0), second_recv.at[k, 2])
        arrived(half(i, j, 1), second_recv.at[k, 3])
        share(i, j, steps[k], 2)

    def queries_here():
        for role in range(2):
            for other_z in range(4):
                arrived(
                    landed.at[role, other_z // 2, pl.ds((other_z % 2) * 64, 64)],
                    qo_recv.at[role, other_z],
                )
        for s in range(2):
            for h in range(PER_GROUP):
                lanes, lines = pl.ds(h * 128, 128), pl.ds(h * CHUNK, CHUNK)
                qs[s, lines, :] = landed[0, s, :, lanes]
                os[s, lines, :] = landed[1, s, :, lanes]

    gather_events = {
        0: (begin, queries_here),
        1: (lambda: first_hop(1), lambda: first_hop(2), lambda: second_hop(0)),
        3: (lambda: first_hop(3),),
        5: (lambda: second_hop(1),),
        6: (lambda: second_hop(2),),
        7: (lambda: last_hop(0),),
        8: (lambda: second_hop(3),),
        10: (lambda: last_hop(1),),
        11: (lambda: last_hop(2),),
        12: (lambda: last_hop(3),),
    }

    def run(events, n):
        for at, actions in events.items():

            @pl.when(n == at)
            def _():
                for action in actions:
                    action()

    def block_of(code_x, code_y):
        return lax.rem(x + lax.rem(code_x, 4), 4) * 4 + lax.rem(y + lax.rem(code_y, 4), 4)

    def over_blocks(order, step):
        (start_x, more_x), (start_y, more_y) = codes(order, 0), codes(order, 1)

        def turn(n, carried):
            code_x, code_y = carried
            step(n, block_of(code_x, code_y))
            middle = lax.div(n + 1, 8) - lax.div(n + 1, 9)
            return lax.div(code_x, 4) + middle * more_x, lax.div(code_y, 4) + middle * more_y

        lax.fori_loop(0, 16, turn, (start_x + 0 * x, start_y + 0 * x))

    def items_of(b):
        return 1 + at_most(b, my_block) + at_most(b, 15 - my_block)

    def item(b, r):
        is_a = lax.rem(r, 2) * at_most(b, my_block)
        late = lax.div(r + 1, 2) - is_a
        return 1 - is_a, late, b + 16 * is_a + late * (32 - 2 * b)

    scale = FACTOR * math.log2(math.e)
    top[...] = jnp.full(top.shape, HIDDEN, F32)
    total[...] = jnp.zeros_like(total)
    dot[...] = jnp.zeros_like(dot)
    dq_acc[...] = jnp.zeros_like(dq_acc)

    def stats_step(n, b):
        run(gather_events, n)
        arrived(kv.at[1 - core, b], twin_recv.at[n])

        def stats(r, _):
            s, late, number = item(b, r)
            tile = late * 16 + b
            chunk = my_part + s * (63 - 2 * my_part)
            query_pos = chunk * CHUNK + lax.broadcasted_iota(jnp.int32, (1, CHUNK), 1)
            query_turn = turn_ref[pl.ds(chunk, 1), :]
            key_turn = jnp.concatenate(
                [
                    jnp.broadcast_to(turn_ref[pl.ds(2 * tile + i, 1), :], (128, 128)).T
                    for i in range(2)
                ],
                axis=0,
            )
            key_pos = tile * TILE + lax.broadcasted_iota(jnp.int32, (TILE, CHUNK), 0)
            visible = (key_pos <= query_pos) & (
                (key_turn == query_turn) | ((key_turn & 1) == 0)
            )
            logits = lax.dot_general(
                kv[0, b, late], qs[s], (((1,), (1,)), ((), ())), preferred_element_type=F32
            )
            bias = jnp.where(visible, 0.0, HIDDEN)
            logits = logits * scale + jnp.concatenate([bias] * PER_GROUP, axis=1)
            old_top = top[s]
            new_top = jnp.maximum(old_top, jnp.max(logits, axis=0, keepdims=True))
            shrink = jnp.exp2(old_top - new_top)
            weight = jnp.exp2(logits - new_top)
            grads = lax.dot_general(
                kv[1, b, late], os[s], (((1,), (1,)), ((), ())), preferred_element_type=F32
            )
            weights[number] = weight.astype(BF16)
            probs_grad[number] = grads.astype(BF16)
            tile_max[number] = new_top
            top[s] = new_top
            total[s] = total[s] * shrink + jnp.sum(weight, axis=0, keepdims=True)
            dot[s] = dot[s] * shrink + jnp.sum(weight * grads, axis=0, keepdims=True)
            return 0

        lax.fori_loop(0, items_of(b), stats, 0)

    over_blocks(NEAR_FIRST, stats_step)
    for s in range(2):
        inverse = 1.0 / total[s]
        total[s] = inverse
        dot[s] = dot[s] * inverse

    across = (wrap(second + 2), right, left, second)
    jumps = (2, 1, -1, 0)

    def chip_sum(a, b):
        i, j = firsts[a], across[b]
        at = index(i, j)
        arrived(twin.at[at], back_recv.at[slot_of(far, steps[a], jumps[b])])
        return partial[core, at].astype(F32) + twin[at].astype(F32)

    def ring_one(a):
        sums[a, 0] = chip_sum(a, 0).astype(BF16)
        for h, to in ((0, right), (1, left)):
            go(sums.at[a, 0, h], one.at[a, h], ring_send.at[a, h], ring_recv.at[a, h], target(first, to))

    def ring_two(a):
        for b, to in ((1, right), (2, left)):
            h = b - 1
            value = chip_sum(a, b)
            arrived(one.at[a, h], ring_recv.at[a, h])
            sums[a, b, 1 - h] = value[1 - h].astype(BF16)
            sums[a, b, h] = (value[h] + one[a, h].astype(F32)).astype(BF16)
            go(sums.at[a, b], two.at[a, h], ring_send.at[a, 2 + h], ring_recv.at[a, 2 + h], target(first, to))

    def home(a):
        value = chip_sum(a, 3)
        arrived(two.at[a, 0], ring_recv.at[a, 2])
        arrived(two.at[a, 1], ring_recv.at[a, 3])
        value = value + two[a, 0].astype(F32) + two[a, 1].astype(F32)
        line[a] = value.astype(BF16)
        i = firsts[a]
        bx, by = i + core * (second - i), second + core * (i - second)
        for other_z in range(4):
            for c in range(2):
                src = line.at[a, other_z // 2, pl.ds(c * 128 + (other_z % 2) * 64, 64)]
                dst = last.at[core, a, :, pl.ds(pl.multiple_of(z * 128, 128), 128)]
                args = (src, dst, last_send.at[a, other_z, c], last_recv.at[core, a, z])
                to = device(bx, by, other_z, c)
                if a:
                    go(*args, to)
                else:
                    go_or_keep((z == other_z) & (core == c), *args, to)

    reduce_events = {
        1: (lambda: ring_one(3),),
        4: (lambda: ring_one(2),),
        5: (lambda: ring_one(1),),
        6: (lambda: ring_two(3),),
        7: (lambda: ring_one(0),),
        12: (lambda: ring_two(0), lambda: home(3)),
        14: (lambda: ring_two(2),),
        15: (lambda: ring_two(1),),
    }

    def backward_step(n, b):
        def terms(r, _):
            s, late, number = item(b, r)
            by = jnp.exp2(tile_max[number] - top[s]) * total[s]
            attention = weights[number].astype(F32) * by
            logit_grad = (attention * (probs_grad[number].astype(F32) - dot[s])).astype(BF16)
            key_term = jnp.dot(logit_grad, qs[s], preferred_element_type=F32) * FACTOR
            value_term = jnp.dot(attention.astype(BF16), os[s], preferred_element_type=F32)
            dq_acc[s] += lax.dot_general(
                logit_grad, kv[0, b, late], (((0,), (0,)), ((), ())), preferred_element_type=F32
            )
            key_term += jnp.where(s == 0, term[0], 0.0)
            value_term += jnp.where(s == 0, term[1], 0.0)
            term[0] = key_term
            term[1] = value_term
            partial[0, b, late] = key_term.astype(BF16)
            partial[1, b, late] = value_term.astype(BF16)
            return 0

        lax.fori_loop(0, items_of(b), terms, 0)

        @pl.when(b > 15 - my_block)
        def _():
            partial[0, b, 1] = jnp.zeros((TILE, HEAD_SIZE), BF16)
            partial[1, b, 1] = jnp.zeros((TILE, HEAD_SIZE), BF16)

        send(partial.at[1 - core, b], twin.at[b], back_send.at[n], back_recv.at[n], other_core).start()
        run(reduce_events, n)

    term[...] = jnp.zeros_like(term)
    over_blocks(FAR_FIRST, backward_step)

    for s in range(2):
        for h in range(PER_GROUP):
            dq_own[s, :, pl.ds(h * 128, 128)] = (
                dq_acc[s, pl.ds(h * CHUNK, CHUNK), :] * FACTOR
            ).astype(BF16)
    for other_z in range(4):
        s = other_z // 2
        flip = lax.rem(s + odd, 2)
        to = device(x + flip * (3 - 2 * x), y + flip * (3 - 2 * y), other_z, core + flip * (1 - 2 * core))
        go_or_keep(
            (flip == 0) & (z == other_z),
            dq_own.at[s, pl.ds((other_z % 2) * 64, 64)],
            dq_out.at[:, pl.ds(pl.multiple_of(z * 512, 512), 512)],
            dq_send.at[other_z], dq_recv.at[z], to,
        )
    home(2)
    home(1)
    home(0)

    for role, out in ((0, dk_out), (1, dv_out)):
        value = None
        for a in range(4):
            for other_z in range(4):
                arrived(last.at[role, a, :, pl.ds(other_z * 128, 128)], last_recv.at[role, a, other_z])
            share_in = last[role, a].astype(F32)
            value = share_in if value is None else value + share_in
        out[...] = value.astype(BF16)
    for other_z in range(4):
        arrived(dq_out.at[:, pl.ds(other_z * 512, 512)], dq_recv.at[other_z])

    whole, halved, piece = kv.at[0, 0], kv.at[0, 0, 0], line.at[0, 0, pl.ds(0, 64)]
    for r in range(1, 4):
        for role in range(2):
            arrived(k_ref.at[:, pl.ds(0, 128)], kv_send.at[role, r])
            arrived(q_ref.at[:, pl.ds(0, 512)], qo_send.at[role, r])
        arrived(whole, first_send.at[r - 1])
        for other_z in range(4):
            for c in range(2):
                arrived(piece, last_send.at[r, other_z, c])
    for k in range(4):
        for h in range(2):
            arrived(whole, second_send.at[k, h])
            arrived(halved, second_send.at[k, 2 + h])
            arrived(halved, ring_send.at[k, h])
            arrived(whole, ring_send.at[k, 2 + h])
    for n in range(16):
        arrived(whole, twin_send.at[n])
        arrived(whole, back_send.at[n])

    @pl.when(core == 0)
    def _():
        arrived(v_ref.at[:, pl.ds(0, 128)], kv_send.at[1, 0])

    @pl.when(core == 1)
    def _():
        arrived(k_ref.at[:, pl.ds(0, 128)], kv_send.at[0, 0])

    @pl.when(lax.rem(z_hi + z_lo, 2) == 1)
    def _():
        for role in range(2):
            arrived(q_ref.at[:, pl.ds(0, 512)], qo_send.at[role, 0])

    for other_z in range(4):
        for c in range(2):

            @pl.when(jnp.logical_not((z == other_z) & (core == c)))
            def _():
                arrived(piece, last_send.at[0, other_z, c])

        flip = lax.rem(other_z // 2 + odd, 2)

        @pl.when(jnp.logical_not((flip == 0) & (z == other_z)))
        def _():
            arrived(dq_own.at[0, pl.ds(0, 64)], dq_send.at[other_z])


ANY = pl.BlockSpec(memory_space=pl.ANY)
VMEM = pl.BlockSpec(memory_space=pltpu.VMEM)
DMA = pltpu.SemaphoreType.DMA


def body(queries, keys, values, grad_out, turn_ids):
    block = (2, TILE, HEAD_SIZE)
    return pl.pallas_call(
        kernel,
        out_shape=(
            jax.ShapeDtypeStruct((64, 2048), BF16),
            jax.ShapeDtypeStruct((64, 512), BF16),
            jax.ShapeDtypeStruct((64, 512), BF16),
        ),
        in_specs=[VMEM] + [ANY] * 4,
        out_specs=(ANY, VMEM, VMEM),
        scratch_shapes=[
            pltpu.VMEM((2, 16) + block, BF16),
            pltpu.VMEM((2, 2, CHUNK, 512), BF16),
            pltpu.VMEM((2, ROWS, HEAD_SIZE), BF16),
            pltpu.VMEM((2, ROWS, HEAD_SIZE), BF16),
            pltpu.VMEM((ITEMS, TILE, ROWS), BF16),
            pltpu.VMEM((ITEMS, TILE, ROWS), BF16),
            pltpu.VMEM((ITEMS, 1, ROWS), F32),
            pltpu.VMEM((2, 1, ROWS), F32),
            pltpu.VMEM((2, 1, ROWS), F32),
            pltpu.VMEM((2, 1, ROWS), F32),
            pltpu.VMEM((2, ROWS, HEAD_SIZE), F32),
            pltpu.VMEM((2, CHUNK, 512), BF16),
            pltpu.VMEM((2, TILE, HEAD_SIZE), F32),
            pltpu.VMEM((2, 16) + block, BF16),
            pltpu.VMEM((16,) + block, BF16),
            pltpu.VMEM((4, 3) + block, BF16),
            pltpu.VMEM((4, 2, TILE, HEAD_SIZE), BF16),
            pltpu.VMEM((4, 2) + block, BF16),
            pltpu.VMEM((4,) + block, BF16),
            pltpu.VMEM((2, 4, 64, 512), BF16),
            DMA((2, 4)), DMA((4, 2)),
            DMA((2, 4)), DMA((2, 4)),
            DMA((3,)), DMA((3,)),
            DMA((4, 4)), DMA((4, 4)),
            DMA((16,)), DMA((16,)),
            DMA((16,)), DMA((16,)),
            DMA((4, 4)), DMA((4, 4)),
            DMA((4, 4, 2)), DMA((2, 4, 4)),
            DMA((4,)), DMA((4,)),
        ],
        compiler_params=pltpu.CompilerParams(
            collective_id=0, has_side_effects=True, vmem_limit_bytes=58 << 20
        ),
        name="attention_backward",
    )(turn_ids.reshape(64, CHUNK), queries, keys, values, grad_out)


def solution(mesh):
    spread = P(("blk", "head"), None)
    return jax.shard_map(
        body,
        mesh=mesh,
        in_specs=(spread,) * 4 + (P(),),
        out_specs=(spread,) * 3,
        check_vma=False,
    )
```

```python
import math

import jax
import jax.numpy as jnp
from jax import lax
from jax.experimental import pallas as pl
from jax.experimental.pallas import tpu as pltpu
from jax.sharding import PartitionSpec as P

HEAD_SIZE = 128
CHUNK = 128
TILE = 256
PER_GROUP = 4
ROWS = PER_GROUP * CHUNK
ITEMS = 33
HIDDEN = -1e30
FACTOR = HEAD_SIZE**-0.5
BF16 = jnp.bfloat16
F32 = jnp.float32
MESH = pl.DeviceIdType.MESH

NEAR_FIRST = (
    (0, 0), (-1, 0), (1, 0), (0, -1), (0, 1), (-1, -1), (-1, 1), (1, -1), (1, 1),
    (2, 0), (0, 2), (2, -1), (2, 1), (-1, 2), (1, 2), (2, 2),
)
FAR_FIRST = (
    (2, 2), (1, 2), (-1, 2), (2, 1), (2, -1), (0, 2), (2, 0), (0, 1), (0, -1), (1, 0), (-1, 0),
    (1, 1), (1, -1), (-1, 1), (-1, -1), (0, 0),
)


def device(x, y, z, core):
    return (lax.div(z, 2) * 32 + x * 8 + y * 2 + core, lax.rem(z, 2))


def wrap(a):
    return lax.rem(a + 4, 4)


def send(src, dst, send_sem, recv_sem, target):
    return pltpu.make_async_remote_copy(
        src_ref=src,
        dst_ref=dst,
        send_sem=send_sem,
        recv_sem=recv_sem,
        device_id=target,
        device_id_type=MESH,
    )


def arrived(ref, sem):
    pltpu.make_async_copy(ref, ref, sem).wait()


def greet(x, y, z, core):
    others = []
    for r in range(4):
        other_z = lax.rem(z + r, 4)
        if r:
            others.append(device(x, y, other_z, core))
            others.append(device(wrap(x + r * (1 - core)), wrap(y + r * core), z, core))
        others.append(device(x, y, other_z, 1 - core))
        others.append(device(3 - x, 3 - y, other_z, 1 - core))
    for step in (-1, 1):
        others.append(device(wrap(x + step * core), wrap(y + step * (1 - core)), z, core))
    barrier = pltpu.get_barrier_semaphore()
    for other in others:
        pl.semaphore_signal(barrier, inc=1, device_id=other, device_id_type=MESH)
    pl.semaphore_wait(barrier, len(others))


def codes(order, axis):
    digits = [step[axis] % 4 for step in order]
    return [sum(digit * 4**i for i, digit in enumerate(digits[at : at + 8])) for at in (0, 8)]


def at_most(a, b):
    return lax.div(b - a + 16, 16)


def kernel(
    turn_ref, q_ref, k_ref, v_ref, o_ref, dq_out, last,
    kv, landed, qs, os, weights, probs_grad, tile_max, top, total, dot, dq_acc, dq_own,
    term, partial, twin, sums, one, two, line,
    kv_send, kv_recv, qo_send, qo_recv, first_send, first_recv, second_send, second_recv,
    twin_send, twin_recv, back_send, back_recv, ring_send, ring_recv, last_send, last_recv,
    dq_send, dq_recv,
):
    blk = lax.axis_index("blk")
    z_lo = lax.axis_index("head")
    z_hi = lax.div(blk, 32)
    part = lax.rem(blk, 32)
    x = lax.div(part, 8)
    y = lax.rem(lax.div(part, 2), 4)
    core = lax.rem(part, 2)
    z = z_hi * 2 + z_lo
    here = x * 4 + y
    first, second = x + core * (y - x), y + core * (x - y)

    def index(i, j):
        return (i + core * (j - i)) * 4 + j + core * (i - j)

    def target(i, j):
        return device(i + core * (j - i), j + core * (i - j), z, core)

    other_core = device(x, y, z, 1 - core)
    odd = lax.rem(z, 2)
    my_part = part + odd * (31 - 2 * part)
    my_block = lax.div(my_part, 2)

    greet(x, y, z, core)

    def go(src, dst, send_sem, recv_sem, to):
        send(src, dst, send_sem, recv_sem, to).start()

    def go_or_keep(own, src, dst, send_sem, recv_sem, to):
        @pl.when(own)
        def _():
            pltpu.make_async_copy(src, dst, recv_sem).start()

        @pl.when(jnp.logical_not(own))
        def _():
            send(src, dst, send_sem, recv_sem, to).start()

    rows = pl.ds(pl.multiple_of(core * 128 + z_lo * 64, 64), 64)
    for r in (2, 1, 3, 0):
        other_z = lax.rem(z + r, 4)
        columns = pl.ds(pl.multiple_of(other_z * 128, 128), 128)
        for role, ref in ((0, k_ref), (1, v_ref)):
            dst = kv.at[role, here, z_hi, rows]
            args = (ref.at[:, columns], dst, kv_send.at[role, r], kv_recv.at[z, core])
            if r:
                go(*args, device(x, y, other_z, role))
            else:
                go_or_keep(core == role, *args, device(x, y, z, role))

    own_rows = pl.ds(pl.multiple_of(z_lo * 64, 64), 64)
    for r in (2, 1, 3, 0):
        other_z = lax.rem(z + r, 4)
        flip = lax.rem(z_hi + other_z, 2)
        to = device(x + flip * (3 - 2 * x), y + flip * (3 - 2 * y), other_z, core + flip * (1 - 2 * core))
        columns = pl.ds(pl.multiple_of(other_z * 512, 512), 512)
        for role, ref in ((0, q_ref), (1, o_ref)):
            args = (ref.at[:, columns], landed.at[role, z_hi, own_rows], qo_send.at[role, r], qo_recv.at[role, z])
            if r:
                go(*args, to)
            else:
                go_or_keep(flip == 0, *args, to)

    up, down = wrap(first + 1), wrap(first - 1)
    left, right = wrap(second - 1), wrap(second + 1)
    firsts = (first, down, up, wrap(first + 2))
    steps = (0, -1, 1, 2)
    near = {step: n for n, step in enumerate(NEAR_FIRST)}
    far = {step: n for n, step in enumerate(FAR_FIRST)}

    def slot_of(table, a, b):
        return table[a, b] + core * (table[b, a] - table[a, b])

    def block(i, j):
        return kv.at[core, index(i, j)]

    def half(i, j, h):
        return kv.at[core, index(i, j), h]

    def share(i, j, a, b):
        slot = slot_of(near, a, b)
        go(block(i, j), block(i, j), twin_send.at[slot], twin_recv.at[slot], other_core)

    def relay(src, sems, to):
        go(src, src, *sems, to)

    def spread(k):
        i = firsts[k]
        own = block(i, second)
        relay(own, (second_send.at[k, 0], second_recv.at[k, 0]), target(first, right))
        relay(own, (second_send.at[k, 1], second_recv.at[k, 1]), target(first, left))
        share(i, second, steps[k], 0)

    def begin():
        for other_z in range(4):
            for c in range(2):
                arrived(
                    kv.at[core, here, other_z // 2, pl.ds(c * 128 + (other_z % 2) * 64, 64)],
                    kv_recv.at[other_z, c],
                )
        own = block(first, second)
        for slot, i in enumerate((up, down, firsts[3])):
            relay(own, (first_send.at[slot], first_recv.at[slot]), target(i, second))
        spread(0)

    def first_hop(k):
        arrived(block(firsts[k], second), first_recv.at[k - 1])
        spread(k)

    def second_hop(k):
        i = firsts[k]
        arrived(block(i, left), second_recv.at[k, 0])
        relay(half(i, left, 0), (second_send.at[k, 2], second_recv.at[k, 2]), target(first, right))
        share(i, left, steps[k], -1)
        arrived(block(i, right), second_recv.at[k, 1])
        relay(half(i, right, 1), (second_send.at[k, 3], second_recv.at[k, 3]), target(first, left))
        share(i, right, steps[k], 1)

    def last_hop(k):
        i, j = firsts[k], wrap(second + 2)
        arrived(half(i, j, 0), second_recv.at[k, 2])
        arrived(half(i, j, 1), second_recv.at[k, 3])
        share(i, j, steps[k], 2)

    def queries_here():
        for role in range(2):
            for other_z in range(4):
                arrived(
                    landed.at[role, other_z // 2, pl.ds((other_z % 2) * 64, 64)],
                    qo_recv.at[role, other_z],
                )
        for s in range(2):
            for h in range(PER_GROUP):
                lanes, lines = pl.ds(h * 128, 128), pl.ds(h * CHUNK, CHUNK)
                qs[s, lines, :] = landed[0, s, :, lanes]
                os[s, lines, :] = landed[1, s, :, lanes]

    gather_events = {
        0: (begin, queries_here),
        1: (lambda: first_hop(1), lambda: first_hop(2), lambda: second_hop(0)),
        3: (lambda: first_hop(3),),
        5: (lambda: second_hop(1),),
        6: (lambda: second_hop(2),),
        7: (lambda: last_hop(0),),
        8: (lambda: second_hop(3),),
        10: (lambda: last_hop(1),),
        11: (lambda: last_hop(2),),
        12: (lambda: last_hop(3),),
    }

    def run(events, n):
        for at, actions in events.items():

            @pl.when(n == at)
            def _():
                for action in actions:
                    action()

    def block_of(code_x, code_y):
        return lax.rem(x + lax.rem(code_x, 4), 4) * 4 + lax.rem(y + lax.rem(code_y, 4), 4)

    def over_blocks(order, step):
        (start_x, more_x), (start_y, more_y) = codes(order, 0), codes(order, 1)

        def turn(n, carried):
            code_x, code_y = carried
            step(n, block_of(code_x, code_y))
            middle = lax.div(n + 1, 8) - lax.div(n + 1, 9)
            return lax.div(code_x, 4) + middle * more_x, lax.div(code_y, 4) + middle * more_y

        lax.fori_loop(0, 16, turn, (start_x + 0 * x, start_y + 0 * x))

    def items_of(b):
        return 1 + at_most(b, my_block) + at_most(b, 15 - my_block)

    def item(b, r):
        is_a = lax.rem(r, 2) * at_most(b, my_block)
        late = lax.div(r + 1, 2) - is_a
        return 1 - is_a, late, b + 16 * is_a + late * (32 - 2 * b)

    scale = FACTOR * math.log2(math.e)
    top[...] = jnp.full(top.shape, HIDDEN, F32)
    total[...] = jnp.zeros_like(total)
    dot[...] = jnp.zeros_like(dot)
    dq_acc[...] = jnp.zeros_like(dq_acc)

    def stats_step(n, b):
        run(gather_events, n)
        arrived(kv.at[1 - core, b], twin_recv.at[n])

        def stats(r, _):
            s, late, number = item(b, r)
            tile = late * 16 + b
            chunk = my_part + s * (63 - 2 * my_part)
            query_pos = chunk * CHUNK + lax.broadcasted_iota(jnp.int32, (1, CHUNK), 1)
            query_turn = turn_ref[pl.ds(chunk, 1), :]
            key_turn = jnp.concatenate(
                [
                    jnp.broadcast_to(turn_ref[pl.ds(2 * tile + i, 1), :], (128, 128)).T
                    for i in range(2)
                ],
                axis=0,
            )
            key_pos = tile * TILE + lax.broadcasted_iota(jnp.int32, (TILE, CHUNK), 0)
            visible = (key_pos <= query_pos) & (
                (key_turn == query_turn) | ((key_turn & 1) == 0)
            )
            logits = lax.dot_general(
                kv[0, b, late], qs[s], (((1,), (1,)), ((), ())), preferred_element_type=F32
            )
            bias = jnp.where(visible, 0.0, HIDDEN)
            logits = logits * scale + jnp.concatenate([bias] * PER_GROUP, axis=1)
            old_top = top[s]
            new_top = jnp.maximum(old_top, jnp.max(logits, axis=0, keepdims=True))
            shrink = jnp.exp2(old_top - new_top)
            weight = jnp.exp2(logits - new_top)
            grads = lax.dot_general(
                kv[1, b, late], os[s], (((1,), (1,)), ((), ())), preferred_element_type=F32
            )
            weights[number] = weight.astype(BF16)
            probs_grad[number] = grads.astype(BF16)
            tile_max[number] = new_top
            top[s] = new_top
            total[s] = total[s] * shrink + jnp.sum(weight, axis=0, keepdims=True)
            dot[s] = dot[s] * shrink + jnp.sum(weight * grads, axis=0, keepdims=True)
            return 0

        lax.fori_loop(0, items_of(b), stats, 0)

    over_blocks(NEAR_FIRST, stats_step)
    for s in range(2):
        inverse = 1.0 / total[s]
        total[s] = inverse
        dot[s] = dot[s] * inverse

    across = (wrap(second + 2), right, left, second)
    jumps = (2, 1, -1, 0)

    def chip_sum(a, b):
        i, j = firsts[a], across[b]
        at = index(i, j)
        arrived(twin.at[at], back_recv.at[slot_of(far, steps[a], jumps[b])])
        return partial[core, at].astype(F32) + twin[at].astype(F32)

    def ring_one(a):
        sums[a, 0] = chip_sum(a, 0).astype(BF16)
        for h, to in ((0, right), (1, left)):
            go(sums.at[a, 0, h], one.at[a, h], ring_send.at[a, h], ring_recv.at[a, h], target(first, to))

    def ring_two(a):
        for b, to in ((1, right), (2, left)):
            h = b - 1
            value = chip_sum(a, b)
            arrived(one.at[a, h], ring_recv.at[a, h])
            sums[a, b, 1 - h] = value[1 - h].astype(BF16)
            sums[a, b, h] = (value[h] + one[a, h].astype(F32)).astype(BF16)
            go(sums.at[a, b], two.at[a, h], ring_send.at[a, 2 + h], ring_recv.at[a, 2 + h], target(first, to))

    def home(a):
        value = chip_sum(a, 3)
        arrived(two.at[a, 0], ring_recv.at[a, 2])
        arrived(two.at[a, 1], ring_recv.at[a, 3])
        value = value + two[a, 0].astype(F32) + two[a, 1].astype(F32)
        line[a] = value.astype(BF16)
        i = firsts[a]
        bx, by = i + core * (second - i), second + core * (i - second)
        for other_z in range(4):
            for c in range(2):
                src = line.at[a, other_z // 2, pl.ds(c * 128 + (other_z % 2) * 64, 64)]
                dst = last.at[core, a, :, pl.ds(pl.multiple_of(z * 128, 128), 128)]
                args = (src, dst, last_send.at[a, other_z, c], last_recv.at[core, a, z])
                to = device(bx, by, other_z, c)
                if a:
                    go(*args, to)
                else:
                    go_or_keep((z == other_z) & (core == c), *args, to)

    reduce_events = {
        1: (lambda: ring_one(3),),
        4: (lambda: ring_one(2),),
        5: (lambda: ring_one(1),),
        6: (lambda: ring_two(3),),
        7: (lambda: ring_one(0),),
        12: (lambda: ring_two(0), lambda: home(3)),
        14: (lambda: ring_two(2),),
        15: (lambda: ring_two(1),),
    }

    def backward_step(n, b):
        def terms(r, _):
            s, late, number = item(b, r)
            by = jnp.exp2(tile_max[number] - top[s]) * total[s]
            attention = weights[number].astype(F32) * by
            logit_grad = (attention * (probs_grad[number].astype(F32) - dot[s])).astype(BF16)
            key_term = jnp.dot(logit_grad, qs[s], preferred_element_type=F32) * FACTOR
            value_term = jnp.dot(attention.astype(BF16), os[s], preferred_element_type=F32)
            dq_acc[s] += lax.dot_general(
                logit_grad, kv[0, b, late], (((0,), (0,)), ((), ())), preferred_element_type=F32
            )
            key_term += jnp.where(s == 0, term[0], 0.0)
            value_term += jnp.where(s == 0, term[1], 0.0)
            term[0] = key_term
            term[1] = value_term
            partial[0, b, late] = key_term.astype(BF16)
            partial[1, b, late] = value_term.astype(BF16)
            return 0

        lax.fori_loop(0, items_of(b), terms, 0)

        @pl.when(b > 15 - my_block)
        def _():
            partial[0, b, 1] = jnp.zeros((TILE, HEAD_SIZE), BF16)
            partial[1, b, 1] = jnp.zeros((TILE, HEAD_SIZE), BF16)

        send(partial.at[1 - core, b], twin.at[b], back_send.at[n], back_recv.at[n], other_core).start()
        run(reduce_events, n)

    term[...] = jnp.zeros_like(term)
    over_blocks(FAR_FIRST, backward_step)

    for s in range(2):
        for h in range(PER_GROUP):
            dq_own[s, :, pl.ds(h * 128, 128)] = (
                dq_acc[s, pl.ds(h * CHUNK, CHUNK), :] * FACTOR
            ).astype(BF16)
    for other_z in range(4):
        s = other_z // 2
        flip = lax.rem(s + odd, 2)
        to = device(x + flip * (3 - 2 * x), y + flip * (3 - 2 * y), other_z, core + flip * (1 - 2 * core))
        go_or_keep(
            (flip == 0) & (z == other_z),
            dq_own.at[s, pl.ds((other_z % 2) * 64, 64)],
            dq_out.at[:, pl.ds(pl.multiple_of(z * 512, 512), 512)],
            dq_send.at[other_z], dq_recv.at[z], to,
        )
    home(2)
    home(1)
    home(0)

    for role in range(2):
        for a in range(4):
            for other_z in range(4):
                arrived(last.at[role, a, :, pl.ds(other_z * 128, 128)], last_recv.at[role, a, other_z])
    for other_z in range(4):
        arrived(dq_out.at[:, pl.ds(other_z * 512, 512)], dq_recv.at[other_z])

    whole, halved, piece = kv.at[0, 0], kv.at[0, 0, 0], line.at[0, 0, pl.ds(0, 64)]
    for r in range(1, 4):
        for role in range(2):
            arrived(k_ref.at[:, pl.ds(0, 128)], kv_send.at[role, r])
            arrived(q_ref.at[:, pl.ds(0, 512)], qo_send.at[role, r])
        arrived(whole, first_send.at[r - 1])
        for other_z in range(4):
            for c in range(2):
                arrived(piece, last_send.at[r, other_z, c])
    for k in range(4):
        for h in range(2):
            arrived(whole, second_send.at[k, h])
            arrived(halved, second_send.at[k, 2 + h])
            arrived(halved, ring_send.at[k, h])
            arrived(whole, ring_send.at[k, 2 + h])
    for n in range(16):
        arrived(whole, twin_send.at[n])
        arrived(whole, back_send.at[n])

    @pl.when(core == 0)
    def _():
        arrived(v_ref.at[:, pl.ds(0, 128)], kv_send.at[1, 0])

    @pl.when(core == 1)
    def _():
        arrived(k_ref.at[:, pl.ds(0, 128)], kv_send.at[0, 0])

    @pl.when(lax.rem(z_hi + z_lo, 2) == 1)
    def _():
        for role in range(2):
            arrived(q_ref.at[:, pl.ds(0, 512)], qo_send.at[role, 0])

    for other_z in range(4):
        for c in range(2):

            @pl.when(jnp.logical_not((z == other_z) & (core == c)))
            def _():
                arrived(piece, last_send.at[0, other_z, c])

        flip = lax.rem(other_z // 2 + odd, 2)

        @pl.when(jnp.logical_not((flip == 0) & (z == other_z)))
        def _():
            arrived(dq_own.at[0, pl.ds(0, 64)], dq_send.at[other_z])


def finish_kernel(dq_ref, dkv_ref, dq_out, dk_out, dv_out):
    dq_out[...] = dq_ref[...]
    for role, out in ((0, dk_out), (1, dv_out)):
        value = dkv_ref[role, 0].astype(F32)
        for a in range(1, 4):
            value = value + dkv_ref[role, a].astype(F32)
        out[...] = value.astype(BF16)


ANY = pl.BlockSpec(memory_space=pl.ANY)
VMEM = pl.BlockSpec(memory_space=pltpu.VMEM)
DMA = pltpu.SemaphoreType.DMA


def body(queries, keys, values, grad_out, turn_ids):
    block = (2, TILE, HEAD_SIZE)
    dq, dkv = pl.pallas_call(
        kernel,
        out_shape=(
            jax.ShapeDtypeStruct((64, 2048), BF16),
            jax.ShapeDtypeStruct((2, 4, 64, 512), BF16),
        ),
        in_specs=[VMEM] + [ANY] * 4,
        out_specs=(ANY, ANY),
        scratch_shapes=[
            pltpu.VMEM((2, 16) + block, BF16),
            pltpu.VMEM((2, 2, CHUNK, 512), BF16),
            pltpu.VMEM((2, ROWS, HEAD_SIZE), BF16),
            pltpu.VMEM((2, ROWS, HEAD_SIZE), BF16),
            pltpu.VMEM((ITEMS, TILE, ROWS), BF16),
            pltpu.VMEM((ITEMS, TILE, ROWS), BF16),
            pltpu.VMEM((ITEMS, 1, ROWS), F32),
            pltpu.VMEM((2, 1, ROWS), F32),
            pltpu.VMEM((2, 1, ROWS), F32),
            pltpu.VMEM((2, 1, ROWS), F32),
            pltpu.VMEM((2, ROWS, HEAD_SIZE), F32),
            pltpu.VMEM((2, CHUNK, 512), BF16),
            pltpu.VMEM((2, TILE, HEAD_SIZE), F32),
            pltpu.VMEM((2, 16) + block, BF16),
            pltpu.VMEM((16,) + block, BF16),
            pltpu.VMEM((4, 3) + block, BF16),
            pltpu.VMEM((4, 2, TILE, HEAD_SIZE), BF16),
            pltpu.VMEM((4, 2) + block, BF16),
            pltpu.VMEM((4,) + block, BF16),
            DMA((2, 4)), DMA((4, 2)),
            DMA((2, 4)), DMA((2, 4)),
            DMA((3,)), DMA((3,)),
            DMA((4, 4)), DMA((4, 4)),
            DMA((16,)), DMA((16,)),
            DMA((16,)), DMA((16,)),
            DMA((4, 4)), DMA((4, 4)),
            DMA((4, 4, 2)), DMA((2, 4, 4)),
            DMA((4,)), DMA((4,)),
        ],
        compiler_params=pltpu.CompilerParams(
            collective_id=0, has_side_effects=True, vmem_limit_bytes=58 << 20
        ),
        name="attention_backward",
    )(turn_ids.reshape(64, CHUNK), queries, keys, values, grad_out)
    return pl.pallas_call(
        finish_kernel,
        out_shape=(
            jax.ShapeDtypeStruct((64, 2048), BF16),
            jax.ShapeDtypeStruct((64, 512), BF16),
            jax.ShapeDtypeStruct((64, 512), BF16),
        ),
        in_specs=[VMEM] * 2,
        out_specs=(VMEM,) * 3,
        compiler_params=pltpu.CompilerParams(vmem_limit_bytes=60 << 20),
        name="finish",
    )(dq, dkv)


def solution(mesh):
    spread = P(("blk", "head"), None)
    return jax.shard_map(
        body,
        mesh=mesh,
        in_specs=(spread,) * 4 + (P(),),
        out_specs=(spread,) * 3,
        check_vma=False,
    )
```

```python
import math

import jax
import jax.numpy as jnp
from jax import lax
from jax.experimental import pallas as pl
from jax.experimental.pallas import tpu as pltpu
from jax.sharding import PartitionSpec as P

HEAD_SIZE = 128
CHUNK = 128
TILE = 256
PER_GROUP = 4
ROWS = PER_GROUP * CHUNK
ITEMS = 33
HIDDEN = -1e30
FACTOR = HEAD_SIZE**-0.5
BF16 = jnp.bfloat16
F32 = jnp.float32
MESH = pl.DeviceIdType.MESH

NEAR_FIRST = (
    (0, 0), (-1, 0), (1, 0), (0, -1), (0, 1), (-1, -1), (-1, 1), (1, -1), (1, 1),
    (2, 0), (0, 2), (2, -1), (2, 1), (-1, 2), (1, 2), (2, 2),
)
FAR_FIRST = (
    (2, 2), (1, 2), (-1, 2), (2, 1), (2, -1), (0, 2), (2, 0), (0, 1), (0, -1), (1, 0), (-1, 0),
    (1, 1), (1, -1), (-1, 1), (-1, -1), (0, 0),
)


def device(x, y, z, core):
    return (lax.div(z, 2) * 32 + x * 8 + y * 2 + core, lax.rem(z, 2))


def wrap(a):
    return lax.rem(a + 4, 4)


def send(src, dst, send_sem, recv_sem, target):
    return pltpu.make_async_remote_copy(
        src_ref=src,
        dst_ref=dst,
        send_sem=send_sem,
        recv_sem=recv_sem,
        device_id=target,
        device_id_type=MESH,
    )


def arrived(ref, sem):
    pltpu.make_async_copy(ref, ref, sem).wait()


def greet(x, y, z, core):
    others = []
    for r in range(4):
        other_z = lax.rem(z + r, 4)
        if r:
            others.append(device(x, y, other_z, core))
        others.append(device(x, y, other_z, 1 - core))
        others.append(device(3 - x, 3 - y, other_z, 1 - core))
    for step in (-1, 1):
        others.append(device(wrap(x + step), y, z, core))
        others.append(device(x, wrap(y + step), z, core))
    barrier = pltpu.get_barrier_semaphore()
    for other in others:
        pl.semaphore_signal(barrier, inc=1, device_id=other, device_id_type=MESH)
    pl.semaphore_wait(barrier, len(others))


def codes(order, axis):
    digits = [step[axis] % 4 for step in order]
    return [sum(digit * 4**i for i, digit in enumerate(digits[at : at + 8])) for at in (0, 8)]


def at_most(a, b):
    return lax.div(b - a + 16, 16)


def kernel(
    turn_ref, q_ref, k_ref, v_ref, o_ref, dq_out, last,
    kv, landed, qs, os, weights, probs_grad, tile_max, top, total, dot, dq_acc, dq_own,
    partial, twin, sums, one, two, line, line_in,
    kv_send, kv_recv, qo_send, qo_recv, first_send, first_recv, second_send, second_recv,
    twin_send, twin_recv, back_send, back_recv, ring_send, ring_recv, last_send, last_recv,
    line_send, line_recv,     dq_send, dq_recv,
):
    blk = lax.axis_index("blk")
    z_lo = lax.axis_index("head")
    z_hi = lax.div(blk, 32)
    part = lax.rem(blk, 32)
    x = lax.div(part, 8)
    y = lax.rem(lax.div(part, 2), 4)
    core = lax.rem(part, 2)
    z = z_hi * 2 + z_lo
    here = x * 4 + y
    first, second = x + core * (y - x), y + core * (x - y)

    def index(i, j):
        return (i + core * (j - i)) * 4 + j + core * (i - j)

    def target(i, j):
        return device(i + core * (j - i), j + core * (i - j), z, core)

    other_core = device(x, y, z, 1 - core)
    odd = lax.rem(z, 2)
    my_part = part + odd * (31 - 2 * part)
    my_block = lax.div(my_part, 2)

    greet(x, y, z, core)

    def go(src, dst, send_sem, recv_sem, to):
        send(src, dst, send_sem, recv_sem, to).start()

    def go_or_keep(own, src, dst, send_sem, recv_sem, to):
        @pl.when(own)
        def _():
            pltpu.make_async_copy(src, dst, recv_sem).start()

        @pl.when(jnp.logical_not(own))
        def _():
            send(src, dst, send_sem, recv_sem, to).start()

    rows = pl.ds(pl.multiple_of(core * 128 + z_lo * 64, 64), 64)
    for r in (2, 1, 3, 0):
        other_z = lax.rem(z + r, 4)
        columns = pl.ds(pl.multiple_of(other_z * 128, 128), 128)
        for role, ref in ((0, k_ref), (1, v_ref)):
            dst = kv.at[role, here, z_hi, rows]
            args = (ref.at[:, columns], dst, kv_send.at[role, r], kv_recv.at[z, core])
            if r:
                go(*args, device(x, y, other_z, role))
            else:
                go_or_keep(core == role, *args, device(x, y, z, role))

    own_rows = pl.ds(pl.multiple_of(z_lo * 64, 64), 64)
    for r in (2, 1, 3, 0):
        other_z = lax.rem(z + r, 4)
        flip = lax.rem(z_hi + other_z, 2)
        to = device(x + flip * (3 - 2 * x), y + flip * (3 - 2 * y), other_z, core + flip * (1 - 2 * core))
        columns = pl.ds(pl.multiple_of(other_z * 512, 512), 512)
        for role, ref in ((0, q_ref), (1, o_ref)):
            args = (ref.at[:, columns], landed.at[role, z_hi, own_rows], qo_send.at[role, r], qo_recv.at[role, z])
            if r:
                go(*args, to)
            else:
                go_or_keep(flip == 0, *args, to)

    up, down = wrap(first + 1), wrap(first - 1)
    left, right = wrap(second - 1), wrap(second + 1)
    firsts = (first, down, up, wrap(first + 2))
    steps = (0, -1, 1, 2)
    near = {step: n for n, step in enumerate(NEAR_FIRST)}
    far = {step: n for n, step in enumerate(FAR_FIRST)}

    def slot_of(table, a, b):
        return table[a, b] + core * (table[b, a] - table[a, b])

    def block(i, j):
        return kv.at[core, index(i, j)]

    def half(i, j, h):
        return kv.at[core, index(i, j), h]

    def share(i, j, a, b):
        slot = slot_of(near, a, b)
        go(block(i, j), block(i, j), twin_send.at[slot], twin_recv.at[slot], other_core)

    def relay(src, sems, to):
        go(src, src, *sems, to)

    def spread(k):
        i = firsts[k]
        own = block(i, second)
        relay(own, (second_send.at[k, 0], second_recv.at[k, 0]), target(first, right))
        relay(own, (second_send.at[k, 1], second_recv.at[k, 1]), target(first, left))
        share(i, second, steps[k], 0)

    def begin():
        for other_z in range(4):
            for c in range(2):
                arrived(
                    kv.at[core, here, other_z // 2, pl.ds(c * 128 + (other_z % 2) * 64, 64)],
                    kv_recv.at[other_z, c],
                )
        own = block(first, second)
        relay(own, (first_send.at[0], first_recv.at[0]), target(up, second))
        relay(own, (first_send.at[1], first_recv.at[1]), target(down, second))
        spread(0)

    def first_hop(k):
        if k < 3:
            h, to = k - 1, (up, down)[k - 1]
            arrived(block(firsts[k], second), first_recv.at[h])
            relay(half(firsts[k], second, h), (first_send.at[2 + h], first_recv.at[2 + h]), target(to, second))
        else:
            for h in range(2):
                arrived(half(firsts[k], second, h), first_recv.at[2 + h])
        spread(k)

    def second_hop(k):
        i = firsts[k]
        arrived(block(i, left), second_recv.at[k, 0])
        relay(half(i, left, 0), (second_send.at[k, 2], second_recv.at[k, 2]), target(first, right))
        share(i, left, steps[k], -1)
        arrived(block(i, right), second_recv.at[k, 1])
        relay(half(i, right, 1), (second_send.at[k, 3], second_recv.at[k, 3]), target(first, left))
        share(i, right, steps[k], 1)

    def last_hop(k):
        i, j = firsts[k], wrap(second + 2)
        arrived(half(i, j, 0), second_recv.at[k, 2])
        arrived(half(i, j, 1), second_recv.at[k, 3])
        share(i, j, steps[k], 2)

    def queries_here():
        for role in range(2):
            for other_z in range(4):
                arrived(
                    landed.at[role, other_z // 2, pl.ds((other_z % 2) * 64, 64)],
                    qo_recv.at[role, other_z],
                )
        for s in range(2):
            for h in range(PER_GROUP):
                lanes, lines = pl.ds(h * 128, 128), pl.ds(h * CHUNK, CHUNK)
                qs[s, lines, :] = landed[0, s, :, lanes]
                os[s, lines, :] = landed[1, s, :, lanes]

    gather_events = {
        0: (begin, queries_here),
        1: (lambda: first_hop(1), lambda: first_hop(2), lambda: second_hop(0)),
        3: (lambda: first_hop(3),),
        5: (lambda: second_hop(1),),
        6: (lambda: second_hop(2),),
        7: (lambda: last_hop(0),),
        8: (lambda: second_hop(3),),
        10: (lambda: last_hop(1),),
        11: (lambda: last_hop(2),),
        12: (lambda: last_hop(3),),
    }

    def run(events, n):
        for at, actions in events.items():

            @pl.when(n == at)
            def _():
                for action in actions:
                    action()

    def block_of(code_x, code_y):
        return lax.rem(x + lax.rem(code_x, 4), 4) * 4 + lax.rem(y + lax.rem(code_y, 4), 4)

    def over_blocks(order, step):
        (start_x, more_x), (start_y, more_y) = codes(order, 0), codes(order, 1)

        def turn(n, carried):
            code_x, code_y = carried
            step(n, block_of(code_x, code_y))
            middle = lax.div(n + 1, 8) - lax.div(n + 1, 9)
            return lax.div(code_x, 4) + middle * more_x, lax.div(code_y, 4) + middle * more_y

        lax.fori_loop(0, 16, turn, (start_x + 0 * x, start_y + 0 * x))

    def in_full(b, work):
        kind = at_most(b, my_block) + 2 * at_most(b, 15 - my_block)
        for number in range(4):

            @pl.when(kind == number)
            def _():
                work(number % 2, number // 2)

    def tiles_of(s, with_late):
        return (0, 1) if s and with_late else (0,)

    def number_of(b, s, late):
        return (32 - b) if late else b + 16 * (1 - s)

    scale = FACTOR * math.log2(math.e)
    top[...] = jnp.full(top.shape, HIDDEN, F32)
    total[...] = jnp.zeros_like(total)
    dot[...] = jnp.zeros_like(dot)
    dq_acc[...] = jnp.zeros_like(dq_acc)

    def stats_step(n, b):
        run(gather_events, n)
        arrived(kv.at[1 - core, b], twin_recv.at[n])

        def stats(with_a, with_late):
            key_turns = [
                jnp.concatenate(
                    [
                        jnp.broadcast_to(turn_ref[pl.ds(2 * (late * 16 + b) + i, 1), :], (128, 128)).T
                        for i in range(2)
                    ],
                    axis=0,
                )
                for late in range(1 + with_late)
            ]
            for s in (1, 0) if with_a else (1,):
                chunk = my_part if s == 0 else 63 - my_part
                query_pos = chunk * CHUNK + lax.broadcasted_iota(jnp.int32, (1, CHUNK), 1)
                query_turn = turn_ref[pl.ds(chunk, 1), :]
                old_top = top[s]
                new_top = old_top
                parts = []
                for late in tiles_of(s, with_late):
                    key_turn = key_turns[late]
                    key_pos = (late * 16 + b) * TILE + lax.broadcasted_iota(
                        jnp.int32, (TILE, CHUNK), 0
                    )
                    visible = (key_pos <= query_pos) & (
                        (key_turn == query_turn) | ((key_turn & 1) == 0)
                    )
                    logits = lax.dot_general(
                        kv[0, b, late], qs[s], (((1,), (1,)), ((), ())), preferred_element_type=F32
                    )
                    bias = jnp.where(visible, 0.0, HIDDEN)
                    logits = logits * scale + jnp.concatenate([bias] * PER_GROUP, axis=1)
                    new_top = jnp.maximum(new_top, jnp.max(logits, axis=0, keepdims=True))
                    grads = lax.dot_general(
                        kv[1, b, late], os[s], (((1,), (1,)), ((), ())), preferred_element_type=F32
                    )
                    parts.append((late, logits, grads))
                shrink = jnp.exp2(old_top - new_top)
                new_total, new_dot = total[s] * shrink, dot[s] * shrink
                for late, logits, grads in parts:
                    number = number_of(b, s, late)
                    weight = jnp.exp2(logits - new_top)
                    weights[number] = weight.astype(BF16)
                    probs_grad[number] = grads.astype(BF16)
                    tile_max[number] = new_top
                    new_total += jnp.sum(weight, axis=0, keepdims=True)
                    new_dot += jnp.sum(weight * grads, axis=0, keepdims=True)
                top[s] = new_top
                total[s] = new_total
                dot[s] = new_dot

        in_full(b, stats)

    over_blocks(NEAR_FIRST, stats_step)
    for s in range(2):
        inverse = 1.0 / total[s]
        total[s] = inverse
        dot[s] = dot[s] * inverse

    across = (wrap(second + 2), right, left, second)
    jumps = (2, 1, -1, 0)

    def chip_sum(a, b):
        i, j = firsts[a], across[b]
        at = index(i, j)
        arrived(twin.at[at], back_recv.at[slot_of(far, steps[a], jumps[b])])
        return partial[core, at].astype(F32) + twin[at].astype(F32)

    def ring_one(a):
        sums[a, 0] = chip_sum(a, 0).astype(BF16)
        for h, to in ((0, right), (1, left)):
            go(sums.at[a, 0, h], one.at[a, h], ring_send.at[a, h], ring_recv.at[a, h], target(first, to))

    def ring_two(a):
        for b, to in ((1, right), (2, left)):
            h = b - 1
            value = chip_sum(a, b)
            arrived(one.at[a, h], ring_recv.at[a, h])
            sums[a, b, 1 - h] = value[1 - h].astype(BF16)
            sums[a, b, h] = (value[h] + one[a, h].astype(F32)).astype(BF16)
            go(sums.at[a, b], two.at[a, h], ring_send.at[a, 2 + h], ring_recv.at[a, 2 + h], target(first, to))

    def home(a):
        value = chip_sum(a, 3)
        arrived(two.at[a, 0], ring_recv.at[a, 2])
        arrived(two.at[a, 1], ring_recv.at[a, 3])
        value = value + two[a, 0].astype(F32) + two[a, 1].astype(F32)
        if a == 3:
            line[a] = value.astype(BF16)
            for h, to in ((0, up), (1, down)):
                go(line.at[a, h], line_in.at[h], line_send.at[h], line_recv.at[h], target(to, second))
            return
        if a:
            h = 2 - a
            arrived(line_in.at[h], line_recv.at[h])
            line[a, 1 - h] = value[1 - h].astype(BF16)
            line[a, h] = (value[h] + line_in[h].astype(F32)).astype(BF16)
        else:
            line[a] = value.astype(BF16)
        i = firsts[a]
        bx, by = i + core * (second - i), second + core * (i - second)
        for other_z in range(4):
            for c in range(2):
                src = line.at[a, other_z // 2, pl.ds(c * 128 + (other_z % 2) * 64, 64)]
                dst = last.at[core, a, :, pl.ds(pl.multiple_of(z * 128, 128), 128)]
                args = (src, dst, last_send.at[a, other_z, c], last_recv.at[core, a, z])
                to = device(bx, by, other_z, c)
                if a:
                    go(*args, to)
                else:
                    go_or_keep((z == other_z) & (core == c), *args, to)

    reduce_events = {
        1: (lambda: ring_one(3),),
        4: (lambda: ring_one(2),),
        5: (lambda: ring_one(1),),
        6: (lambda: ring_two(3),),
        7: (lambda: ring_one(0),),
        11: (lambda: ring_two(0), lambda: home(3)),
        14: (lambda: ring_two(2),),
        15: (lambda: ring_two(1),),
    }

    def backward_step(n, b):
        def terms(with_a, with_late):
            keys_sum, values_sum = [0.0, 0.0], [0.0, 0.0]
            for s in (1, 0) if with_a else (1,):
                query_sum = dq_acc[s]
                for late in tiles_of(s, with_late):
                    number = number_of(b, s, late)
                    by = jnp.exp2(tile_max[number] - top[s]) * total[s]
                    attention = weights[number].astype(F32) * by
                    logit_grad = (attention * (probs_grad[number].astype(F32) - dot[s])).astype(BF16)
                    values_sum[late] += jnp.dot(
                        attention.astype(BF16), os[s], preferred_element_type=F32
                    )
                    keys_sum[late] += jnp.dot(logit_grad, qs[s], preferred_element_type=F32)
                    query_sum += lax.dot_general(
                        logit_grad, kv[0, b, late], (((0,), (0,)), ((), ())),
                        preferred_element_type=F32,
                    )
                dq_acc[s] = query_sum
            for late in range(2):
                if late <= with_late:
                    partial[0, b, late] = (keys_sum[late] * FACTOR).astype(BF16)
                    partial[1, b, late] = values_sum[late].astype(BF16)
                else:
                    partial[0, b, late] = jnp.zeros((TILE, HEAD_SIZE), BF16)
                    partial[1, b, late] = jnp.zeros((TILE, HEAD_SIZE), BF16)

        in_full(b, terms)
        send(partial.at[1 - core, b], twin.at[b], back_send.at[n], back_recv.at[n], other_core).start()
        run(reduce_events, n)

    over_blocks(FAR_FIRST, backward_step)

    home(0)
    for s in range(2):
        for h in range(PER_GROUP):
            dq_own[s, :, pl.ds(h * 128, 128)] = (
                dq_acc[s, pl.ds(h * CHUNK, CHUNK), :] * FACTOR
            ).astype(BF16)
    for other_z in range(4):
        s = other_z // 2
        flip = lax.rem(s + odd, 2)
        to = device(x + flip * (3 - 2 * x), y + flip * (3 - 2 * y), other_z, core + flip * (1 - 2 * core))
        go_or_keep(
            (flip == 0) & (z == other_z),
            dq_own.at[s, pl.ds((other_z % 2) * 64, 64)],
            dq_out.at[:, pl.ds(pl.multiple_of(z * 512, 512), 512)],
            dq_send.at[other_z], dq_recv.at[z], to,
        )
    home(2)
    home(1)

    for role in range(2):
        for a in range(3):
            for other_z in range(4):
                arrived(last.at[role, a, :, pl.ds(other_z * 128, 128)], last_recv.at[role, a, other_z])
    for other_z in range(4):
        arrived(dq_out.at[:, pl.ds(other_z * 512, 512)], dq_recv.at[other_z])

    whole, halved, piece = kv.at[0, 0], kv.at[0, 0, 0], line.at[0, 0, pl.ds(0, 64)]
    for r in range(1, 4):
        for role in range(2):
            arrived(k_ref.at[:, pl.ds(0, 128)], kv_send.at[role, r])
            arrived(q_ref.at[:, pl.ds(0, 512)], qo_send.at[role, r])
    for r in range(1, 3):
        for other_z in range(4):
            for c in range(2):
                arrived(piece, last_send.at[r, other_z, c])
    for h in range(2):
        arrived(whole, first_send.at[h])
        arrived(halved, first_send.at[2 + h])
        arrived(halved, line_send.at[h])
    for k in range(4):
        for h in range(2):
            arrived(whole, second_send.at[k, h])
            arrived(halved, second_send.at[k, 2 + h])
            arrived(halved, ring_send.at[k, h])
            arrived(whole, ring_send.at[k, 2 + h])
    for n in range(16):
        arrived(whole, twin_send.at[n])
        arrived(whole, back_send.at[n])

    @pl.when(core == 0)
    def _():
        arrived(v_ref.at[:, pl.ds(0, 128)], kv_send.at[1, 0])

    @pl.when(core == 1)
    def _():
        arrived(k_ref.at[:, pl.ds(0, 128)], kv_send.at[0, 0])

    @pl.when(lax.rem(z_hi + z_lo, 2) == 1)
    def _():
        for role in range(2):
            arrived(q_ref.at[:, pl.ds(0, 512)], qo_send.at[role, 0])

    for other_z in range(4):
        for c in range(2):

            @pl.when(jnp.logical_not((z == other_z) & (core == c)))
            def _():
                arrived(piece, last_send.at[0, other_z, c])

        flip = lax.rem(other_z // 2 + odd, 2)

        @pl.when(jnp.logical_not((flip == 0) & (z == other_z)))
        def _():
            arrived(dq_own.at[0, pl.ds(0, 64)], dq_send.at[other_z])


def finish_kernel(dq_ref, dkv_ref, dq_out, dk_out, dv_out):
    dq_out[...] = dq_ref[...]
    for role, out in ((0, dk_out), (1, dv_out)):
        value = dkv_ref[role, 0].astype(F32)
        for a in range(1, 3):
            value = value + dkv_ref[role, a].astype(F32)
        out[...] = value.astype(BF16)


ANY = pl.BlockSpec(memory_space=pl.ANY)
VMEM = pl.BlockSpec(memory_space=pltpu.VMEM)
DMA = pltpu.SemaphoreType.DMA


def body(queries, keys, values, grad_out, turn_ids):
    block = (2, TILE, HEAD_SIZE)
    dq, dkv = pl.pallas_call(
        kernel,
        out_shape=(
            jax.ShapeDtypeStruct((64, 2048), BF16),
            jax.ShapeDtypeStruct((2, 3, 64, 512), BF16),
        ),
        in_specs=[VMEM] + [ANY] * 4,
        out_specs=(ANY, ANY),
        scratch_shapes=[
            pltpu.VMEM((2, 16) + block, BF16),
            pltpu.VMEM((2, 2, CHUNK, 512), BF16),
            pltpu.VMEM((2, ROWS, HEAD_SIZE), BF16),
            pltpu.VMEM((2, ROWS, HEAD_SIZE), BF16),
            pltpu.VMEM((ITEMS, TILE, ROWS), BF16),
            pltpu.VMEM((ITEMS, TILE, ROWS), BF16),
            pltpu.VMEM((ITEMS, 1, ROWS), F32),
            pltpu.VMEM((2, 1, ROWS), F32),
            pltpu.VMEM((2, 1, ROWS), F32),
            pltpu.VMEM((2, 1, ROWS), F32),
            pltpu.VMEM((2, ROWS, HEAD_SIZE), F32),
            pltpu.VMEM((2, CHUNK, 512), BF16),
            pltpu.VMEM((2, 16) + block, BF16),
            pltpu.VMEM((16,) + block, BF16),
            pltpu.VMEM((4, 3) + block, BF16),
            pltpu.VMEM((4, 2, TILE, HEAD_SIZE), BF16),
            pltpu.VMEM((4, 2) + block, BF16),
            pltpu.VMEM((4,) + block, BF16),
            pltpu.VMEM(block, BF16),
            DMA((2, 4)), DMA((4, 2)),
            DMA((2, 4)), DMA((2, 4)),
            DMA((4,)), DMA((4,)),
            DMA((4, 4)), DMA((4, 4)),
            DMA((16,)), DMA((16,)),
            DMA((16,)), DMA((16,)),
            DMA((4, 4)), DMA((4, 4)),
            DMA((3, 4, 2)), DMA((2, 3, 4)),
            DMA((2,)), DMA((2,)),
            DMA((4,)), DMA((4,)),
        ],
        compiler_params=pltpu.CompilerParams(
            collective_id=0, has_side_effects=True, vmem_limit_bytes=58 << 20
        ),
        name="attention_backward",
    )(turn_ids.reshape(64, CHUNK), queries, keys, values, grad_out)
    return pl.pallas_call(
        finish_kernel,
        out_shape=(
            jax.ShapeDtypeStruct((64, 2048), BF16),
            jax.ShapeDtypeStruct((64, 512), BF16),
            jax.ShapeDtypeStruct((64, 512), BF16),
        ),
        in_specs=[VMEM] * 2,
        out_specs=(VMEM,) * 3,
        compiler_params=pltpu.CompilerParams(vmem_limit_bytes=60 << 20),
        name="finish",
    )(dq, dkv)


def solution(mesh):
    spread = P(("blk", "head"), None)
    return jax.shard_map(
        body,
        mesh=mesh,
        in_specs=(spread,) * 4 + (P(),),
        out_specs=(spread,) * 3,
        check_vma=False,
    )
```

```python
import math

import jax
import jax.numpy as jnp
from jax import lax
from jax.experimental import pallas as pl
from jax.experimental.pallas import tpu as pltpu
from jax.sharding import PartitionSpec as P

HEAD_SIZE = 128
CHUNK = 128
TILE = 256
PER_GROUP = 4
ROWS = PER_GROUP * CHUNK
ITEMS = 33
HIDDEN = -1e30
FACTOR = HEAD_SIZE**-0.5
BF16 = jnp.bfloat16
F32 = jnp.float32
MESH = pl.DeviceIdType.MESH

NEAR_FIRST = (
    (0, 0), (-1, 0), (1, 0), (0, -1), (0, 1), (-1, -1), (-1, 1), (1, -1), (1, 1),
    (2, 0), (0, 2), (2, -1), (2, 1), (-1, 2), (1, 2), (2, 2),
)
FAR_FIRST = (
    (2, 2), (1, 2), (-1, 2), (2, 1), (2, -1), (0, 2), (2, 0), (1, 1), (1, -1), (-1, 1), (-1, -1),
    (0, 1), (0, -1), (1, 0), (-1, 0), (0, 0),
)


def device(x, y, z, core):
    return (lax.div(z, 2) * 32 + x * 8 + y * 2 + core, lax.rem(z, 2))


def wrap(a):
    return lax.rem(a + 4, 4)


def send(src, dst, send_sem, recv_sem, target):
    return pltpu.make_async_remote_copy(
        src_ref=src,
        dst_ref=dst,
        send_sem=send_sem,
        recv_sem=recv_sem,
        device_id=target,
        device_id_type=MESH,
    )


def arrived(ref, sem):
    pltpu.make_async_copy(ref, ref, sem).wait()


def greet(x, y, z, core):
    others = []
    for r in range(4):
        other_z = lax.rem(z + r, 4)
        if r:
            others.append(device(x, y, other_z, core))
        others.append(device(x, y, other_z, 1 - core))
        others.append(device(3 - x, 3 - y, other_z, 1 - core))
    for step in (-1, 1):
        others.append(device(wrap(x + step), y, z, core))
        others.append(device(x, wrap(y + step), z, core))
    barrier = pltpu.get_barrier_semaphore()
    for other in others:
        pl.semaphore_signal(barrier, inc=1, device_id=other, device_id_type=MESH)
    pl.semaphore_wait(barrier, len(others))


def codes(order, axis):
    digits = [step[axis] % 4 for step in order]
    return [sum(digit * 4**i for i, digit in enumerate(digits[at : at + 8])) for at in (0, 8)]


def at_most(a, b):
    return lax.div(b - a + 16, 16)


def kernel(
    turn_ref, q_ref, k_ref, v_ref, o_ref, dq_out, last,
    kv, landed, qs, os, weights, probs_grad, tile_max, top, total, dot, dq_acc, dq_own,
    partial, twin, sums, one, two, line, line_in,
    kv_send, kv_recv, qo_send, qo_recv, first_send, first_recv, second_send, second_recv,
    twin_send, twin_recv, back_send, back_recv, ring_send, ring_recv, last_send, last_recv,
    line_send, line_recv,     dq_send, dq_recv,
):
    blk = lax.axis_index("blk")
    z_lo = lax.axis_index("head")
    z_hi = lax.div(blk, 32)
    part = lax.rem(blk, 32)
    x = lax.div(part, 8)
    y = lax.rem(lax.div(part, 2), 4)
    core = lax.rem(part, 2)
    z = z_hi * 2 + z_lo
    here = x * 4 + y
    first, second = x + core * (y - x), y + core * (x - y)

    def index(i, j):
        return (i + core * (j - i)) * 4 + j + core * (i - j)

    def target(i, j):
        return device(i + core * (j - i), j + core * (i - j), z, core)

    other_core = device(x, y, z, 1 - core)
    odd = lax.rem(z, 2)
    my_part = part + odd * (31 - 2 * part)
    my_block = lax.div(my_part, 2)

    greet(x, y, z, core)

    def go(src, dst, send_sem, recv_sem, to):
        send(src, dst, send_sem, recv_sem, to).start()

    def go_or_keep(own, src, dst, send_sem, recv_sem, to):
        @pl.when(own)
        def _():
            pltpu.make_async_copy(src, dst, recv_sem).start()

        @pl.when(jnp.logical_not(own))
        def _():
            send(src, dst, send_sem, recv_sem, to).start()

    rows = pl.ds(pl.multiple_of(core * 128 + z_lo * 64, 64), 64)
    for r in (2, 1, 3, 0):
        other_z = lax.rem(z + r, 4)
        columns = pl.ds(pl.multiple_of(other_z * 128, 128), 128)
        for role, ref in ((0, k_ref), (1, v_ref)):
            dst = kv.at[role, here, z_hi, rows]
            args = (ref.at[:, columns], dst, kv_send.at[role, r], kv_recv.at[z, core])
            if r:
                go(*args, device(x, y, other_z, role))
            else:
                go_or_keep(core == role, *args, device(x, y, z, role))

    own_rows = pl.ds(pl.multiple_of(z_lo * 64, 64), 64)
    for r in (2, 1, 3, 0):
        other_z = lax.rem(z + r, 4)
        flip = lax.rem(z_hi + other_z, 2)
        to = device(x + flip * (3 - 2 * x), y + flip * (3 - 2 * y), other_z, core + flip * (1 - 2 * core))
        columns = pl.ds(pl.multiple_of(other_z * 512, 512), 512)
        for role, ref in ((0, q_ref), (1, o_ref)):
            args = (ref.at[:, columns], landed.at[role, z_hi, own_rows], qo_send.at[role, r], qo_recv.at[role, z])
            if r:
                go(*args, to)
            else:
                go_or_keep(flip == 0, *args, to)

    up, down = wrap(first + 1), wrap(first - 1)
    left, right = wrap(second - 1), wrap(second + 1)
    firsts = (first, down, up, wrap(first + 2))
    steps = (0, -1, 1, 2)
    near = {step: n for n, step in enumerate(NEAR_FIRST)}
    far = {step: n for n, step in enumerate(FAR_FIRST)}

    def slot_of(table, a, b):
        return table[a, b] + core * (table[b, a] - table[a, b])

    def block(i, j):
        return kv.at[core, index(i, j)]

    def half(i, j, h):
        return kv.at[core, index(i, j), h]

    def share(i, j, a, b):
        slot = slot_of(near, a, b)
        go(block(i, j), block(i, j), twin_send.at[slot], twin_recv.at[slot], other_core)

    def relay(src, sems, to):
        go(src, src, *sems, to)

    def spread(k):
        i = firsts[k]
        own = block(i, second)
        relay(own, (second_send.at[k, 0], second_recv.at[k, 0]), target(first, right))
        relay(own, (second_send.at[k, 1], second_recv.at[k, 1]), target(first, left))
        share(i, second, steps[k], 0)

    def begin():
        for other_z in range(4):
            for c in range(2):
                arrived(
                    kv.at[core, here, other_z // 2, pl.ds(c * 128 + (other_z % 2) * 64, 64)],
                    kv_recv.at[other_z, c],
                )
        own = block(first, second)
        relay(own, (first_send.at[0], first_recv.at[0]), target(up, second))
        relay(own, (first_send.at[1], first_recv.at[1]), target(down, second))
        spread(0)

    def first_hop(k):
        if k < 3:
            h, to = k - 1, (up, down)[k - 1]
            arrived(block(firsts[k], second), first_recv.at[h])
            relay(half(firsts[k], second, h), (first_send.at[2 + h], first_recv.at[2 + h]), target(to, second))
        else:
            for h in range(2):
                arrived(half(firsts[k], second, h), first_recv.at[2 + h])
        spread(k)

    second_odd = lax.rem(second, 2)
    onward, behind = wrap(second + 1 - 2 * second_odd), wrap(second - 1 + 2 * second_odd)

    def second_hop(k):
        i = firsts[k]
        arrived(block(i, behind), second_recv.at[k, second_odd])
        relay(block(i, behind), (second_send.at[k, 2], second_recv.at[k, 2]), target(first, onward))
        arrived(block(i, onward), second_recv.at[k, 1 - second_odd])
        share(i, left, steps[k], -1)
        share(i, right, steps[k], 1)

    def last_hop(k):
        i, j = firsts[k], wrap(second + 2)
        arrived(block(i, j), second_recv.at[k, 2])
        share(i, j, steps[k], 2)

    def queries_here():
        for role in range(2):
            for other_z in range(4):
                arrived(
                    landed.at[role, other_z // 2, pl.ds((other_z % 2) * 64, 64)],
                    qo_recv.at[role, other_z],
                )
        for s in range(2):
            for h in range(PER_GROUP):
                lanes, lines = pl.ds(h * 128, 128), pl.ds(h * CHUNK, CHUNK)
                qs[s, lines, :] = landed[0, s, :, lanes]
                os[s, lines, :] = landed[1, s, :, lanes]

    gather_events = {
        0: (begin, queries_here),
        1: (lambda: first_hop(1), lambda: first_hop(2), lambda: second_hop(0)),
        3: (lambda: first_hop(3),),
        5: (lambda: second_hop(1),),
        6: (lambda: second_hop(2),),
        7: (lambda: last_hop(0),),
        8: (lambda: second_hop(3),),
        10: (lambda: last_hop(1),),
        11: (lambda: last_hop(2),),
        12: (lambda: last_hop(3),),
    }

    def run(events, n):
        for at, actions in events.items():

            @pl.when(n == at)
            def _():
                for action in actions:
                    action()

    def block_of(code_x, code_y):
        return lax.rem(x + lax.rem(code_x, 4), 4) * 4 + lax.rem(y + lax.rem(code_y, 4), 4)

    def over_blocks(order, step):
        (start_x, more_x), (start_y, more_y) = codes(order, 0), codes(order, 1)

        def turn(n, carried):
            code_x, code_y = carried
            step(n, block_of(code_x, code_y))
            middle = lax.div(n + 1, 8) - lax.div(n + 1, 9)
            return lax.div(code_x, 4) + middle * more_x, lax.div(code_y, 4) + middle * more_y

        lax.fori_loop(0, 16, turn, (start_x + 0 * x, start_y + 0 * x))

    def in_full(b, work):
        kind = at_most(b, my_block) + 2 * at_most(b, 15 - my_block)
        for number in range(4):

            @pl.when(kind == number)
            def _():
                work(number % 2, number // 2)

    def tiles_of(s, with_late):
        return (0, 1) if s and with_late else (0,)

    def number_of(b, s, late):
        return (32 - b) if late else b + 16 * (1 - s)

    scale = FACTOR * math.log2(math.e)
    top[...] = jnp.full(top.shape, HIDDEN, F32)
    total[...] = jnp.zeros_like(total)
    dot[...] = jnp.zeros_like(dot)
    dq_acc[...] = jnp.zeros_like(dq_acc)

    def stats_step(n, b):
        run(gather_events, n)
        arrived(kv.at[1 - core, b], twin_recv.at[n])

        def stats(with_a, with_late):
            key_turns = [
                jnp.concatenate(
                    [
                        jnp.broadcast_to(turn_ref[pl.ds(2 * (late * 16 + b) + i, 1), :], (128, 128)).T
                        for i in range(2)
                    ],
                    axis=0,
                )
                for late in range(1 + with_late)
            ]
            for s in (1, 0) if with_a else (1,):
                chunk = my_part if s == 0 else 63 - my_part
                query_pos = chunk * CHUNK + lax.broadcasted_iota(jnp.int32, (1, CHUNK), 1)
                query_turn = turn_ref[pl.ds(chunk, 1), :]
                old_top = top[s]
                new_top = old_top
                parts = []
                for late in tiles_of(s, with_late):
                    key_turn = key_turns[late]
                    key_pos = (late * 16 + b) * TILE + lax.broadcasted_iota(
                        jnp.int32, (TILE, CHUNK), 0
                    )
                    visible = (key_pos <= query_pos) & (
                        (key_turn == query_turn) | ((key_turn & 1) == 0)
                    )
                    logits = lax.dot_general(
                        kv[0, b, late], qs[s], (((1,), (1,)), ((), ())), preferred_element_type=F32
                    )
                    bias = jnp.where(visible, 0.0, HIDDEN)
                    logits = logits * scale + jnp.concatenate([bias] * PER_GROUP, axis=1)
                    new_top = jnp.maximum(new_top, jnp.max(logits, axis=0, keepdims=True))
                    grads = lax.dot_general(
                        kv[1, b, late], os[s], (((1,), (1,)), ((), ())), preferred_element_type=F32
                    )
                    parts.append((late, logits, grads))
                shrink = jnp.exp2(old_top - new_top)
                new_total, new_dot = total[s] * shrink, dot[s] * shrink
                for late, logits, grads in parts:
                    number = number_of(b, s, late)
                    weight = jnp.exp2(logits - new_top)
                    weights[number] = weight.astype(BF16)
                    probs_grad[number] = grads.astype(BF16)
                    tile_max[number] = new_top
                    new_total += jnp.sum(weight, axis=0, keepdims=True)
                    new_dot += jnp.sum(weight * grads, axis=0, keepdims=True)
                top[s] = new_top
                total[s] = new_total
                dot[s] = new_dot

        in_full(b, stats)

    over_blocks(NEAR_FIRST, stats_step)
    for s in range(2):
        inverse = 1.0 / total[s]
        total[s] = inverse
        dot[s] = dot[s] * inverse

    across = (wrap(second + 2), right, left, second)
    jumps = (2, 1, -1, 0)

    def chip_sum(a, b):
        i, j = firsts[a], across[b]
        at = index(i, j)
        arrived(twin.at[at], back_recv.at[slot_of(far, steps[a], jumps[b])])
        return partial[core, at].astype(F32) + twin[at].astype(F32)

    def ring_one(a):
        sums[a, 0] = chip_sum(a, 0).astype(BF16)
        for h, to in ((0, right), (1, left)):
            go(sums.at[a, 0, h], one.at[a, h], ring_send.at[a, h], ring_recv.at[a, h], target(first, to))

    def ring_two(a):
        for b, to in ((1, right), (2, left)):
            h = b - 1
            value = chip_sum(a, b)
            arrived(one.at[a, h], ring_recv.at[a, h])
            sums[a, b, 1 - h] = value[1 - h].astype(BF16)
            sums[a, b, h] = (value[h] + one[a, h].astype(F32)).astype(BF16)
            go(sums.at[a, b], two.at[a, h], ring_send.at[a, 2 + h], ring_recv.at[a, 2 + h], target(first, to))

    def home(a):
        value = chip_sum(a, 3)
        arrived(two.at[a, 0], ring_recv.at[a, 2])
        arrived(two.at[a, 1], ring_recv.at[a, 3])
        value = value + two[a, 0].astype(F32) + two[a, 1].astype(F32)
        if a == 3:
            line[a] = value.astype(BF16)
            for h, to in ((0, up), (1, down)):
                go(line.at[a, h], line_in.at[h], line_send.at[h], line_recv.at[h], target(to, second))
            return
        if a:
            h = 2 - a
            arrived(line_in.at[h], line_recv.at[h])
            line[a, 1 - h] = value[1 - h].astype(BF16)
            line[a, h] = (value[h] + line_in[h].astype(F32)).astype(BF16)
        else:
            line[a] = value.astype(BF16)
        i = firsts[a]
        bx, by = i + core * (second - i), second + core * (i - second)
        for other_z in range(4):
            for c in range(2):
                src = line.at[a, other_z // 2, pl.ds(c * 128 + (other_z % 2) * 64, 64)]
                dst = last.at[core, a, :, pl.ds(pl.multiple_of(z * 128, 128), 128)]
                args = (src, dst, last_send.at[a, other_z, c], last_recv.at[core, a, z])
                to = device(bx, by, other_z, c)
                if a:
                    go(*args, to)
                else:
                    go_or_keep((z == other_z) & (core == c), *args, to)

    reduce_events = {
        1: (lambda: ring_one(3),),
        4: (lambda: ring_one(2),),
        5: (lambda: ring_one(1),),
        6: (lambda: ring_two(3),),
        7: (lambda: ring_one(0),),
        10: (lambda: ring_two(2),),
        11: (lambda: ring_two(1),),
        12: (lambda: home(3),),
        15: (lambda: ring_two(0),),
    }

    def backward_step(n, b):
        def terms(with_a, with_late):
            keys_sum, values_sum = [0.0, 0.0], [0.0, 0.0]
            for s in (1, 0) if with_a else (1,):
                query_sum = dq_acc[s]
                for late in tiles_of(s, with_late):
                    number = number_of(b, s, late)
                    by = jnp.exp2(tile_max[number] - top[s]) * total[s]
                    attention = weights[number].astype(F32) * by
                    logit_grad = (attention * (probs_grad[number].astype(F32) - dot[s])).astype(BF16)
                    values_sum[late] += jnp.dot(
                        attention.astype(BF16), os[s], preferred_element_type=F32
                    )
                    keys_sum[late] += jnp.dot(logit_grad, qs[s], preferred_element_type=F32)
                    query_sum += lax.dot_general(
                        logit_grad, kv[0, b, late], (((0,), (0,)), ((), ())),
                        preferred_element_type=F32,
                    )
                dq_acc[s] = query_sum
            for late in range(2):
                if late <= with_late:
                    partial[0, b, late] = (keys_sum[late] * FACTOR).astype(BF16)
                    partial[1, b, late] = values_sum[late].astype(BF16)
                else:
                    partial[0, b, late] = jnp.zeros((TILE, HEAD_SIZE), BF16)
                    partial[1, b, late] = jnp.zeros((TILE, HEAD_SIZE), BF16)

        in_full(b, terms)
        send(partial.at[1 - core, b], twin.at[b], back_send.at[n], back_recv.at[n], other_core).start()
        run(reduce_events, n)

    over_blocks(FAR_FIRST, backward_step)

    for s in range(2):
        for h in range(PER_GROUP):
            dq_own[s, :, pl.ds(h * 128, 128)] = (
                dq_acc[s, pl.ds(h * CHUNK, CHUNK), :] * FACTOR
            ).astype(BF16)
    for other_z in range(4):
        s = other_z // 2
        flip = lax.rem(s + odd, 2)
        to = device(x + flip * (3 - 2 * x), y + flip * (3 - 2 * y), other_z, core + flip * (1 - 2 * core))
        go_or_keep(
            (flip == 0) & (z == other_z),
            dq_own.at[s, pl.ds((other_z % 2) * 64, 64)],
            dq_out.at[:, pl.ds(pl.multiple_of(z * 512, 512), 512)],
            dq_send.at[other_z], dq_recv.at[z], to,
        )
    home(2)
    home(1)
    home(0)

    for role in range(2):
        for a in range(3):
            for other_z in range(4):
                arrived(last.at[role, a, :, pl.ds(other_z * 128, 128)], last_recv.at[role, a, other_z])
    for other_z in range(4):
        arrived(dq_out.at[:, pl.ds(other_z * 512, 512)], dq_recv.at[other_z])

    whole, halved, piece = kv.at[0, 0], kv.at[0, 0, 0], line.at[0, 0, pl.ds(0, 64)]
    for r in range(1, 4):
        for role in range(2):
            arrived(k_ref.at[:, pl.ds(0, 128)], kv_send.at[role, r])
            arrived(q_ref.at[:, pl.ds(0, 512)], qo_send.at[role, r])
    for r in range(1, 3):
        for other_z in range(4):
            for c in range(2):
                arrived(piece, last_send.at[r, other_z, c])
    for h in range(2):
        arrived(whole, first_send.at[h])
        arrived(halved, first_send.at[2 + h])
        arrived(halved, line_send.at[h])
    for k in range(4):
        for h in range(2):
            arrived(whole, second_send.at[k, h])
            arrived(halved, ring_send.at[k, h])
            arrived(whole, ring_send.at[k, 2 + h])
        arrived(whole, second_send.at[k, 2])
    for n in range(16):
        arrived(whole, twin_send.at[n])
        arrived(whole, back_send.at[n])

    @pl.when(core == 0)
    def _():
        arrived(v_ref.at[:, pl.ds(0, 128)], kv_send.at[1, 0])

    @pl.when(core == 1)
    def _():
        arrived(k_ref.at[:, pl.ds(0, 128)], kv_send.at[0, 0])

    @pl.when(lax.rem(z_hi + z_lo, 2) == 1)
    def _():
        for role in range(2):
            arrived(q_ref.at[:, pl.ds(0, 512)], qo_send.at[role, 0])

    for other_z in range(4):
        for c in range(2):

            @pl.when(jnp.logical_not((z == other_z) & (core == c)))
            def _():
                arrived(piece, last_send.at[0, other_z, c])

        flip = lax.rem(other_z // 2 + odd, 2)

        @pl.when(jnp.logical_not((flip == 0) & (z == other_z)))
        def _():
            arrived(dq_own.at[0, pl.ds(0, 64)], dq_send.at[other_z])


def finish_kernel(dq_ref, dkv_ref, dq_out, dk_out, dv_out):
    dq_out[...] = dq_ref[...]
    for role, out in ((0, dk_out), (1, dv_out)):
        value = dkv_ref[role, 0].astype(F32)
        for a in range(1, 3):
            value = value + dkv_ref[role, a].astype(F32)
        out[...] = value.astype(BF16)


ANY = pl.BlockSpec(memory_space=pl.ANY)
VMEM = pl.BlockSpec(memory_space=pltpu.VMEM)
DMA = pltpu.SemaphoreType.DMA


def body(queries, keys, values, grad_out, turn_ids):
    block = (2, TILE, HEAD_SIZE)
    dq, dkv = pl.pallas_call(
        kernel,
        out_shape=(
            jax.ShapeDtypeStruct((64, 2048), BF16),
            jax.ShapeDtypeStruct((2, 3, 64, 512), BF16),
        ),
        in_specs=[VMEM] + [ANY] * 4,
        out_specs=(ANY, ANY),
        scratch_shapes=[
            pltpu.VMEM((2, 16) + block, BF16),
            pltpu.VMEM((2, 2, CHUNK, 512), BF16),
            pltpu.VMEM((2, ROWS, HEAD_SIZE), BF16),
            pltpu.VMEM((2, ROWS, HEAD_SIZE), BF16),
            pltpu.VMEM((ITEMS, TILE, ROWS), BF16),
            pltpu.VMEM((ITEMS, TILE, ROWS), BF16),
            pltpu.VMEM((ITEMS, 1, ROWS), F32),
            pltpu.VMEM((2, 1, ROWS), F32),
            pltpu.VMEM((2, 1, ROWS), F32),
            pltpu.VMEM((2, 1, ROWS), F32),
            pltpu.VMEM((2, ROWS, HEAD_SIZE), F32),
            pltpu.VMEM((2, CHUNK, 512), BF16),
            pltpu.VMEM((2, 16) + block, BF16),
            pltpu.VMEM((16,) + block, BF16),
            pltpu.VMEM((4, 3) + block, BF16),
            pltpu.VMEM((4, 2, TILE, HEAD_SIZE), BF16),
            pltpu.VMEM((4, 2) + block, BF16),
            pltpu.VMEM((4,) + block, BF16),
            pltpu.VMEM(block, BF16),
            DMA((2, 4)), DMA((4, 2)),
            DMA((2, 4)), DMA((2, 4)),
            DMA((4,)), DMA((4,)),
            DMA((4, 3)), DMA((4, 3)),
            DMA((16,)), DMA((16,)),
            DMA((16,)), DMA((16,)),
            DMA((4, 4)), DMA((4, 4)),
            DMA((3, 4, 2)), DMA((2, 3, 4)),
            DMA((2,)), DMA((2,)),
            DMA((4,)), DMA((4,)),
        ],
        compiler_params=pltpu.CompilerParams(
            collective_id=0, has_side_effects=True, vmem_limit_bytes=58 << 20
        ),
        name="attention_backward",
    )(turn_ids.reshape(64, CHUNK), queries, keys, values, grad_out)
    return pl.pallas_call(
        finish_kernel,
        out_shape=(
            jax.ShapeDtypeStruct((64, 2048), BF16),
            jax.ShapeDtypeStruct((64, 512), BF16),
            jax.ShapeDtypeStruct((64, 512), BF16),
        ),
        in_specs=[VMEM] * 2,
        out_specs=(VMEM,) * 3,
        compiler_params=pltpu.CompilerParams(vmem_limit_bytes=60 << 20),
        name="finish",
    )(dq, dkv)


def solution(mesh):
    spread = P(("blk", "head"), None)
    return jax.shard_map(
        body,
        mesh=mesh,
        in_specs=(spread,) * 4 + (P(),),
        out_specs=(spread,) * 3,
        check_vma=False,
    )
```

```python
import math

import jax
import jax.numpy as jnp
from jax import lax
from jax.experimental import pallas as pl
from jax.experimental.pallas import tpu as pltpu
from jax.sharding import PartitionSpec as P

HEAD_SIZE = 128
CHUNK = 128
TILE = 256
PER_GROUP = 4
ROWS = PER_GROUP * CHUNK
ITEMS = 48
HIDDEN = -1e30
FACTOR = HEAD_SIZE**-0.5
BF16 = jnp.bfloat16
F32 = jnp.float32
MESH = pl.DeviceIdType.MESH

NEAR_FIRST = (
    (0, 0), (-1, 0), (1, 0), (0, -1), (0, 1), (-1, -1), (-1, 1), (1, -1), (1, 1),
    (2, 0), (0, 2), (2, -1), (2, 1), (-1, 2), (1, 2), (2, 2),
)
FAR_FIRST = (
    (2, 2), (1, 2), (-1, 2), (2, 1), (2, -1), (0, 2), (2, 0), (1, 1), (1, -1), (-1, 1), (-1, -1),
    (0, 1), (0, -1), (1, 0), (-1, 0), (0, 0),
)


def device(x, y, z, core):
    return (lax.div(z, 2) * 32 + x * 8 + y * 2 + core, lax.rem(z, 2))


def wrap(a):
    return lax.rem(a + 4, 4)


def send(src, dst, send_sem, recv_sem, target):
    return pltpu.make_async_remote_copy(
        src_ref=src,
        dst_ref=dst,
        send_sem=send_sem,
        recv_sem=recv_sem,
        device_id=target,
        device_id_type=MESH,
    )


def arrived(ref, sem):
    pltpu.make_async_copy(ref, ref, sem).wait()


def greet(x, y, z, core):
    others = []
    for r in range(4):
        other_z = lax.rem(z + r, 4)
        if r:
            others.append(device(x, y, other_z, core))
        others.append(device(x, y, other_z, 1 - core))
    for step in (-1, 1):
        others.append(device(wrap(x + step), y, z, core))
        others.append(device(x, wrap(y + step), z, core))
    barrier = pltpu.get_barrier_semaphore()
    for other in others:
        pl.semaphore_signal(barrier, inc=1, device_id=other, device_id_type=MESH)
    pl.semaphore_wait(barrier, len(others))


def codes(order, axis):
    digits = [step[axis] % 4 for step in order]
    return [sum(digit * 4**i for i, digit in enumerate(digits[at : at + 8])) for at in (0, 8)]


def at_most(a, b):
    return lax.div(b - a + 16, 16)


def kernel(
    turn_ref, q_ref, k_ref, v_ref, o_ref, dq_out, last,
    kv, landed, qs, os, weights, probs_grad, tile_max, top, total, dot, dq_acc, dq_own,
    partial, twin, sums, one, two, line, line_in,
    kv_send, kv_recv, qo_send, qo_recv, first_send, first_recv, second_send, second_recv,
    twin_send, twin_recv, back_send, back_recv, ring_send, ring_recv, last_send, last_recv,
    line_send, line_recv,     dq_send, dq_recv,
):
    blk = lax.axis_index("blk")
    z_lo = lax.axis_index("head")
    z_hi = lax.div(blk, 32)
    part = lax.rem(blk, 32)
    x = lax.div(part, 8)
    y = lax.rem(lax.div(part, 2), 4)
    core = lax.rem(part, 2)
    z = z_hi * 2 + z_lo
    here = x * 4 + y
    first, second = x + core * (y - x), y + core * (x - y)

    def index(i, j):
        return (i + core * (j - i)) * 4 + j + core * (i - j)

    def target(i, j):
        return device(i + core * (j - i), j + core * (i - j), z, core)

    other_core = device(x, y, z, 1 - core)
    my_block = lax.div(part, 2)

    greet(x, y, z, core)

    def go(src, dst, send_sem, recv_sem, to):
        send(src, dst, send_sem, recv_sem, to).start()

    def go_or_keep(own, src, dst, send_sem, recv_sem, to):
        @pl.when(own)
        def _():
            pltpu.make_async_copy(src, dst, recv_sem).start()

        @pl.when(jnp.logical_not(own))
        def _():
            send(src, dst, send_sem, recv_sem, to).start()

    rows = pl.ds(pl.multiple_of(core * 128 + z_lo * 64, 64), 64)
    for r in (2, 1, 3, 0):
        other_z = lax.rem(z + r, 4)
        columns = pl.ds(pl.multiple_of(other_z * 128, 128), 128)
        for role, ref in ((0, k_ref), (1, v_ref)):
            dst = kv.at[role, here, z_hi, rows]
            args = (ref.at[:, columns], dst, kv_send.at[role, r], kv_recv.at[z, core])
            if r:
                go(*args, device(x, y, other_z, role))
            else:
                go_or_keep(core == role, *args, device(x, y, z, role))

    own_rows = pl.ds(pl.multiple_of(z_lo * 64, 64), 64)
    for r in (2, 1, 3, 0):
        other_z = lax.rem(z + r, 4)
        to = device(x, y, other_z, core)
        columns = pl.ds(pl.multiple_of(other_z * 512, 512), 512)
        for role, ref in ((0, q_ref), (1, o_ref)):
            args = (ref.at[:, columns], landed.at[role, z_hi, own_rows], qo_send.at[role, r], qo_recv.at[role, z])
            if r:
                go(*args, to)
            else:
                pltpu.make_async_copy(args[0], args[1], args[3]).start()

    up, down = wrap(first + 1), wrap(first - 1)
    left, right = wrap(second - 1), wrap(second + 1)
    firsts = (first, down, up, wrap(first + 2))
    steps = (0, -1, 1, 2)
    near = {step: n for n, step in enumerate(NEAR_FIRST)}
    far = {step: n for n, step in enumerate(FAR_FIRST)}

    def slot_of(table, a, b):
        return table[a, b] + core * (table[b, a] - table[a, b])

    def block(i, j):
        return kv.at[core, index(i, j)]

    def half(i, j, h):
        return kv.at[core, index(i, j), h]

    def share(i, j, a, b):
        slot = slot_of(near, a, b)
        go(block(i, j), block(i, j), twin_send.at[slot], twin_recv.at[slot], other_core)

    def relay(src, sems, to):
        go(src, src, *sems, to)

    def spread(k):
        i = firsts[k]
        own = block(i, second)
        relay(own, (second_send.at[k, 0], second_recv.at[k, 0]), target(first, right))
        relay(own, (second_send.at[k, 1], second_recv.at[k, 1]), target(first, left))
        share(i, second, steps[k], 0)

    def begin():
        for other_z in range(4):
            for c in range(2):
                arrived(
                    kv.at[core, here, other_z // 2, pl.ds(c * 128 + (other_z % 2) * 64, 64)],
                    kv_recv.at[other_z, c],
                )
        own = block(first, second)
        relay(own, (first_send.at[0], first_recv.at[0]), target(up, second))
        relay(own, (first_send.at[1], first_recv.at[1]), target(down, second))
        spread(0)

    def first_hop(k):
        if k < 3:
            h, to = k - 1, (up, down)[k - 1]
            arrived(block(firsts[k], second), first_recv.at[h])
            relay(half(firsts[k], second, h), (first_send.at[2 + h], first_recv.at[2 + h]), target(to, second))
        else:
            for h in range(2):
                arrived(half(firsts[k], second, h), first_recv.at[2 + h])
        spread(k)

    def second_hop(k):
        i = firsts[k]
        arrived(block(i, left), second_recv.at[k, 0])
        relay(half(i, left, 0), (second_send.at[k, 2], second_recv.at[k, 2]), target(first, right))
        share(i, left, steps[k], -1)
        arrived(block(i, right), second_recv.at[k, 1])
        relay(half(i, right, 1), (second_send.at[k, 3], second_recv.at[k, 3]), target(first, left))
        share(i, right, steps[k], 1)

    def last_hop(k):
        i, j = firsts[k], wrap(second + 2)
        arrived(half(i, j, 0), second_recv.at[k, 2])
        arrived(half(i, j, 1), second_recv.at[k, 3])
        share(i, j, steps[k], 2)

    def queries_here():
        for role in range(2):
            for other_z in range(4):
                arrived(
                    landed.at[role, other_z // 2, pl.ds((other_z % 2) * 64, 64)],
                    qo_recv.at[role, other_z],
                )
        for s in range(2):
            for h in range(PER_GROUP):
                lanes, lines = pl.ds(h * 128, 128), pl.ds(h * CHUNK, CHUNK)
                qs[s, lines, :] = landed[0, s, :, lanes]
                os[s, lines, :] = landed[1, s, :, lanes]

    gather_events = {
        0: (begin, lambda: first_hop(1), lambda: first_hop(2), queries_here),
        1: (lambda: second_hop(0), lambda: first_hop(3)),
        3: (lambda: second_hop(1),),
        4: (lambda: second_hop(2),),
        6: (lambda: last_hop(0),),
        7: (lambda: second_hop(3),),
        9: (lambda: last_hop(1),),
        10: (lambda: last_hop(2),),
        11: (lambda: last_hop(3),),
    }

    def run(events, n):
        for at, actions in events.items():

            @pl.when(n == at)
            def _():
                for action in actions:
                    action()

    def block_of(code_x, code_y):
        return lax.rem(x + lax.rem(code_x, 4), 4) * 4 + lax.rem(y + lax.rem(code_y, 4), 4)

    def over_blocks(order, step):
        (start_x, more_x), (start_y, more_y) = codes(order, 0), codes(order, 1)

        def turn(n, carried):
            code_x, code_y = carried
            step(n, block_of(code_x, code_y))
            middle = lax.div(n + 1, 8) - lax.div(n + 1, 9)
            return lax.div(code_x, 4) + middle * more_x, lax.div(code_y, 4) + middle * more_y

        lax.fori_loop(0, 16, turn, (start_x + 0 * x, start_y + 0 * x))

    def in_full(b, work):
        kind = 3 * at_most(b, my_block)
        for number in (0, 3):

            @pl.when(kind == number)
            def _():
                work(number % 2, number // 2)

    def tiles_of(s, with_late):
        return (0, 1) if s and with_late else (0,)

    def number_of(b, s, late):
        return (32 + b) if late else b + 16 * (1 - s)

    scale = FACTOR * math.log2(math.e)
    top[...] = jnp.full(top.shape, HIDDEN, F32)
    total[...] = jnp.zeros_like(total)
    dot[...] = jnp.zeros_like(dot)
    dq_acc[...] = jnp.zeros_like(dq_acc)

    def stats_step(n, b):
        run(gather_events, n)
        arrived(kv.at[1 - core, b], twin_recv.at[n])

        def stats(with_a, with_late):
            key_turns = [
                jnp.concatenate(
                    [
                        jnp.broadcast_to(turn_ref[pl.ds(2 * (late * 16 + b) + i, 1), :], (128, 128)).T
                        for i in range(2)
                    ],
                    axis=0,
                )
                for late in range(1 + with_late)
            ]
            for s in (1, 0) if with_a else (1,):
                chunk = part + 32 * s
                query_pos = chunk * CHUNK + lax.broadcasted_iota(jnp.int32, (1, CHUNK), 1)
                query_turn = turn_ref[pl.ds(chunk, 1), :]
                old_top = top[s]
                new_top = old_top
                parts = []
                for late in tiles_of(s, with_late):
                    key_turn = key_turns[late]
                    key_pos = (late * 16 + b) * TILE + lax.broadcasted_iota(
                        jnp.int32, (TILE, CHUNK), 0
                    )
                    visible = (key_pos <= query_pos) & (
                        (key_turn == query_turn) | ((key_turn & 1) == 0)
                    )
                    logits = lax.dot_general(
                        kv[0, b, late], qs[s], (((1,), (1,)), ((), ())), preferred_element_type=F32
                    )
                    bias = jnp.where(visible, 0.0, HIDDEN)
                    logits = logits * scale + jnp.concatenate([bias] * PER_GROUP, axis=1)
                    new_top = jnp.maximum(new_top, jnp.max(logits, axis=0, keepdims=True))
                    grads = lax.dot_general(
                        kv[1, b, late], os[s], (((1,), (1,)), ((), ())), preferred_element_type=F32
                    )
                    parts.append((late, logits, grads))
                shrink = jnp.exp2(old_top - new_top)
                new_total, new_dot = total[s] * shrink, dot[s] * shrink
                for late, logits, grads in parts:
                    number = number_of(b, s, late)
                    weight = jnp.exp2(logits - new_top)
                    weights[number] = weight.astype(BF16)
                    probs_grad[number] = grads.astype(BF16)
                    tile_max[number] = new_top
                    new_total += jnp.sum(weight, axis=0, keepdims=True)
                    new_dot += jnp.sum(weight * grads, axis=0, keepdims=True)
                top[s] = new_top
                total[s] = new_total
                dot[s] = new_dot

        in_full(b, stats)

    over_blocks(NEAR_FIRST, stats_step)
    for s in range(2):
        inverse = 1.0 / total[s]
        total[s] = inverse
        dot[s] = dot[s] * inverse

    across = (wrap(second + 2), right, left, second)
    jumps = (2, 1, -1, 0)

    def chip_sum(a, b):
        i, j = firsts[a], across[b]
        at = index(i, j)
        arrived(twin.at[at], back_recv.at[slot_of(far, steps[a], jumps[b])])
        return partial[core, at].astype(F32) + twin[at].astype(F32)

    def ring_one(a):
        sums[a, 0] = chip_sum(a, 0).astype(BF16)
        for h, to in ((0, right), (1, left)):
            go(sums.at[a, 0, h], one.at[a, h], ring_send.at[a, h], ring_recv.at[a, h], target(first, to))

    def ring_two(a):
        for b, to in ((1, right), (2, left)):
            h = b - 1
            value = chip_sum(a, b)
            arrived(one.at[a, h], ring_recv.at[a, h])
            sums[a, b, 1 - h] = value[1 - h].astype(BF16)
            sums[a, b, h] = (value[h] + one[a, h].astype(F32)).astype(BF16)
            go(sums.at[a, b], two.at[a, h], ring_send.at[a, 2 + h], ring_recv.at[a, 2 + h], target(first, to))

    def home(a):
        value = chip_sum(a, 3)
        arrived(two.at[a, 0], ring_recv.at[a, 2])
        arrived(two.at[a, 1], ring_recv.at[a, 3])
        value = value + two[a, 0].astype(F32) + two[a, 1].astype(F32)
        if a == 3:
            line[a] = value.astype(BF16)
            for h, to in ((0, up), (1, down)):
                go(line.at[a, h], line_in.at[h], line_send.at[h], line_recv.at[h], target(to, second))
            return
        if a:
            h = 2 - a
            arrived(line_in.at[h], line_recv.at[h])
            line[a, 1 - h] = value[1 - h].astype(BF16)
            line[a, h] = (value[h] + line_in[h].astype(F32)).astype(BF16)
        else:
            line[a] = value.astype(BF16)
        i = firsts[a]
        bx, by = i + core * (second - i), second + core * (i - second)
        for other_z in range(4):
            for c in range(2):
                src = line.at[a, other_z // 2, pl.ds(c * 128 + (other_z % 2) * 64, 64)]
                dst = last.at[core, a, :, pl.ds(pl.multiple_of(z * 128, 128), 128)]
                args = (src, dst, last_send.at[a, other_z, c], last_recv.at[core, a, z])
                to = device(bx, by, other_z, c)
                if a:
                    go(*args, to)
                else:
                    go_or_keep((z == other_z) & (core == c), *args, to)

    reduce_events = {
        1: (lambda: ring_one(3),),
        4: (lambda: ring_one(2),),
        5: (lambda: ring_one(1),),
        6: (lambda: ring_two(3),),
        7: (lambda: ring_one(0),),
        10: (lambda: ring_two(2),),
        11: (lambda: ring_two(1),),
        12: (lambda: home(3),),
        15: (lambda: ring_two(0),),
    }

    def backward_step(n, b):
        def terms(with_a, with_late):
            keys_sum, values_sum = [0.0, 0.0], [0.0, 0.0]
            for s in (1, 0) if with_a else (1,):
                query_sum = dq_acc[s]
                for late in tiles_of(s, with_late):
                    number = number_of(b, s, late)
                    by = jnp.exp2(tile_max[number] - top[s]) * total[s]
                    attention = weights[number].astype(F32) * by
                    logit_grad = (attention * (probs_grad[number].astype(F32) - dot[s])).astype(BF16)
                    values_sum[late] += jnp.dot(
                        attention.astype(BF16), os[s], preferred_element_type=F32
                    )
                    keys_sum[late] += jnp.dot(logit_grad, qs[s], preferred_element_type=F32)
                    query_sum += lax.dot_general(
                        logit_grad, kv[0, b, late], (((0,), (0,)), ((), ())),
                        preferred_element_type=F32,
                    )
                dq_acc[s] = query_sum
            for late in range(2):
                if late <= with_late:
                    partial[0, b, late] = (keys_sum[late] * FACTOR).astype(BF16)
                    partial[1, b, late] = values_sum[late].astype(BF16)
                else:
                    partial[0, b, late] = jnp.zeros((TILE, HEAD_SIZE), BF16)
                    partial[1, b, late] = jnp.zeros((TILE, HEAD_SIZE), BF16)

        in_full(b, terms)
        send(partial.at[1 - core, b], twin.at[b], back_send.at[n], back_recv.at[n], other_core).start()
        run(reduce_events, n)

    over_blocks(FAR_FIRST, backward_step)

    for s in range(2):
        for h in range(PER_GROUP):
            dq_own[s, :, pl.ds(h * 128, 128)] = (
                dq_acc[s, pl.ds(h * CHUNK, CHUNK), :] * FACTOR
            ).astype(BF16)
    for other_z in range(4):
        s = other_z // 2
        to = device(x, y, other_z, core)
        go_or_keep(
            z == other_z,
            dq_own.at[s, pl.ds((other_z % 2) * 64, 64)],
            dq_out.at[:, pl.ds(pl.multiple_of(z * 512, 512), 512)],
            dq_send.at[other_z], dq_recv.at[z], to,
        )
    home(2)
    home(1)
    home(0)

    for role in range(2):
        for a in range(3):
            for other_z in range(4):
                arrived(last.at[role, a, :, pl.ds(other_z * 128, 128)], last_recv.at[role, a, other_z])
    for other_z in range(4):
        arrived(dq_out.at[:, pl.ds(other_z * 512, 512)], dq_recv.at[other_z])

    whole, halved, piece = kv.at[0, 0], kv.at[0, 0, 0], line.at[0, 0, pl.ds(0, 64)]
    for r in range(1, 4):
        for role in range(2):
            arrived(k_ref.at[:, pl.ds(0, 128)], kv_send.at[role, r])
            arrived(q_ref.at[:, pl.ds(0, 512)], qo_send.at[role, r])
    for r in range(1, 3):
        for other_z in range(4):
            for c in range(2):
                arrived(piece, last_send.at[r, other_z, c])
    for h in range(2):
        arrived(whole, first_send.at[h])
        arrived(halved, first_send.at[2 + h])
        arrived(halved, line_send.at[h])
    for k in range(4):
        for h in range(2):
            arrived(whole, second_send.at[k, h])
            arrived(halved, second_send.at[k, 2 + h])
            arrived(halved, ring_send.at[k, h])
            arrived(whole, ring_send.at[k, 2 + h])
    for n in range(16):
        arrived(whole, twin_send.at[n])
        arrived(whole, back_send.at[n])

    @pl.when(core == 0)
    def _():
        arrived(v_ref.at[:, pl.ds(0, 128)], kv_send.at[1, 0])

    @pl.when(core == 1)
    def _():
        arrived(k_ref.at[:, pl.ds(0, 128)], kv_send.at[0, 0])

    for other_z in range(4):
        for c in range(2):

            @pl.when(jnp.logical_not((z == other_z) & (core == c)))
            def _():
                arrived(piece, last_send.at[0, other_z, c])

        @pl.when(z != other_z)
        def _():
            arrived(dq_own.at[0, pl.ds(0, 64)], dq_send.at[other_z])


def finish_kernel(dq_ref, dkv_ref, dq_out, dk_out, dv_out):
    dq_out[...] = dq_ref[...]
    for role, out in ((0, dk_out), (1, dv_out)):
        value = dkv_ref[role, 0].astype(F32)
        for a in range(1, 3):
            value = value + dkv_ref[role, a].astype(F32)
        out[...] = value.astype(BF16)


ANY = pl.BlockSpec(memory_space=pl.ANY)
VMEM = pl.BlockSpec(memory_space=pltpu.VMEM)
DMA = pltpu.SemaphoreType.DMA


def body(queries, keys, values, grad_out, turn_ids):
    block = (2, TILE, HEAD_SIZE)
    dq, dkv = pl.pallas_call(
        kernel,
        out_shape=(
            jax.ShapeDtypeStruct((64, 2048), BF16),
            jax.ShapeDtypeStruct((2, 3, 64, 512), BF16),
        ),
        in_specs=[VMEM] + [ANY] * 4,
        out_specs=(ANY, ANY),
        scratch_shapes=[
            pltpu.VMEM((2, 16) + block, BF16),
            pltpu.VMEM((2, 2, CHUNK, 512), BF16),
            pltpu.VMEM((2, ROWS, HEAD_SIZE), BF16),
            pltpu.VMEM((2, ROWS, HEAD_SIZE), BF16),
            pltpu.VMEM((ITEMS, TILE, ROWS), BF16),
            pltpu.VMEM((ITEMS, TILE, ROWS), BF16),
            pltpu.VMEM((ITEMS, 1, ROWS), F32),
            pltpu.VMEM((2, 1, ROWS), F32),
            pltpu.VMEM((2, 1, ROWS), F32),
            pltpu.VMEM((2, 1, ROWS), F32),
            pltpu.VMEM((2, ROWS, HEAD_SIZE), F32),
            pltpu.VMEM((2, CHUNK, 512), BF16),
            pltpu.VMEM((2, 16) + block, BF16),
            pltpu.VMEM((16,) + block, BF16),
            pltpu.VMEM((4, 3) + block, BF16),
            pltpu.VMEM((4, 2, TILE, HEAD_SIZE), BF16),
            pltpu.VMEM((4, 2) + block, BF16),
            pltpu.VMEM((4,) + block, BF16),
            pltpu.VMEM(block, BF16),
            DMA((2, 4)), DMA((4, 2)),
            DMA((2, 4)), DMA((2, 4)),
            DMA((4,)), DMA((4,)),
            DMA((4, 4)), DMA((4, 4)),
            DMA((16,)), DMA((16,)),
            DMA((16,)), DMA((16,)),
            DMA((4, 4)), DMA((4, 4)),
            DMA((3, 4, 2)), DMA((2, 3, 4)),
            DMA((2,)), DMA((2,)),
            DMA((4,)), DMA((4,)),
        ],
        compiler_params=pltpu.CompilerParams(
            collective_id=0, has_side_effects=True, vmem_limit_bytes=58 << 20
        ),
        name="attention_backward",
    )(turn_ids.reshape(64, CHUNK), queries, keys, values, grad_out)
    return pl.pallas_call(
        finish_kernel,
        out_shape=(
            jax.ShapeDtypeStruct((64, 2048), BF16),
            jax.ShapeDtypeStruct((64, 512), BF16),
            jax.ShapeDtypeStruct((64, 512), BF16),
        ),
        in_specs=[VMEM] * 2,
        out_specs=(VMEM,) * 3,
        compiler_params=pltpu.CompilerParams(vmem_limit_bytes=60 << 20),
        name="finish",
    )(dq, dkv)


def solution(mesh):
    spread = P(("blk", "head"), None)
    return jax.shard_map(
        body,
        mesh=mesh,
        in_specs=(spread,) * 4 + (P(),),
        out_specs=(spread,) * 3,
        check_vma=False,
    )
```

```python
import math

import jax
import jax.numpy as jnp
from jax import lax
from jax.experimental import pallas as pl
from jax.experimental.pallas import tpu as pltpu
from jax.sharding import PartitionSpec as P

HEAD_SIZE = 128
CHUNK = 128
TILE = 256
PER_GROUP = 4
ROWS = PER_GROUP * CHUNK
HIDDEN = -1e30
FACTOR = HEAD_SIZE**-0.5
BF16 = jnp.bfloat16
F32 = jnp.float32
MESH = pl.DeviceIdType.MESH

NEAR_FIRST = (
    (0, 0), (-1, 0), (1, 0), (0, -1), (0, 1), (-1, -1), (-1, 1), (1, -1), (1, 1),
    (2, 0), (0, 2), (2, -1), (2, 1), (-1, 2), (1, 2), (2, 2),
)
FAR_FIRST = (
    (2, 2), (1, 2), (-1, 2), (2, 1), (2, -1), (0, 2), (2, 0), (1, 1), (1, -1), (-1, 1), (-1, -1),
    (0, 1), (0, -1), (1, 0), (-1, 0), (0, 0),
)


def device(x, y, z, core):
    return (lax.div(z, 2) * 32 + x * 8 + y * 2 + core, lax.rem(z, 2))


def wrap(a):
    return lax.rem(a + 4, 4)


def send(src, dst, send_sem, recv_sem, target):
    return pltpu.make_async_remote_copy(
        src_ref=src,
        dst_ref=dst,
        send_sem=send_sem,
        recv_sem=recv_sem,
        device_id=target,
        device_id_type=MESH,
    )


def arrived(ref, sem):
    pltpu.make_async_copy(ref, ref, sem).wait()


def greet(x, y, z, core):
    others = []
    for r in range(4):
        other_z = lax.rem(z + r, 4)
        if r:
            others.append(device(x, y, other_z, core))
        others.append(device(x, y, other_z, 1 - core))
    for step in (-1, 1):
        others.append(device(wrap(x + step), y, z, core))
        others.append(device(x, wrap(y + step), z, core))
    barrier = pltpu.get_barrier_semaphore()
    for other in others:
        pl.semaphore_signal(barrier, inc=1, device_id=other, device_id_type=MESH)
    pl.semaphore_wait(barrier, len(others))


def codes(order, axis):
    digits = [step[axis] % 4 for step in order]
    return [sum(digit * 4**i for i, digit in enumerate(digits[at : at + 8])) for at in (0, 8)]


def at_most(a, b):
    return lax.div(b - a + 16, 16)


def kernel(
    turn_ref, q_ref, k_ref, v_ref, o_ref, dq_out, last,
    kv, landed, qs, os, weights_b, weights_a, grads_b, grads_a, tile_max, top, total, dot, dq_acc, dq_own,
    partial, twin, sums, one, two, line, line_in,
    kv_send, kv_recv, qo_send, qo_recv, first_send, first_recv, second_send, second_recv,
    twin_send, twin_recv, back_send, back_recv, ring_send, ring_recv, last_send, last_recv,
    line_send, line_recv,     dq_send, dq_recv,
):
    blk = lax.axis_index("blk")
    z_lo = lax.axis_index("head")
    z_hi = lax.div(blk, 32)
    part = lax.rem(blk, 32)
    x = lax.div(part, 8)
    y = lax.rem(lax.div(part, 2), 4)
    core = lax.rem(part, 2)
    z = z_hi * 2 + z_lo
    here = x * 4 + y
    first, second = x + core * (y - x), y + core * (x - y)

    def index(i, j):
        return (i + core * (j - i)) * 4 + j + core * (i - j)

    def target(i, j):
        return device(i + core * (j - i), j + core * (i - j), z, core)

    other_core = device(x, y, z, 1 - core)
    my_block = lax.div(part, 2)

    greet(x, y, z, core)

    def go(src, dst, send_sem, recv_sem, to):
        send(src, dst, send_sem, recv_sem, to).start()

    def go_or_keep(own, src, dst, send_sem, recv_sem, to):
        @pl.when(own)
        def _():
            pltpu.make_async_copy(src, dst, recv_sem).start()

        @pl.when(jnp.logical_not(own))
        def _():
            send(src, dst, send_sem, recv_sem, to).start()

    rows = pl.ds(pl.multiple_of(core * 128 + z_lo * 64, 64), 64)
    for r in (2, 1, 3, 0):
        other_z = lax.rem(z + r, 4)
        columns = pl.ds(pl.multiple_of(other_z * 128, 128), 128)
        for role, ref in ((0, k_ref), (1, v_ref)):
            dst = kv.at[role, here, z_hi, rows]
            args = (ref.at[:, columns], dst, kv_send.at[role, r], kv_recv.at[z, core])
            if r:
                go(*args, device(x, y, other_z, role))
            else:
                go_or_keep(core == role, *args, device(x, y, z, role))

    own_rows = pl.ds(pl.multiple_of(z_lo * 64, 64), 64)
    for r in (2, 1, 3, 0):
        other_z = lax.rem(z + r, 4)
        to = device(x, y, other_z, core)
        columns = pl.ds(pl.multiple_of(other_z * 512, 512), 512)
        for role, ref in ((0, q_ref), (1, o_ref)):
            args = (ref.at[:, columns], landed.at[role, z_hi, own_rows], qo_send.at[role, r], qo_recv.at[role, z])
            if r:
                go(*args, to)
            else:
                pltpu.make_async_copy(args[0], args[1], args[3]).start()

    up, down = wrap(first + 1), wrap(first - 1)
    left, right = wrap(second - 1), wrap(second + 1)
    firsts = (first, down, up, wrap(first + 2))
    steps = (0, -1, 1, 2)
    near = {step: n for n, step in enumerate(NEAR_FIRST)}
    far = {step: n for n, step in enumerate(FAR_FIRST)}

    def slot_of(table, a, b):
        return table[a, b] + core * (table[b, a] - table[a, b])

    def block(i, j):
        return kv.at[core, index(i, j)]

    def half(i, j, h):
        return kv.at[core, index(i, j), h]

    def share(i, j, a, b):
        slot = slot_of(near, a, b)
        go(block(i, j), block(i, j), twin_send.at[slot], twin_recv.at[slot], other_core)

    def relay(src, sems, to):
        go(src, src, *sems, to)

    def spread(k):
        i = firsts[k]
        own = block(i, second)
        relay(own, (second_send.at[k, 0], second_recv.at[k, 0]), target(first, right))
        relay(own, (second_send.at[k, 1], second_recv.at[k, 1]), target(first, left))
        share(i, second, steps[k], 0)

    def begin():
        for other_z in range(4):
            for c in range(2):
                arrived(
                    kv.at[core, here, other_z // 2, pl.ds(c * 128 + (other_z % 2) * 64, 64)],
                    kv_recv.at[other_z, c],
                )
        own = block(first, second)
        relay(own, (first_send.at[0], first_recv.at[0]), target(up, second))
        relay(own, (first_send.at[1], first_recv.at[1]), target(down, second))
        spread(0)

    def first_hop(k):
        if k < 3:
            h, to = k - 1, (up, down)[k - 1]
            arrived(block(firsts[k], second), first_recv.at[h])
            relay(half(firsts[k], second, h), (first_send.at[2 + h], first_recv.at[2 + h]), target(to, second))
        else:
            for h in range(2):
                arrived(half(firsts[k], second, h), first_recv.at[2 + h])
        spread(k)

    def second_hop(k):
        i = firsts[k]
        arrived(block(i, left), second_recv.at[k, 0])
        relay(half(i, left, 0), (second_send.at[k, 2], second_recv.at[k, 2]), target(first, right))
        share(i, left, steps[k], -1)
        arrived(block(i, right), second_recv.at[k, 1])
        relay(half(i, right, 1), (second_send.at[k, 3], second_recv.at[k, 3]), target(first, left))
        share(i, right, steps[k], 1)

    def last_hop(k):
        i, j = firsts[k], wrap(second + 2)
        arrived(half(i, j, 0), second_recv.at[k, 2])
        arrived(half(i, j, 1), second_recv.at[k, 3])
        share(i, j, steps[k], 2)

    def queries_here():
        for role in range(2):
            for other_z in range(4):
                arrived(
                    landed.at[role, other_z // 2, pl.ds((other_z % 2) * 64, 64)],
                    qo_recv.at[role, other_z],
                )
        for s in range(2):
            for h in range(PER_GROUP):
                lanes, lines = pl.ds(h * 128, 128), pl.ds(h * CHUNK, CHUNK)
                qs[s, lines, :] = landed[0, s, :, lanes]
                os[s, lines, :] = landed[1, s, :, lanes]

    gather_events = {
        0: (begin, lambda: first_hop(1), lambda: first_hop(2), queries_here),
        1: (lambda: second_hop(0), lambda: first_hop(3)),
        3: (lambda: second_hop(1),),
        4: (lambda: second_hop(2),),
        6: (lambda: last_hop(0),),
        7: (lambda: second_hop(3),),
        9: (lambda: last_hop(1),),
        10: (lambda: last_hop(2),),
        11: (lambda: last_hop(3),),
    }

    def run(events, n):
        for at, actions in events.items():

            @pl.when(n == at)
            def _():
                for action in actions:
                    action()

    def block_of(code_x, code_y):
        return lax.rem(x + lax.rem(code_x, 4), 4) * 4 + lax.rem(y + lax.rem(code_y, 4), 4)

    def over_blocks(order, step):
        (start_x, more_x), (start_y, more_y) = codes(order, 0), codes(order, 1)

        def turn(n, carried):
            code_x, code_y = carried
            step(n, block_of(code_x, code_y))
            middle = lax.div(n + 1, 8) - lax.div(n + 1, 9)
            return lax.div(code_x, 4) + middle * more_x, lax.div(code_y, 4) + middle * more_y

        lax.fori_loop(0, 16, turn, (start_x + 0 * x, start_y + 0 * x))

    def in_full(b, work):
        kind = 3 * at_most(b, my_block)
        for number in (0, 3):

            @pl.when(kind == number)
            def _():
                work(number % 2, number // 2)

    def groups(with_a, with_late):
        return ((1, TILE * (1 + with_late)),) + ((0, TILE),) * with_a

    def held(ref_b, ref_a, b, s, count):
        return ref_b.at[b, pl.ds(0, count)] if s else ref_a.at[b]

    def keys_of(b, role, count):
        return kv[role, b].reshape(2 * TILE, HEAD_SIZE) if count > TILE else kv[role, b, 0]

    scale = FACTOR * math.log2(math.e)
    top[...] = jnp.full(top.shape, HIDDEN, F32)
    total[...] = jnp.zeros_like(total)
    dot[...] = jnp.zeros_like(dot)
    dq_acc[...] = jnp.zeros_like(dq_acc)

    def stats_step(n, b):
        run(gather_events, n)
        arrived(kv.at[1 - core, b], twin_recv.at[n])

        def stats(with_a, with_late):
            count = TILE * (1 + with_late)
            key_turns = jnp.concatenate(
                [
                    jnp.broadcast_to(turn_ref[pl.ds(2 * (late * 16 + b) + i, 1), :], (128, 128)).T
                    for late in range(1 + with_late)
                    for i in range(2)
                ],
                axis=0,
            )
            row = lax.broadcasted_iota(jnp.int32, (count, CHUNK), 0)
            key_places = b * TILE + row + jnp.where(row >= TILE, 15 * TILE, 0)
            parts = []
            for s, count in groups(with_a, with_late):
                query_pos = (part + 32 * s) * CHUNK + lax.broadcasted_iota(jnp.int32, (1, CHUNK), 1)
                query_turn = turn_ref[pl.ds(part + 32 * s, 1), :]
                key_turn, key_pos = key_turns[:count], key_places[:count]
                visible = (key_pos <= query_pos) & (
                    (key_turn == query_turn) | ((key_turn & 1) == 0)
                )
                logits = lax.dot_general(
                    keys_of(b, 0, count), qs[s], (((1,), (1,)), ((), ())), preferred_element_type=F32
                )
                grads = lax.dot_general(
                    keys_of(b, 1, count), os[s], (((1,), (1,)), ((), ())), preferred_element_type=F32
                )
                bias = jnp.where(visible, 0.0, HIDDEN)
                parts.append((s, count, logits * scale + jnp.concatenate([bias] * PER_GROUP, axis=1), grads))
            for s, count, logits, grads in parts:
                old_top = top[s]
                new_top = jnp.maximum(old_top, jnp.max(logits, axis=0, keepdims=True))
                shrink = jnp.exp2(old_top - new_top)
                weight = jnp.exp2(logits - new_top)
                held(weights_b, weights_a, b, s, count)[...] = weight.astype(BF16)
                held(grads_b, grads_a, b, s, count)[...] = grads.astype(BF16)
                tile_max[s, b] = new_top
                top[s] = new_top
                total[s] = total[s] * shrink + jnp.sum(weight, axis=0, keepdims=True)
                dot[s] = dot[s] * shrink + jnp.sum(weight * grads, axis=0, keepdims=True)

        in_full(b, stats)

    over_blocks(NEAR_FIRST, stats_step)
    for s in range(2):
        inverse = 1.0 / total[s]
        total[s] = inverse
        dot[s] = dot[s] * inverse

    across = (wrap(second + 2), right, left, second)
    jumps = (2, 1, -1, 0)

    def chip_sum(a, b):
        i, j = firsts[a], across[b]
        at = index(i, j)
        arrived(twin.at[at], back_recv.at[slot_of(far, steps[a], jumps[b])])
        return partial[core, at].astype(F32) + twin[at].astype(F32)

    def ring_one(a):
        sums[a, 0] = chip_sum(a, 0).astype(BF16)
        for h, to in ((0, right), (1, left)):
            go(sums.at[a, 0, h], one.at[a, h], ring_send.at[a, h], ring_recv.at[a, h], target(first, to))

    def ring_two(a):
        for b, to in ((1, right), (2, left)):
            h = b - 1
            value = chip_sum(a, b)
            arrived(one.at[a, h], ring_recv.at[a, h])
            sums[a, b, 1 - h] = value[1 - h].astype(BF16)
            sums[a, b, h] = (value[h] + one[a, h].astype(F32)).astype(BF16)
            go(sums.at[a, b], two.at[a, h], ring_send.at[a, 2 + h], ring_recv.at[a, 2 + h], target(first, to))

    def home(a):
        value = chip_sum(a, 3)
        arrived(two.at[a, 0], ring_recv.at[a, 2])
        arrived(two.at[a, 1], ring_recv.at[a, 3])
        value = value + two[a, 0].astype(F32) + two[a, 1].astype(F32)
        if a == 3:
            line[a] = value.astype(BF16)
            for h, to in ((0, up), (1, down)):
                go(line.at[a, h], line_in.at[h], line_send.at[h], line_recv.at[h], target(to, second))
            return
        if a:
            h = 2 - a
            arrived(line_in.at[h], line_recv.at[h])
            line[a, 1 - h] = value[1 - h].astype(BF16)
            line[a, h] = (value[h] + line_in[h].astype(F32)).astype(BF16)
        else:
            line[a] = value.astype(BF16)
        i = firsts[a]
        bx, by = i + core * (second - i), second + core * (i - second)
        for other_z in range(4):
            for c in range(2):
                src = line.at[a, other_z // 2, pl.ds(c * 128 + (other_z % 2) * 64, 64)]
                dst = last.at[core, a, :, pl.ds(pl.multiple_of(z * 128, 128), 128)]
                args = (src, dst, last_send.at[a, other_z, c], last_recv.at[core, a, z])
                to = device(bx, by, other_z, c)
                if a:
                    go(*args, to)
                else:
                    go_or_keep((z == other_z) & (core == c), *args, to)

    reduce_events = {
        1: (lambda: ring_one(3),),
        4: (lambda: ring_one(2),),
        5: (lambda: ring_one(1),),
        6: (lambda: ring_two(3),),
        7: (lambda: ring_one(0),),
        10: (lambda: ring_two(2),),
        11: (lambda: ring_two(1),),
        12: (lambda: home(3),),
        15: (lambda: ring_two(0),),
    }

    def backward_step(n, b):
        def terms(with_a, with_late):
            sums_of = []
            for s, count in groups(with_a, with_late):
                by = jnp.exp2(tile_max[s, b] - top[s]) * total[s]
                attention = held(weights_b, weights_a, b, s, count)[...].astype(F32) * by
                grads = held(grads_b, grads_a, b, s, count)[...].astype(F32)
                logit_grad = (attention * (grads - dot[s])).astype(BF16)
                value_sum = jnp.dot(attention.astype(BF16), os[s], preferred_element_type=F32)
                key_sum = jnp.dot(logit_grad, qs[s], preferred_element_type=F32)
                dq_acc[s] += lax.dot_general(
                    logit_grad, keys_of(b, 0, count), (((0,), (0,)), ((), ())),
                    preferred_element_type=F32,
                )
                sums_of.append((key_sum * FACTOR, value_sum))
            for role in range(2):
                early = sums_of[0][role][:TILE]
                if with_a:
                    early = early + sums_of[1][role]
                partial[role, b, 0] = early.astype(BF16)
                if with_late:
                    partial[role, b, 1] = sums_of[0][role][TILE:].astype(BF16)
                else:
                    partial[role, b, 1] = jnp.zeros((TILE, HEAD_SIZE), BF16)

        in_full(b, terms)
        send(partial.at[1 - core, b], twin.at[b], back_send.at[n], back_recv.at[n], other_core).start()
        run(reduce_events, n)

    over_blocks(FAR_FIRST, backward_step)

    for s in range(2):
        for h in range(PER_GROUP):
            dq_own[s, :, pl.ds(h * 128, 128)] = (
                dq_acc[s, pl.ds(h * CHUNK, CHUNK), :] * FACTOR
            ).astype(BF16)
    for other_z in range(4):
        s = other_z // 2
        to = device(x, y, other_z, core)
        go_or_keep(
            z == other_z,
            dq_own.at[s, pl.ds((other_z % 2) * 64, 64)],
            dq_out.at[:, pl.ds(pl.multiple_of(z * 512, 512), 512)],
            dq_send.at[other_z], dq_recv.at[z], to,
        )
    home(2)
    home(1)
    home(0)

    for role in range(2):
        for a in range(3):
            for other_z in range(4):
                arrived(last.at[role, a, :, pl.ds(other_z * 128, 128)], last_recv.at[role, a, other_z])
    for other_z in range(4):
        arrived(dq_out.at[:, pl.ds(other_z * 512, 512)], dq_recv.at[other_z])

    whole, halved, piece = kv.at[0, 0], kv.at[0, 0, 0], line.at[0, 0, pl.ds(0, 64)]
    for r in range(1, 4):
        for role in range(2):
            arrived(k_ref.at[:, pl.ds(0, 128)], kv_send.at[role, r])
            arrived(q_ref.at[:, pl.ds(0, 512)], qo_send.at[role, r])
    for r in range(1, 3):
        for other_z in range(4):
            for c in range(2):
                arrived(piece, last_send.at[r, other_z, c])
    for h in range(2):
        arrived(whole, first_send.at[h])
        arrived(halved, first_send.at[2 + h])
        arrived(halved, line_send.at[h])
    for k in range(4):
        for h in range(2):
            arrived(whole, second_send.at[k, h])
            arrived(halved, second_send.at[k, 2 + h])
            arrived(halved, ring_send.at[k, h])
            arrived(whole, ring_send.at[k, 2 + h])
    for n in range(16):
        arrived(whole, twin_send.at[n])
        arrived(whole, back_send.at[n])

    @pl.when(core == 0)
    def _():
        arrived(v_ref.at[:, pl.ds(0, 128)], kv_send.at[1, 0])

    @pl.when(core == 1)
    def _():
        arrived(k_ref.at[:, pl.ds(0, 128)], kv_send.at[0, 0])

    for other_z in range(4):
        for c in range(2):

            @pl.when(jnp.logical_not((z == other_z) & (core == c)))
            def _():
                arrived(piece, last_send.at[0, other_z, c])

        @pl.when(z != other_z)
        def _():
            arrived(dq_own.at[0, pl.ds(0, 64)], dq_send.at[other_z])


def finish_kernel(dq_ref, dkv_ref, dq_out, dk_out, dv_out):
    dq_out[...] = dq_ref[...]
    for role, out in ((0, dk_out), (1, dv_out)):
        value = dkv_ref[role, 0].astype(F32)
        for a in range(1, 3):
            value = value + dkv_ref[role, a].astype(F32)
        out[...] = value.astype(BF16)


ANY = pl.BlockSpec(memory_space=pl.ANY)
VMEM = pl.BlockSpec(memory_space=pltpu.VMEM)
DMA = pltpu.SemaphoreType.DMA


def body(queries, keys, values, grad_out, turn_ids):
    block = (2, TILE, HEAD_SIZE)
    dq, dkv = pl.pallas_call(
        kernel,
        out_shape=(
            jax.ShapeDtypeStruct((64, 2048), BF16),
            jax.ShapeDtypeStruct((2, 3, 64, 512), BF16),
        ),
        in_specs=[VMEM] + [ANY] * 4,
        out_specs=(ANY, ANY),
        scratch_shapes=[
            pltpu.VMEM((2, 16) + block, BF16),
            pltpu.VMEM((2, 2, CHUNK, 512), BF16),
            pltpu.VMEM((2, ROWS, HEAD_SIZE), BF16),
            pltpu.VMEM((2, ROWS, HEAD_SIZE), BF16),
            pltpu.VMEM((16, 2 * TILE, ROWS), BF16),
            pltpu.VMEM((16, TILE, ROWS), BF16),
            pltpu.VMEM((16, 2 * TILE, ROWS), BF16),
            pltpu.VMEM((16, TILE, ROWS), BF16),
            pltpu.VMEM((2, 16, 1, ROWS), F32),
            pltpu.VMEM((2, 1, ROWS), F32),
            pltpu.VMEM((2, 1, ROWS), F32),
            pltpu.VMEM((2, 1, ROWS), F32),
            pltpu.VMEM((2, ROWS, HEAD_SIZE), F32),
            pltpu.VMEM((2, CHUNK, 512), BF16),
            pltpu.VMEM((2, 16) + block, BF16),
            pltpu.VMEM((16,) + block, BF16),
            pltpu.VMEM((4, 3) + block, BF16),
            pltpu.VMEM((4, 2, TILE, HEAD_SIZE), BF16),
            pltpu.VMEM((4, 2) + block, BF16),
            pltpu.VMEM((4,) + block, BF16),
            pltpu.VMEM(block, BF16),
            DMA((2, 4)), DMA((4, 2)),
            DMA((2, 4)), DMA((2, 4)),
            DMA((4,)), DMA((4,)),
            DMA((4, 4)), DMA((4, 4)),
            DMA((16,)), DMA((16,)),
            DMA((16,)), DMA((16,)),
            DMA((4, 4)), DMA((4, 4)),
            DMA((3, 4, 2)), DMA((2, 3, 4)),
            DMA((2,)), DMA((2,)),
            DMA((4,)), DMA((4,)),
        ],
        compiler_params=pltpu.CompilerParams(
            collective_id=0, has_side_effects=True, vmem_limit_bytes=58 << 20
        ),
        name="attention_backward",
    )(turn_ids.reshape(64, CHUNK), queries, keys, values, grad_out)
    return pl.pallas_call(
        finish_kernel,
        out_shape=(
            jax.ShapeDtypeStruct((64, 2048), BF16),
            jax.ShapeDtypeStruct((64, 512), BF16),
            jax.ShapeDtypeStruct((64, 512), BF16),
        ),
        in_specs=[VMEM] * 2,
        out_specs=(VMEM,) * 3,
        compiler_params=pltpu.CompilerParams(vmem_limit_bytes=60 << 20),
        name="finish",
    )(dq, dkv)


def solution(mesh):
    spread = P(("blk", "head"), None)
    return jax.shard_map(
        body,
        mesh=mesh,
        in_specs=(spread,) * 4 + (P(),),
        out_specs=(spread,) * 3,
        check_vma=False,
    )
```

```python
import math

import jax
import jax.numpy as jnp
from jax import lax
from jax.experimental import pallas as pl
from jax.experimental.pallas import tpu as pltpu
from jax.sharding import PartitionSpec as P

HEAD_SIZE = 128
CHUNK = 128
TILE = 256
PER_GROUP = 4
ROWS = PER_GROUP * CHUNK
HIDDEN = -1e30
FACTOR = HEAD_SIZE**-0.5
BF16 = jnp.bfloat16
F32 = jnp.float32
MESH = pl.DeviceIdType.MESH

NEAR_FIRST = (
    (0, 0), (-1, 0), (1, 0), (0, -1), (0, 1), (-1, -1), (-1, 1), (1, -1), (1, 1),
    (2, 0), (0, 2), (2, -1), (2, 1), (-1, 2), (1, 2), (2, 2),
)
FAR_FIRST = (
    (2, 2), (1, 2), (-1, 2), (2, 1), (2, -1), (0, 2), (2, 0), (1, 1), (1, -1), (-1, 1), (-1, -1),
    (0, 1), (0, -1), (1, 0), (-1, 0), (0, 0),
)


def device(x, y, z, core):
    return (lax.div(z, 2) * 32 + x * 8 + y * 2 + core, lax.rem(z, 2))


def wrap(a):
    return lax.rem(a + 4, 4)


def send(src, dst, send_sem, recv_sem, target):
    return pltpu.make_async_remote_copy(
        src_ref=src,
        dst_ref=dst,
        send_sem=send_sem,
        recv_sem=recv_sem,
        device_id=target,
        device_id_type=MESH,
    )


def arrived(ref, sem):
    pltpu.make_async_copy(ref, ref, sem).wait()


def greet(x, y, z, core):
    others = []
    for r in range(4):
        other_z = lax.rem(z + r, 4)
        if r:
            others.append(device(x, y, other_z, core))
        others.append(device(x, y, other_z, 1 - core))
    for step in (-1, 1):
        others.append(device(wrap(x + step), y, z, core))
        others.append(device(x, wrap(y + step), z, core))
    barrier = pltpu.get_barrier_semaphore()
    for other in others:
        pl.semaphore_signal(barrier, inc=1, device_id=other, device_id_type=MESH)
    pl.semaphore_wait(barrier, len(others))


def codes(order, axis):
    digits = [step[axis] % 4 for step in order]
    return [sum(digit * 4**i for i, digit in enumerate(digits[at : at + 8])) for at in (0, 8)]


def at_most(a, b):
    return lax.div(b - a + 16, 16)


def kernel(
    turns, q_ref, k_ref, v_ref, o_ref, dq_out, last,
    turn_ref, kv, landed, qs, os, weights_b, weights_a, grads_b, grads_a, tile_max, top, total, dot, dq_acc, dq_own,
    partial, twin, sums, one, two, line, line_in,
    kv_send, kv_recv, qo_send, qo_recv, first_send, first_recv, second_send, second_recv,
    twin_send, twin_recv, back_send, back_recv, ring_send, ring_recv, last_send, last_recv,
    line_send, line_recv,     dq_send, dq_recv, turn_sem,
):
    blk = lax.axis_index("blk")
    z_lo = lax.axis_index("head")
    z_hi = lax.div(blk, 32)
    part = lax.rem(blk, 32)
    x = lax.div(part, 8)
    y = lax.rem(lax.div(part, 2), 4)
    core = lax.rem(part, 2)
    z = z_hi * 2 + z_lo
    here = x * 4 + y
    first, second = x + core * (y - x), y + core * (x - y)

    def index(i, j):
        return (i + core * (j - i)) * 4 + j + core * (i - j)

    def target(i, j):
        return device(i + core * (j - i), j + core * (i - j), z, core)

    other_core = device(x, y, z, 1 - core)
    my_block = lax.div(part, 2)

    pltpu.make_async_copy(turns, turn_ref, turn_sem).start()
    greet(x, y, z, core)

    def go(src, dst, send_sem, recv_sem, to):
        send(src, dst, send_sem, recv_sem, to).start()

    def go_or_keep(own, src, dst, send_sem, recv_sem, to):
        @pl.when(own)
        def _():
            pltpu.make_async_copy(src, dst, recv_sem).start()

        @pl.when(jnp.logical_not(own))
        def _():
            send(src, dst, send_sem, recv_sem, to).start()

    rows = pl.ds(pl.multiple_of(core * 128 + z_lo * 64, 64), 64)
    for r in (2, 1, 3, 0):
        other_z = lax.rem(z + r, 4)
        columns = pl.ds(pl.multiple_of(other_z * 128, 128), 128)
        for role, ref in ((0, k_ref), (1, v_ref)):
            dst = kv.at[role, here, z_hi, rows]
            args = (ref.at[:, columns], dst, kv_send.at[role, r], kv_recv.at[z, core])
            if r:
                go(*args, device(x, y, other_z, role))
            else:
                go_or_keep(core == role, *args, device(x, y, z, role))

    own_rows = pl.ds(pl.multiple_of(z_lo * 64, 64), 64)
    for r in (2, 1, 3, 0):
        other_z = lax.rem(z + r, 4)
        to = device(x, y, other_z, core)
        columns = pl.ds(pl.multiple_of(other_z * 512, 512), 512)
        for role, ref in ((0, q_ref), (1, o_ref)):
            args = (ref.at[:, columns], landed.at[role, z_hi, own_rows], qo_send.at[role, r], qo_recv.at[role, z])
            if r:
                go(*args, to)
            else:
                pltpu.make_async_copy(args[0], args[1], args[3]).start()

    up, down = wrap(first + 1), wrap(first - 1)
    left, right = wrap(second - 1), wrap(second + 1)
    firsts = (first, down, up, wrap(first + 2))
    steps = (0, -1, 1, 2)
    near = {step: n for n, step in enumerate(NEAR_FIRST)}
    far = {step: n for n, step in enumerate(FAR_FIRST)}

    def slot_of(table, a, b):
        return table[a, b] + core * (table[b, a] - table[a, b])

    def block(i, j):
        return kv.at[core, index(i, j)]

    def half(i, j, h):
        return kv.at[core, index(i, j), h]

    def share(i, j, a, b):
        slot = slot_of(near, a, b)
        go(block(i, j), block(i, j), twin_send.at[slot], twin_recv.at[slot], other_core)

    def relay(src, sems, to):
        go(src, src, *sems, to)

    def spread(k):
        i = firsts[k]
        own = block(i, second)
        relay(own, (second_send.at[k, 0], second_recv.at[k, 0]), target(first, right))
        relay(own, (second_send.at[k, 1], second_recv.at[k, 1]), target(first, left))
        share(i, second, steps[k], 0)

    def begin():
        for other_z in range(4):
            for c in range(2):
                arrived(
                    kv.at[core, here, other_z // 2, pl.ds(c * 128 + (other_z % 2) * 64, 64)],
                    kv_recv.at[other_z, c],
                )
        own = block(first, second)
        relay(own, (first_send.at[0], first_recv.at[0]), target(up, second))
        relay(own, (first_send.at[1], first_recv.at[1]), target(down, second))
        spread(0)

    def first_hop(k):
        if k < 3:
            h, to = k - 1, (up, down)[k - 1]
            arrived(block(firsts[k], second), first_recv.at[h])
            relay(half(firsts[k], second, h), (first_send.at[2 + h], first_recv.at[2 + h]), target(to, second))
        else:
            for h in range(2):
                arrived(half(firsts[k], second, h), first_recv.at[2 + h])
        spread(k)

    def second_hop(k):
        i = firsts[k]
        arrived(block(i, left), second_recv.at[k, 0])
        relay(half(i, left, 0), (second_send.at[k, 2], second_recv.at[k, 2]), target(first, right))
        share(i, left, steps[k], -1)
        arrived(block(i, right), second_recv.at[k, 1])
        relay(half(i, right, 1), (second_send.at[k, 3], second_recv.at[k, 3]), target(first, left))
        share(i, right, steps[k], 1)

    def last_hop(k):
        i, j = firsts[k], wrap(second + 2)
        arrived(half(i, j, 0), second_recv.at[k, 2])
        arrived(half(i, j, 1), second_recv.at[k, 3])
        share(i, j, steps[k], 2)

    def queries_here():
        arrived(turn_ref, turn_sem)
        for role in range(2):
            for other_z in range(4):
                arrived(
                    landed.at[role, other_z // 2, pl.ds((other_z % 2) * 64, 64)],
                    qo_recv.at[role, other_z],
                )
        for s in range(2):
            for h in range(PER_GROUP):
                lanes, lines = pl.ds(h * 128, 128), pl.ds(h * CHUNK, CHUNK)
                qs[s, lines, :] = landed[0, s, :, lanes]
                os[s, lines, :] = landed[1, s, :, lanes]

    gather_events = {
        0: (begin, lambda: first_hop(1), lambda: first_hop(2), queries_here),
        1: (lambda: second_hop(0), lambda: first_hop(3)),
        3: (lambda: second_hop(1),),
        4: (lambda: second_hop(2),),
        6: (lambda: last_hop(0),),
        7: (lambda: second_hop(3),),
        9: (lambda: last_hop(1),),
        10: (lambda: last_hop(2),),
        11: (lambda: last_hop(3),),
    }

    def run(events, n):
        for at, actions in events.items():

            @pl.when(n == at)
            def _():
                for action in actions:
                    action()

    def block_of(code_x, code_y):
        return lax.rem(x + lax.rem(code_x, 4), 4) * 4 + lax.rem(y + lax.rem(code_y, 4), 4)

    def over_blocks(order, step):
        (start_x, more_x), (start_y, more_y) = codes(order, 0), codes(order, 1)

        def turn(n, carried):
            code_x, code_y = carried
            step(n, block_of(code_x, code_y))
            middle = lax.div(n + 1, 8) - lax.div(n + 1, 9)
            return lax.div(code_x, 4) + middle * more_x, lax.div(code_y, 4) + middle * more_y

        lax.fori_loop(0, 16, turn, (start_x + 0 * x, start_y + 0 * x))

    def in_full(b, work):
        kind = 3 * at_most(b, my_block)
        for number in (0, 3):

            @pl.when(kind == number)
            def _():
                work(number % 2, number // 2)

    def groups(with_a, with_late):
        return ((1, TILE * (1 + with_late)),) + ((0, TILE),) * with_a

    def held(ref_b, ref_a, b, s, count):
        return ref_b.at[b, pl.ds(0, count)] if s else ref_a.at[b]

    def keys_of(b, role, count):
        return kv[role, b].reshape(2 * TILE, HEAD_SIZE) if count > TILE else kv[role, b, 0]

    scale = FACTOR * math.log2(math.e)
    top[...] = jnp.full(top.shape, HIDDEN, F32)
    total[...] = jnp.zeros_like(total)
    dot[...] = jnp.zeros_like(dot)
    dq_acc[...] = jnp.zeros_like(dq_acc)

    def stats_step(n, b):
        run(gather_events, n)
        arrived(kv.at[1 - core, b], twin_recv.at[n])

        def stats(with_a, with_late):
            count = TILE * (1 + with_late)
            key_turns = jnp.concatenate(
                [
                    jnp.broadcast_to(turn_ref[pl.ds(2 * (late * 16 + b) + i, 1), :], (128, 128)).T
                    for late in range(1 + with_late)
                    for i in range(2)
                ],
                axis=0,
            )
            row = lax.broadcasted_iota(jnp.int32, (count, CHUNK), 0)
            key_places = b * TILE + row + jnp.where(row >= TILE, 15 * TILE, 0)
            parts = []
            for s, count in groups(with_a, with_late):
                query_pos = (part + 32 * s) * CHUNK + lax.broadcasted_iota(jnp.int32, (1, CHUNK), 1)
                query_turn = turn_ref[pl.ds(part + 32 * s, 1), :]
                key_turn, key_pos = key_turns[:count], key_places[:count]
                visible = (key_pos <= query_pos) & (
                    (key_turn == query_turn) | ((key_turn & 1) == 0)
                )
                logits = lax.dot_general(
                    keys_of(b, 0, count), qs[s], (((1,), (1,)), ((), ())), preferred_element_type=F32
                )
                bias = jnp.where(visible, 0.0, HIDDEN)
                parts.append((s, count, logits * scale + jnp.concatenate([bias] * PER_GROUP, axis=1)))
            for s, count, logits in parts:
                old_top = top[s]
                new_top = jnp.maximum(old_top, jnp.max(logits, axis=0, keepdims=True))
                shrink = jnp.exp2(old_top - new_top)
                weight = jnp.exp2(logits - new_top)
                grads = lax.dot_general(
                    keys_of(b, 1, count), os[s], (((1,), (1,)), ((), ())), preferred_element_type=F32
                )
                held(weights_b, weights_a, b, s, count)[...] = weight.astype(BF16)
                held(grads_b, grads_a, b, s, count)[...] = grads.astype(BF16)
                tile_max[s, b] = new_top
                top[s] = new_top
                total[s] = total[s] * shrink + jnp.sum(weight, axis=0, keepdims=True)
                dot[s] = dot[s] * shrink + jnp.sum(weight * grads, axis=0, keepdims=True)

        in_full(b, stats)

    over_blocks(NEAR_FIRST, stats_step)
    for s in range(2):
        inverse = 1.0 / total[s]
        total[s] = inverse
        dot[s] = dot[s] * inverse

    across = (wrap(second + 2), right, left, second)
    jumps = (2, 1, -1, 0)

    def chip_sum(a, b):
        i, j = firsts[a], across[b]
        at = index(i, j)
        arrived(twin.at[at], back_recv.at[slot_of(far, steps[a], jumps[b])])
        return partial[core, at].astype(F32) + twin[at].astype(F32)

    def ring_one(a):
        sums[a, 0] = chip_sum(a, 0).astype(BF16)
        for h, to in ((0, right), (1, left)):
            go(sums.at[a, 0, h], one.at[a, h], ring_send.at[a, h], ring_recv.at[a, h], target(first, to))

    def ring_two(a):
        for b, to in ((1, right), (2, left)):
            h = b - 1
            value = chip_sum(a, b)
            arrived(one.at[a, h], ring_recv.at[a, h])
            sums[a, b, 1 - h] = value[1 - h].astype(BF16)
            sums[a, b, h] = (value[h] + one[a, h].astype(F32)).astype(BF16)
            go(sums.at[a, b], two.at[a, h], ring_send.at[a, 2 + h], ring_recv.at[a, 2 + h], target(first, to))

    def home(a):
        value = chip_sum(a, 3)
        arrived(two.at[a, 0], ring_recv.at[a, 2])
        arrived(two.at[a, 1], ring_recv.at[a, 3])
        value = value + two[a, 0].astype(F32) + two[a, 1].astype(F32)
        if a == 3:
            line[a] = value.astype(BF16)
            for h, to in ((0, up), (1, down)):
                go(line.at[a, h], line_in.at[h], line_send.at[h], line_recv.at[h], target(to, second))
            return
        if a:
            h = 2 - a
            arrived(line_in.at[h], line_recv.at[h])
            line[a, 1 - h] = value[1 - h].astype(BF16)
            line[a, h] = (value[h] + line_in[h].astype(F32)).astype(BF16)
        else:
            line[a] = value.astype(BF16)
        i = firsts[a]
        bx, by = i + core * (second - i), second + core * (i - second)
        for other_z in range(4):
            for c in range(2):
                src = line.at[a, other_z // 2, pl.ds(c * 128 + (other_z % 2) * 64, 64)]
                dst = last.at[core, a, :, pl.ds(pl.multiple_of(z * 128, 128), 128)]
                args = (src, dst, last_send.at[a, other_z, c], last_recv.at[core, a, z])
                to = device(bx, by, other_z, c)
                if a:
                    go(*args, to)
                else:
                    go_or_keep((z == other_z) & (core == c), *args, to)

    reduce_events = {
        1: (lambda: ring_one(3),),
        4: (lambda: ring_one(2),),
        5: (lambda: ring_one(1),),
        6: (lambda: ring_two(3),),
        7: (lambda: ring_one(0),),
        10: (lambda: ring_two(2),),
        11: (lambda: ring_two(1),),
        12: (lambda: home(3),),
        15: (lambda: ring_two(0),),
    }

    def backward_step(n, b):
        def terms(with_a, with_late):
            sums_of = []
            for s, count in groups(with_a, with_late):
                by = jnp.exp2(tile_max[s, b] - top[s]) * total[s]
                attention = held(weights_b, weights_a, b, s, count)[...].astype(F32) * by
                grads = held(grads_b, grads_a, b, s, count)[...].astype(F32)
                logit_grad = (attention * (grads - dot[s])).astype(BF16)
                value_sum = jnp.dot(attention.astype(BF16), os[s], preferred_element_type=F32)
                key_sum = jnp.dot(logit_grad, qs[s], preferred_element_type=F32)
                dq_acc[s] += lax.dot_general(
                    logit_grad, keys_of(b, 0, count), (((0,), (0,)), ((), ())),
                    preferred_element_type=F32,
                )
                sums_of.append((key_sum * FACTOR, value_sum))
            for role in range(2):
                early = sums_of[0][role][:TILE]
                if with_a:
                    early = early + sums_of[1][role]
                partial[role, b, 0] = early.astype(BF16)
                if with_late:
                    partial[role, b, 1] = sums_of[0][role][TILE:].astype(BF16)
                else:
                    partial[role, b, 1] = jnp.zeros((TILE, HEAD_SIZE), BF16)

        in_full(b, terms)
        send(partial.at[1 - core, b], twin.at[b], back_send.at[n], back_recv.at[n], other_core).start()
        run(reduce_events, n)

    over_blocks(FAR_FIRST, backward_step)

    for s in range(2):
        for h in range(PER_GROUP):
            dq_own[s, :, pl.ds(h * 128, 128)] = (
                dq_acc[s, pl.ds(h * CHUNK, CHUNK), :] * FACTOR
            ).astype(BF16)
    for other_z in range(4):
        s = other_z // 2
        to = device(x, y, other_z, core)
        go_or_keep(
            z == other_z,
            dq_own.at[s, pl.ds((other_z % 2) * 64, 64)],
            dq_out.at[:, pl.ds(pl.multiple_of(z * 512, 512), 512)],
            dq_send.at[other_z], dq_recv.at[z], to,
        )
    home(2)
    home(1)
    home(0)

    for role in range(2):
        for a in range(3):
            for other_z in range(4):
                arrived(last.at[role, a, :, pl.ds(other_z * 128, 128)], last_recv.at[role, a, other_z])
    for other_z in range(4):
        arrived(dq_out.at[:, pl.ds(other_z * 512, 512)], dq_recv.at[other_z])

    whole, halved, piece = kv.at[0, 0], kv.at[0, 0, 0], line.at[0, 0, pl.ds(0, 64)]
    for r in range(1, 4):
        for role in range(2):
            arrived(k_ref.at[:, pl.ds(0, 128)], kv_send.at[role, r])
            arrived(q_ref.at[:, pl.ds(0, 512)], qo_send.at[role, r])
    for r in range(1, 3):
        for other_z in range(4):
            for c in range(2):
                arrived(piece, last_send.at[r, other_z, c])
    for h in range(2):
        arrived(whole, first_send.at[h])
        arrived(halved, first_send.at[2 + h])
        arrived(halved, line_send.at[h])
    for k in range(4):
        for h in range(2):
            arrived(whole, second_send.at[k, h])
            arrived(halved, second_send.at[k, 2 + h])
            arrived(halved, ring_send.at[k, h])
            arrived(whole, ring_send.at[k, 2 + h])
    for n in range(16):
        arrived(whole, twin_send.at[n])
        arrived(whole, back_send.at[n])

    @pl.when(core == 0)
    def _():
        arrived(v_ref.at[:, pl.ds(0, 128)], kv_send.at[1, 0])

    @pl.when(core == 1)
    def _():
        arrived(k_ref.at[:, pl.ds(0, 128)], kv_send.at[0, 0])

    for other_z in range(4):
        for c in range(2):

            @pl.when(jnp.logical_not((z == other_z) & (core == c)))
            def _():
                arrived(piece, last_send.at[0, other_z, c])

        @pl.when(z != other_z)
        def _():
            arrived(dq_own.at[0, pl.ds(0, 64)], dq_send.at[other_z])


def finish_kernel(dq_ref, dkv_ref, dq_out, dk_out, dv_out):
    dq_out[...] = dq_ref[...]
    for role, out in ((0, dk_out), (1, dv_out)):
        value = dkv_ref[role, 0].astype(F32)
        for a in range(1, 3):
            value = value + dkv_ref[role, a].astype(F32)
        out[...] = value.astype(BF16)


ANY = pl.BlockSpec(memory_space=pl.ANY)
VMEM = pl.BlockSpec(memory_space=pltpu.VMEM)
DMA = pltpu.SemaphoreType.DMA


def body(queries, keys, values, grad_out, turn_ids):
    block = (2, TILE, HEAD_SIZE)
    dq, dkv = pl.pallas_call(
        kernel,
        out_shape=(
            jax.ShapeDtypeStruct((64, 2048), BF16),
            jax.ShapeDtypeStruct((2, 3, 64, 512), BF16),
        ),
        in_specs=[ANY] * 5,
        out_specs=(ANY, ANY),
        scratch_shapes=[
            pltpu.VMEM((64, CHUNK), jnp.int32),
            pltpu.VMEM((2, 16) + block, BF16),
            pltpu.VMEM((2, 2, CHUNK, 512), BF16),
            pltpu.VMEM((2, ROWS, HEAD_SIZE), BF16),
            pltpu.VMEM((2, ROWS, HEAD_SIZE), BF16),
            pltpu.VMEM((16, 2 * TILE, ROWS), BF16),
            pltpu.VMEM((16, TILE, ROWS), BF16),
            pltpu.VMEM((16, 2 * TILE, ROWS), BF16),
            pltpu.VMEM((16, TILE, ROWS), BF16),
            pltpu.VMEM((2, 16, 1, ROWS), F32),
            pltpu.VMEM((2, 1, ROWS), F32),
            pltpu.VMEM((2, 1, ROWS), F32),
            pltpu.VMEM((2, 1, ROWS), F32),
            pltpu.VMEM((2, ROWS, HEAD_SIZE), F32),
            pltpu.VMEM((2, CHUNK, 512), BF16),
            pltpu.VMEM((2, 16) + block, BF16),
            pltpu.VMEM((16,) + block, BF16),
            pltpu.VMEM((4, 3) + block, BF16),
            pltpu.VMEM((4, 2, TILE, HEAD_SIZE), BF16),
            pltpu.VMEM((4, 2) + block, BF16),
            pltpu.VMEM((4,) + block, BF16),
            pltpu.VMEM(block, BF16),
            DMA((2, 4)), DMA((4, 2)),
            DMA((2, 4)), DMA((2, 4)),
            DMA((4,)), DMA((4,)),
            DMA((4, 4)), DMA((4, 4)),
            DMA((16,)), DMA((16,)),
            DMA((16,)), DMA((16,)),
            DMA((4, 4)), DMA((4, 4)),
            DMA((3, 4, 2)), DMA((2, 3, 4)),
            DMA((2,)), DMA((2,)),
            DMA((4,)), DMA((4,)),
            DMA,
        ],
        compiler_params=pltpu.CompilerParams(
            collective_id=0, has_side_effects=True, vmem_limit_bytes=58 << 20
        ),
        name="attention_backward",
    )(turn_ids.reshape(64, CHUNK), queries, keys, values, grad_out)
    return pl.pallas_call(
        finish_kernel,
        out_shape=(
            jax.ShapeDtypeStruct((64, 2048), BF16),
            jax.ShapeDtypeStruct((64, 512), BF16),
            jax.ShapeDtypeStruct((64, 512), BF16),
        ),
        in_specs=[VMEM] * 2,
        out_specs=(VMEM,) * 3,
        compiler_params=pltpu.CompilerParams(vmem_limit_bytes=60 << 20),
        name="finish",
    )(dq, dkv)


def solution(mesh):
    spread = P(("blk", "head"), None)
    return jax.shard_map(
        body,
        mesh=mesh,
        in_specs=(spread,) * 4 + (P(),),
        out_specs=(spread,) * 3,
        check_vma=False,
    )
```

```python
import math

import jax
import jax.numpy as jnp
from jax import lax
from jax.experimental import pallas as pl
from jax.experimental.pallas import tpu as pltpu
from jax.sharding import PartitionSpec as P

HEAD_SIZE = 128
CHUNK = 128
TILE = 256
PER_GROUP = 4
ROWS = PER_GROUP * CHUNK
HIDDEN = -1e30
FACTOR = HEAD_SIZE**-0.5
BF16 = jnp.bfloat16
F32 = jnp.float32
MESH = pl.DeviceIdType.MESH

NEAR_FIRST = (
    (0, 0), (-1, 0), (1, 0), (0, -1), (0, 1), (-1, -1), (-1, 1), (1, -1), (1, 1),
    (2, 0), (0, 2), (2, -1), (2, 1), (-1, 2), (1, 2), (2, 2),
)
FAR_FIRST = (
    (2, 2), (1, 2), (-1, 2), (2, 1), (2, -1), (0, 2), (2, 0), (1, 1), (1, -1), (-1, 1), (-1, -1),
    (0, 1), (0, -1), (1, 0), (-1, 0), (0, 0),
)


def device(x, y, z, core):
    return (lax.div(z, 2) * 32 + x * 8 + y * 2 + core, lax.rem(z, 2))


def wrap(a):
    return lax.rem(a + 4, 4)


def send(src, dst, send_sem, recv_sem, target):
    return pltpu.make_async_remote_copy(
        src_ref=src,
        dst_ref=dst,
        send_sem=send_sem,
        recv_sem=recv_sem,
        device_id=target,
        device_id_type=MESH,
    )


def arrived(ref, sem):
    pltpu.make_async_copy(ref, ref, sem).wait()


def greet(x, y, z, core):
    others = []
    for r in range(4):
        other_z = lax.rem(z + r, 4)
        if r:
            others.append(device(x, y, other_z, core))
        others.append(device(x, y, other_z, 1 - core))
    for step in (-1, 1):
        others.append(device(wrap(x + step), y, z, core))
        others.append(device(x, wrap(y + step), z, core))
    barrier = pltpu.get_barrier_semaphore()
    for other in others:
        pl.semaphore_signal(barrier, inc=1, device_id=other, device_id_type=MESH)
    pl.semaphore_wait(barrier, len(others))


def codes(order, axis):
    digits = [step[axis] % 4 for step in order]
    return [sum(digit * 4**i for i, digit in enumerate(digits[at : at + 8])) for at in (0, 8)]


def at_most(a, b):
    return lax.div(b - a + 16, 16)


def kernel(
    turns, q_ref, k_ref, v_ref, o_ref, dq_out, last,
    turn_ref, kv, landed, qs, os, weights_b, weights_a, grads_b, grads_a, tile_max, top, total, dot, dq_acc, dq_own,
    partial, twin, sums, one, two, line, line_in,
    kv_send, kv_recv, qo_send, qo_recv, first_send, first_recv, second_send, second_recv,
    twin_send, twin_recv, back_send, back_recv, ring_send, ring_recv, last_send, last_recv,
    line_send, line_recv,     dq_send, dq_recv, turn_sem,
):
    blk = lax.axis_index("blk")
    z_lo = lax.axis_index("head")
    z_hi = lax.div(blk, 32)
    part = lax.rem(blk, 32)
    x = lax.div(part, 8)
    y = lax.rem(lax.div(part, 2), 4)
    core = lax.rem(part, 2)
    z = z_hi * 2 + z_lo
    here = x * 4 + y
    first, second = x + core * (y - x), y + core * (x - y)

    def index(i, j):
        return (i + core * (j - i)) * 4 + j + core * (i - j)

    def target(i, j):
        return device(i + core * (j - i), j + core * (i - j), z, core)

    other_core = device(x, y, z, 1 - core)
    my_block = lax.div(part, 2)

    pltpu.make_async_copy(turns, turn_ref, turn_sem).start()
    greet(x, y, z, core)

    def go(src, dst, send_sem, recv_sem, to):
        send(src, dst, send_sem, recv_sem, to).start()

    def go_or_keep(own, src, dst, send_sem, recv_sem, to):
        @pl.when(own)
        def _():
            pltpu.make_async_copy(src, dst, recv_sem).start()

        @pl.when(jnp.logical_not(own))
        def _():
            send(src, dst, send_sem, recv_sem, to).start()

    rows = pl.ds(pl.multiple_of(core * 128 + z_lo * 64, 64), 64)
    for r in (2, 1, 3, 0):
        other_z = lax.rem(z + r, 4)
        columns = pl.ds(pl.multiple_of(other_z * 128, 128), 128)
        for role, ref in ((0, k_ref), (1, v_ref)):
            dst = kv.at[role, here, z_hi, rows]
            args = (ref.at[:, columns], dst, kv_send.at[role, r], kv_recv.at[z, core])
            if r:
                go(*args, device(x, y, other_z, role))
            else:
                go_or_keep(core == role, *args, device(x, y, z, role))

    own_rows = pl.ds(pl.multiple_of(z_lo * 64, 64), 64)
    for r in (2, 1, 3, 0):
        other_z = lax.rem(z + r, 4)
        to = device(x, y, other_z, core)
        columns = pl.ds(pl.multiple_of(other_z * 512, 512), 512)
        for role, ref in ((0, q_ref), (1, o_ref)):
            args = (ref.at[:, columns], landed.at[role, z_hi, own_rows], qo_send.at[role, r], qo_recv.at[role, z])
            if r:
                go(*args, to)
            else:
                pltpu.make_async_copy(args[0], args[1], args[3]).start()

    up, down = wrap(first + 1), wrap(first - 1)
    left, right = wrap(second - 1), wrap(second + 1)
    firsts = (first, down, up, wrap(first + 2))
    steps = (0, -1, 1, 2)
    near = {step: n for n, step in enumerate(NEAR_FIRST)}
    far = {step: n for n, step in enumerate(FAR_FIRST)}

    def slot_of(table, a, b):
        return table[a, b] + core * (table[b, a] - table[a, b])

    def block(i, j):
        return kv.at[core, index(i, j)]

    def half(i, j, h):
        return kv.at[core, index(i, j), h]

    def share(i, j, a, b):
        slot = slot_of(near, a, b)
        go(block(i, j), block(i, j), twin_send.at[slot], twin_recv.at[slot], other_core)

    def relay(src, sems, to):
        go(src, src, *sems, to)

    def spread(k):
        i = firsts[k]
        own = block(i, second)
        relay(own, (second_send.at[k, 0], second_recv.at[k, 0]), target(first, right))
        relay(own, (second_send.at[k, 1], second_recv.at[k, 1]), target(first, left))
        share(i, second, steps[k], 0)

    def begin():
        for other_z in range(4):
            for c in range(2):
                arrived(
                    kv.at[core, here, other_z // 2, pl.ds(c * 128 + (other_z % 2) * 64, 64)],
                    kv_recv.at[other_z, c],
                )
        own = block(first, second)
        relay(own, (first_send.at[0], first_recv.at[0]), target(up, second))
        relay(own, (first_send.at[1], first_recv.at[1]), target(down, second))
        spread(0)

    def first_hop(k):
        if k < 3:
            h, to = k - 1, (up, down)[k - 1]
            arrived(block(firsts[k], second), first_recv.at[h])
            relay(half(firsts[k], second, h), (first_send.at[2 + h], first_recv.at[2 + h]), target(to, second))
        else:
            for h in range(2):
                arrived(half(firsts[k], second, h), first_recv.at[2 + h])
        spread(k)

    def second_hop(k):
        i = firsts[k]
        arrived(block(i, left), second_recv.at[k, 0])
        relay(half(i, left, 0), (second_send.at[k, 2], second_recv.at[k, 2]), target(first, right))
        share(i, left, steps[k], -1)
        arrived(block(i, right), second_recv.at[k, 1])
        relay(half(i, right, 1), (second_send.at[k, 3], second_recv.at[k, 3]), target(first, left))
        share(i, right, steps[k], 1)

    def last_hop(k):
        i, j = firsts[k], wrap(second + 2)
        arrived(half(i, j, 0), second_recv.at[k, 2])
        arrived(half(i, j, 1), second_recv.at[k, 3])
        share(i, j, steps[k], 2)

    def queries_here():
        arrived(turn_ref, turn_sem)
        for role in range(2):
            for other_z in range(4):
                arrived(
                    landed.at[role, other_z // 2, pl.ds((other_z % 2) * 64, 64)],
                    qo_recv.at[role, other_z],
                )
        for s in range(2):
            for h in range(PER_GROUP):
                lanes, lines = pl.ds(h * 128, 128), pl.ds(h * CHUNK, CHUNK)
                qs[s, lines, :] = landed[0, s, :, lanes]
                os[s, lines, :] = landed[1, s, :, lanes]

    gather_events = {
        0: (begin, lambda: first_hop(1), lambda: first_hop(2), queries_here),
        1: (lambda: second_hop(0), lambda: first_hop(3)),
        3: (lambda: second_hop(1),),
        4: (lambda: second_hop(2),),
        6: (lambda: last_hop(0),),
        7: (lambda: second_hop(3),),
        9: (lambda: last_hop(1),),
        10: (lambda: last_hop(2),),
        11: (lambda: last_hop(3),),
    }

    def run(events, n):
        for at, actions in events.items():

            @pl.when(n == at)
            def _():
                for action in actions:
                    action()

    def block_of(code_x, code_y):
        return lax.rem(x + lax.rem(code_x, 4), 4) * 4 + lax.rem(y + lax.rem(code_y, 4), 4)

    def over_blocks(order, step):
        (start_x, more_x), (start_y, more_y) = codes(order, 0), codes(order, 1)

        def turn(n, carried):
            code_x, code_y = carried
            step(n, block_of(code_x, code_y))
            middle = lax.div(n + 1, 8) - lax.div(n + 1, 9)
            return lax.div(code_x, 4) + middle * more_x, lax.div(code_y, 4) + middle * more_y

        lax.fori_loop(0, 16, turn, (start_x + 0 * x, start_y + 0 * x))

    def in_full(b, work):
        kind = 3 * at_most(b, my_block)
        for number in (0, 3):

            @pl.when(kind == number)
            def _():
                work(number % 2, number // 2)

    def groups(with_a, with_late):
        return ((1, TILE * (1 + with_late)),) + ((0, TILE),) * with_a

    def held(ref_b, ref_a, b, s, count):
        return ref_b.at[b, pl.ds(0, count)] if s else ref_a.at[b]

    def keys_of(b, role, count):
        return kv[role, b].reshape(2 * TILE, HEAD_SIZE) if count > TILE else kv[role, b, 0]

    scale = FACTOR * math.log2(math.e)
    top[...] = jnp.full(top.shape, HIDDEN, F32)
    total[...] = jnp.zeros_like(total)
    dot[...] = jnp.zeros_like(dot)
    dq_acc[...] = jnp.zeros_like(dq_acc)

    def stats_step(n, b):
        run(gather_events, n)
        arrived(kv.at[1 - core, b], twin_recv.at[n])

        def stats(with_a, with_late):
            count = TILE * (1 + with_late)
            key_turns = jnp.concatenate(
                [
                    jnp.broadcast_to(turn_ref[pl.ds(2 * (late * 16 + b) + i, 1), :], (128, 128)).T
                    for late in range(1 + with_late)
                    for i in range(2)
                ],
                axis=0,
            )
            row = lax.broadcasted_iota(jnp.int32, (count, CHUNK), 0)
            key_places = b * TILE + row + jnp.where(row >= TILE, 15 * TILE, 0)
            parts = []
            for s, count in groups(with_a, with_late):
                query_pos = (part + 32 * s) * CHUNK + lax.broadcasted_iota(jnp.int32, (1, CHUNK), 1)
                query_turn = turn_ref[pl.ds(part + 32 * s, 1), :]
                key_turn, key_pos = key_turns[:count], key_places[:count]
                visible = (key_pos <= query_pos) & (
                    (key_turn == query_turn) | ((key_turn & 1) == 0)
                )
                logits = lax.dot_general(
                    keys_of(b, 0, count), qs[s], (((1,), (1,)), ((), ())), preferred_element_type=F32
                )
                bias = jnp.where(visible, 0.0, HIDDEN)
                parts.append((s, count, logits * scale + jnp.concatenate([bias] * PER_GROUP, axis=1)))
            for s, count, logits in parts:
                old_top = top[s]
                new_top = jnp.maximum(old_top, jnp.max(logits, axis=0, keepdims=True))
                shrink = jnp.exp2(old_top - new_top)
                weight = jnp.exp2(logits - new_top)
                grads = lax.dot_general(
                    keys_of(b, 1, count), os[s], (((1,), (1,)), ((), ())), preferred_element_type=F32
                )
                held(weights_b, weights_a, b, s, count)[...] = weight.astype(BF16)
                held(grads_b, grads_a, b, s, count)[...] = grads.astype(BF16)
                tile_max[s, b] = new_top
                top[s] = new_top
                total[s] = total[s] * shrink + jnp.sum(weight, axis=0, keepdims=True)
                dot[s] = dot[s] * shrink + jnp.sum(weight * grads, axis=0, keepdims=True)

        in_full(b, stats)

    over_blocks(NEAR_FIRST, stats_step)
    for s in range(2):
        inverse = 1.0 / total[s]
        total[s] = inverse
        dot[s] = dot[s] * inverse

    across = (wrap(second + 2), right, left, second)
    jumps = (2, 1, -1, 0)

    def chip_sum(a, b):
        i, j = firsts[a], across[b]
        at = index(i, j)
        arrived(twin.at[at], back_recv.at[slot_of(far, steps[a], jumps[b])])
        return partial[core, at].astype(F32) + twin[at].astype(F32)

    def ring_one(a):
        sums[a, 0] = chip_sum(a, 0).astype(BF16)
        for h, to in ((0, right), (1, left)):
            go(sums.at[a, 0, h], one.at[a, h], ring_send.at[a, h], ring_recv.at[a, h], target(first, to))

    def ring_two(a):
        for b, to in ((1, right), (2, left)):
            h = b - 1
            value = chip_sum(a, b)
            arrived(one.at[a, h], ring_recv.at[a, h])
            sums[a, b, 1 - h] = value[1 - h].astype(BF16)
            sums[a, b, h] = (value[h] + one[a, h].astype(F32)).astype(BF16)
            go(sums.at[a, b], two.at[a, h], ring_send.at[a, 2 + h], ring_recv.at[a, 2 + h], target(first, to))

    def home(a):
        value = chip_sum(a, 3)
        arrived(two.at[a, 0], ring_recv.at[a, 2])
        arrived(two.at[a, 1], ring_recv.at[a, 3])
        value = value + two[a, 0].astype(F32) + two[a, 1].astype(F32)
        if a == 3:
            line[a] = value.astype(BF16)
            for h, to in ((0, up), (1, down)):
                go(line.at[a, h], line_in.at[h], line_send.at[h], line_recv.at[h], target(to, second))
            return
        if a:
            h = 2 - a
            arrived(line_in.at[h], line_recv.at[h])
            line[a, 1 - h] = value[1 - h].astype(BF16)
            line[a, h] = (value[h] + line_in[h].astype(F32)).astype(BF16)
        else:
            line[a] = value.astype(BF16)
        i = firsts[a]
        bx, by = i + core * (second - i), second + core * (i - second)
        for other_z in range(4):
            for c in range(2):
                src = line.at[a, other_z // 2, pl.ds(c * 128 + (other_z % 2) * 64, 64)]
                dst = last.at[core, a, :, pl.ds(pl.multiple_of(z * 128, 128), 128)]
                args = (src, dst, last_send.at[a, other_z, c], last_recv.at[core, a, z])
                to = device(bx, by, other_z, c)
                if a:
                    go(*args, to)
                else:
                    go_or_keep((z == other_z) & (core == c), *args, to)

    reduce_events = {
        1: (lambda: ring_one(3),),
        4: (lambda: ring_one(2),),
        5: (lambda: ring_one(1),),
        7: (lambda: ring_one(0), lambda: ring_two(3)),
        11: (lambda: ring_two(2),),
        12: (lambda: ring_two(1),),
        13: (lambda: home(3),),
        15: (lambda: ring_two(0),),
    }

    def backward_step(n, b):
        def terms(with_a, with_late):
            sums_of = []
            for s, count in groups(with_a, with_late):
                by = jnp.exp2(tile_max[s, b] - top[s]) * total[s]
                attention = held(weights_b, weights_a, b, s, count)[...].astype(F32) * by
                grads = held(grads_b, grads_a, b, s, count)[...].astype(F32)
                logit_grad = (attention * (grads - dot[s])).astype(BF16)
                value_sum = jnp.dot(attention.astype(BF16), os[s], preferred_element_type=F32)
                key_sum = jnp.dot(logit_grad, qs[s], preferred_element_type=F32)
                dq_acc[s] += lax.dot_general(
                    logit_grad, keys_of(b, 0, count), (((0,), (0,)), ((), ())),
                    preferred_element_type=F32,
                )
                sums_of.append((key_sum * FACTOR, value_sum))
            for role in range(2):
                early = sums_of[0][role][:TILE]
                if with_a:
                    early = early + sums_of[1][role]
                partial[role, b, 0] = early.astype(BF16)
                if with_late:
                    partial[role, b, 1] = sums_of[0][role][TILE:].astype(BF16)
                else:
                    partial[role, b, 1] = jnp.zeros((TILE, HEAD_SIZE), BF16)

        in_full(b, terms)
        send(partial.at[1 - core, b], twin.at[b], back_send.at[n], back_recv.at[n], other_core).start()
        run(reduce_events, n)

    over_blocks(FAR_FIRST, backward_step)

    for s in range(2):
        for h in range(PER_GROUP):
            dq_own[s, :, pl.ds(h * 128, 128)] = (
                dq_acc[s, pl.ds(h * CHUNK, CHUNK), :] * FACTOR
            ).astype(BF16)
    for other_z in range(4):
        s = other_z // 2
        to = device(x, y, other_z, core)
        go_or_keep(
            z == other_z,
            dq_own.at[s, pl.ds((other_z % 2) * 64, 64)],
            dq_out.at[:, pl.ds(pl.multiple_of(z * 512, 512), 512)],
            dq_send.at[other_z], dq_recv.at[z], to,
        )
    home(2)
    home(1)
    home(0)

    for role in range(2):
        for a in range(3):
            for other_z in range(4):
                arrived(last.at[role, a, :, pl.ds(other_z * 128, 128)], last_recv.at[role, a, other_z])
    for other_z in range(4):
        arrived(dq_out.at[:, pl.ds(other_z * 512, 512)], dq_recv.at[other_z])

    whole, halved, piece = kv.at[0, 0], kv.at[0, 0, 0], line.at[0, 0, pl.ds(0, 64)]
    for r in range(1, 4):
        for role in range(2):
            arrived(k_ref.at[:, pl.ds(0, 128)], kv_send.at[role, r])
            arrived(q_ref.at[:, pl.ds(0, 512)], qo_send.at[role, r])
    for r in range(1, 3):
        for other_z in range(4):
            for c in range(2):
                arrived(piece, last_send.at[r, other_z, c])
    for h in range(2):
        arrived(whole, first_send.at[h])
        arrived(halved, first_send.at[2 + h])
        arrived(halved, line_send.at[h])
    for k in range(4):
        for h in range(2):
            arrived(whole, second_send.at[k, h])
            arrived(halved, second_send.at[k, 2 + h])
            arrived(halved, ring_send.at[k, h])
            arrived(whole, ring_send.at[k, 2 + h])
    for n in range(16):
        arrived(whole, twin_send.at[n])
        arrived(whole, back_send.at[n])

    @pl.when(core == 0)
    def _():
        arrived(v_ref.at[:, pl.ds(0, 128)], kv_send.at[1, 0])

    @pl.when(core == 1)
    def _():
        arrived(k_ref.at[:, pl.ds(0, 128)], kv_send.at[0, 0])

    for other_z in range(4):
        for c in range(2):

            @pl.when(jnp.logical_not((z == other_z) & (core == c)))
            def _():
                arrived(piece, last_send.at[0, other_z, c])

        @pl.when(z != other_z)
        def _():
            arrived(dq_own.at[0, pl.ds(0, 64)], dq_send.at[other_z])


def finish_kernel(dq_ref, dkv_ref, dq_out, dk_out, dv_out):
    dq_out[...] = dq_ref[...]
    for role, out in ((0, dk_out), (1, dv_out)):
        value = dkv_ref[role, 0].astype(F32)
        for a in range(1, 3):
            value = value + dkv_ref[role, a].astype(F32)
        out[...] = value.astype(BF16)


ANY = pl.BlockSpec(memory_space=pl.ANY)
VMEM = pl.BlockSpec(memory_space=pltpu.VMEM)
DMA = pltpu.SemaphoreType.DMA


def body(queries, keys, values, grad_out, turn_ids):
    block = (2, TILE, HEAD_SIZE)
    dq, dkv = pl.pallas_call(
        kernel,
        out_shape=(
            jax.ShapeDtypeStruct((64, 2048), BF16),
            jax.ShapeDtypeStruct((2, 3, 64, 512), BF16),
        ),
        in_specs=[ANY] * 5,
        out_specs=(ANY, ANY),
        scratch_shapes=[
            pltpu.VMEM((64, CHUNK), jnp.int32),
            pltpu.VMEM((2, 16) + block, BF16),
            pltpu.VMEM((2, 2, CHUNK, 512), BF16),
            pltpu.VMEM((2, ROWS, HEAD_SIZE), BF16),
            pltpu.VMEM((2, ROWS, HEAD_SIZE), BF16),
            pltpu.VMEM((16, 2 * TILE, ROWS), BF16),
            pltpu.VMEM((16, TILE, ROWS), BF16),
            pltpu.VMEM((16, 2 * TILE, ROWS), BF16),
            pltpu.VMEM((16, TILE, ROWS), BF16),
            pltpu.VMEM((2, 16, 1, ROWS), F32),
            pltpu.VMEM((2, 1, ROWS), F32),
            pltpu.VMEM((2, 1, ROWS), F32),
            pltpu.VMEM((2, 1, ROWS), F32),
            pltpu.VMEM((2, ROWS, HEAD_SIZE), F32),
            pltpu.VMEM((2, CHUNK, 512), BF16),
            pltpu.VMEM((2, 16) + block, BF16),
            pltpu.VMEM((16,) + block, BF16),
            pltpu.VMEM((4, 3) + block, BF16),
            pltpu.VMEM((4, 2, TILE, HEAD_SIZE), BF16),
            pltpu.VMEM((4, 2) + block, BF16),
            pltpu.VMEM((4,) + block, BF16),
            pltpu.VMEM(block, BF16),
            DMA((2, 4)), DMA((4, 2)),
            DMA((2, 4)), DMA((2, 4)),
            DMA((4,)), DMA((4,)),
            DMA((4, 4)), DMA((4, 4)),
            DMA((16,)), DMA((16,)),
            DMA((16,)), DMA((16,)),
            DMA((4, 4)), DMA((4, 4)),
            DMA((3, 4, 2)), DMA((2, 3, 4)),
            DMA((2,)), DMA((2,)),
            DMA((4,)), DMA((4,)),
            DMA,
        ],
        compiler_params=pltpu.CompilerParams(
            collective_id=0, has_side_effects=True, vmem_limit_bytes=58 << 20
        ),
        name="attention_backward",
    )(turn_ids.reshape(64, CHUNK), queries, keys, values, grad_out)
    return pl.pallas_call(
        finish_kernel,
        out_shape=(
            jax.ShapeDtypeStruct((64, 2048), BF16),
            jax.ShapeDtypeStruct((64, 512), BF16),
            jax.ShapeDtypeStruct((64, 512), BF16),
        ),
        in_specs=[VMEM] * 2,
        out_specs=(VMEM,) * 3,
        compiler_params=pltpu.CompilerParams(vmem_limit_bytes=60 << 20),
        name="finish",
    )(dq, dkv)


def solution(mesh):
    spread = P(("blk", "head"), None)
    return jax.shard_map(
        body,
        mesh=mesh,
        in_specs=(spread,) * 4 + (P(),),
        out_specs=(spread,) * 3,
        check_vma=False,
    )
```
